32 devices in a mesh: grp: 2 (over x), prompt: 4 (over y, core), resp: 4 (over z).
Axes of the slice: x: 2, y: 2, z: 4, core: 2. Of those that a mesh axis runs over, the one named last changes fastest.
Arguments:
- prompt_states: bfloat16 [2, 256, 4096], P('grp', 'prompt'), may hold values from -6 to 6
- response_states: bfloat16 [2, 16, 512, 4096], P('grp', ('prompt', 'resp')), may hold values from -6 to 6
- queries: bfloat16 [2, 16, 512, 2048], P('grp', ('prompt', 'resp'))
- grad_output: bfloat16 [2, 16, 512, 2048], P('grp', ('prompt', 'resp')), may hold values from -24 to 24
- key_weight: bfloat16 [4096, 512], replicated, may hold values from -0.09375 to 0.09375
- value_weight: bfloat16 [4096, 512], replicated, may hold values from -0.09375 to 0.09375
- rewards: float32 [2, 16], P('grp', ('prompt', 'resp'))
- lengths: int32 [2, 16], P('grp', ('prompt', 'resp')), may hold values from 1 to 512, 4915 in all within a row
- group_ids: int32 [2, 16], P('grp', ('prompt', 'resp')), may hold values from 0 to 7
Outputs:
- query_grad: bfloat16 [2, 16, 512, 2048], P('grp', ('prompt', 'resp'))
- key_weight_grad: float32 [4096, 512], P(('prompt', 'resp'))
- value_weight_grad: float32 [4096, 512], P(('prompt', 'resp'))
The draws below stay inside these ranges and needn't reach their ends.
Inputs may be any that keep to these rules, and one draw needn't show every extreme that they name: `lengths`: token slots at and above a response's length are padding; in every rollout group some response has all 512.
All inputs are finite; a program needn't handle non-finite values.
Results may differ from the reference program's by a relative error of at most 0.009.
The reference program's roundings to bfloat16 on the way (of `dout`, `probs_b` and `dscores`) count: a program that leaves them out, or rounds other values in their place, can miss the bound.
Values may be sent and summed in bfloat16 or wider, within the bound.
No kernel may reach another device: no remote copies, remote signals or barrier semaphores. Data moves between devices by JAX's collectives and lax.ppermute only.
A program may use at most 128 MiB of HBM per device.

```python
import math
import jax
import jax.numpy as jnp
import numpy as np
from jax import lax

D = 4096
HEADS = 16
KV_HEADS = 4
HEAD_DIM = 128
RLEN = 512
NADV = 8
PSHARD = 64
PROMPT = 256
RESPS = 16
GROUPS = 2
N_GRP = 2
N_PROMPT = 4


def advantage_ids(key):
    return jax.random.randint(key, (GROUPS, RESPS), 0, NADV, dtype=jnp.int32)


def draw_group_ids(key, part):
    return advantage_ids(key)


def draw_rewards(key, part):
    labels = advantage_ids(key)
    key = jax.random.fold_in(key, 11)
    first_key, second_key, third_key, fourth_key = jax.random.split(key, 4)
    rising = 1.0 + 2.0 * jnp.arange(RESPS, dtype=jnp.float32) / max(RESPS - 1, 1)
    index = jnp.arange(NADV, dtype=jnp.int32)
    failing = jax.random.randint(first_key, (GROUPS, 1), 0, NADV, dtype=jnp.int32)
    closed = (index[None, :] == failing) | (index[None, :] == (failing + NADV // 2) % NADV)
    rate = jnp.where(closed, 0.0, jax.random.uniform(second_key, (GROUPS, NADV), jnp.float32, 0.3, 0.7))
    onehot = (labels[:, :, None] == index[None, None, :]).astype(jnp.float32)
    own_rate = jnp.sum(onehot * rate[:, None, :], axis=-1)
    success = jnp.where(jax.random.uniform(third_key, (GROUPS, RESPS), jnp.float32) < own_rate, 1.0, 0.0)
    noise = 0.15 * jax.random.normal(fourth_key, (GROUPS, RESPS), jnp.float32)
    return (success + noise) * rising[None, :]


def draw_queries(key, part):
    key = jax.random.fold_in(key, 23)
    first_key = jax.random.fold_in(key, 0)
    shape = (GROUPS, RESPS, RLEN, HEADS * HEAD_DIM)
    base = jax.random.normal(first_key, shape, jnp.float32)
    return base.astype(jnp.bfloat16)


def block_scale(stream_key, extent, cuts, smallest, high):
    loudness = 1.0
    for position, parts in cuts:
        draws = jax.random.uniform(jax.random.fold_in(jax.random.fold_in(stream_key, 6), position), (parts,), jnp.float32, smallest / len(cuts), high / len(cuts))
        loudness = loudness * jnp.repeat(jnp.exp(draws), extent[position] // parts).reshape((-1,) + (1,) * (len(extent) - 1 - position))
    return loudness


def length_profile(amount, total, reach, slope):
    loads = [(1 << 20) // math.isqrt(rank ** slope) + 1 for rank in range(2, amount + 1)]
    rest, counts = total - reach - (amount - 1), [1] * (amount - 1)
    while rest > 0:
        candidates = [i for i in range(amount - 1) if counts[i] < reach]
        mass, budget = sum([loads[i] for i in candidates]), rest
        for i in candidates:
            more = min(reach - counts[i], max(1, budget * loads[i] // mass), rest)
            counts[i] = counts[i] + more
            rest = rest - more
    return np.array([reach] + counts)


def uneven_parts(rng, number_of, total, bound, skew):
    if number_of == 2:
        one = jax.random.randint(rng, (), max(1, total - bound), min(bound, total - 1) + 1)
        return jnp.stack([one, total - one])
    tallies = jnp.asarray(length_profile(number_of, total, bound, skew), jnp.int32)
    couples = (number_of - 1) // 2
    donor, sink = tallies[1:1 + 2 * couples:2], tallies[2:2 + 2 * couples:2]
    margin = jnp.minimum(donor - 1, bound - sink)
    passed = jax.random.randint(jax.random.fold_in(rng, 1), (couples,), 0, 1 << 20) % (margin + 1)
    tallies = tallies.at[1:1 + 2 * couples:2].set(donor - passed).at[2:2 + 2 * couples:2].set(sink + passed)
    return tallies[jax.random.permutation(jax.random.fold_in(rng, 2), number_of)]


def gaussian(stream_key, shape, scale, limit, cuts=(), kind=jnp.bfloat16):
    array = scale * jax.random.normal(stream_key, shape, jnp.float32)
    if cuts:
        array = array * block_scale(stream_key, shape, cuts, -0.22, 0.18)
    return jnp.clip(array, -limit, limit).astype(kind)


def setup_inputs(seed: int = 0) -> dict:
    key_of = jax.random.split(jax.random.key(seed), 10)
    return {
        "prompt_states": gaussian(key_of[0], (GROUPS, PROMPT, D), 1.0, 6.0, ((0, 2), (1, 4))),
        "response_states": gaussian(key_of[1], (GROUPS, RESPS, RLEN, D), 1.0, 6.0, ((0, 2), (1, 16))),
        "queries": draw_queries(jax.random.fold_in(key_of[9], 71), 0),
        "grad_output": gaussian(key_of[3], (GROUPS, RESPS, RLEN, HEADS * HEAD_DIM), 4.0, 24.0, ((0, 2), (1, 16))),
        "key_weight": gaussian(key_of[4], (D, KV_HEADS * HEAD_DIM), D ** -0.5, 0.09375),
        "value_weight": gaussian(key_of[5], (D, KV_HEADS * HEAD_DIM), D ** -0.5, 0.09375),
        "rewards": draw_rewards(jax.random.fold_in(key_of[9], 71), 0),
        "lengths": jax.vmap(lambda own: uneven_parts(own, RESPS, RESPS * RLEN * 3 // 5, RLEN, 2))(jax.random.split(key_of[7], GROUPS)).reshape((GROUPS, RESPS)).astype(jnp.int32),
        "group_ids": draw_group_ids(jax.random.fold_in(key_of[9], 71), 0),
    }


THETA = 1000000.0
EPS = 1e-06

def rotary_tables(positions, half):
    steps = jnp.arange(half, dtype=jnp.float32)
    freq = THETA ** (-2.0 * steps / (2.0 * half))
    angle = positions.astype(jnp.float32)[:, None] * freq[None, :]
    return (jnp.cos(angle)[:, None, :], jnp.sin(angle)[:, None, :])

def finish_keys(raw, positions):
    count = raw.shape[0]
    heads = raw.reshape(count, -1, HEAD_DIM)
    factor = lax.rsqrt(lax.optimization_barrier(jnp.mean(heads * heads, axis=-1, keepdims=True)) + EPS)
    normed = heads * factor
    half = HEAD_DIM // 2
    cosine, sine = rotary_tables(positions, half)
    first = normed[..., :half]
    second = normed[..., half:]
    turned = jnp.concatenate([first * cosine - second * sine, second * cosine + first * sine], axis=-1)
    return turned.reshape(count, -1)

def keys_backward(grad, raw, positions):
    count = raw.shape[0]
    heads = raw.reshape(count, -1, HEAD_DIM)
    factor = lax.rsqrt(lax.optimization_barrier(jnp.mean(heads * heads, axis=-1, keepdims=True)) + EPS)
    normed = heads * factor
    half = HEAD_DIM // 2
    cosine, sine = rotary_tables(positions, half)
    upper = grad.reshape(count, -1, HEAD_DIM)
    grad_a = upper[..., :half]
    grad_b = upper[..., half:]
    unturned = jnp.concatenate([grad_a * cosine + grad_b * sine, grad_b * cosine - grad_a * sine], axis=-1)
    inner = lax.optimization_barrier(jnp.mean(unturned * normed, axis=-1, keepdims=True))
    return (factor * (unturned - normed * inner)).reshape(count, -1)

def attend(query, dout, keys, values, row_start, prompt_len):
    rows = query.shape[0]
    total = keys.shape[0]
    kv_heads = keys.shape[1] // HEAD_DIM
    fold = query.shape[1] // keys.shape[1]
    scale = HEAD_DIM ** (-0.5)
    q_all = query.reshape(rows, kv_heads, fold, HEAD_DIM).astype(jnp.float32)
    k_all = keys.reshape(total, kv_heads, HEAD_DIM).astype(jnp.float32)
    v_all = values.reshape(total, kv_heads, HEAD_DIM).astype(jnp.float32)
    d_all = dout.reshape(rows, kv_heads, fold, HEAD_DIM).astype(jnp.float32)
    scores = jnp.einsum('rhgd,nhd->hgrn', q_all, k_all) * scale
    key_pos = jnp.arange(total, dtype=jnp.int32)
    row_pos = row_start + jnp.arange(rows, dtype=jnp.int32)
    visible = (key_pos[None, :] < prompt_len) | (key_pos[None, :] - prompt_len <= row_pos[:, None])
    scores = jnp.where(visible, scores, -jnp.inf)
    peak = lax.optimization_barrier(jnp.max(scores, axis=-1, keepdims=True))
    expo = jnp.exp(scores - peak)
    probs = expo / lax.optimization_barrier(jnp.sum(expo, axis=-1, keepdims=True))
    probs_b = probs.astype(jnp.bfloat16).astype(jnp.float32)
    attn = jnp.einsum('hgrn,nhd->rhgd', probs_b, v_all)
    delta = lax.optimization_barrier(jnp.sum(d_all * attn, axis=-1))
    dprobs = jnp.einsum('rhgd,nhd->hgrn', d_all, v_all)
    dscores = (probs * (dprobs - jnp.transpose(delta, (1, 2, 0))[..., None])).astype(jnp.bfloat16).astype(jnp.float32)
    grad_q = jnp.einsum('hgrn,nhd->rhgd', dscores, k_all) * scale
    grad_k = jnp.einsum('hgrn,rhgd->nhd', dscores, q_all) * scale
    grad_v = jnp.einsum('hgrn,rhgd->nhd', probs_b, d_all)
    return (grad_q.reshape(rows, -1).astype(jnp.bfloat16), grad_k.reshape(total, -1), grad_v.reshape(total, -1))

def from_sums(rewards, onehot, count, total, square):
    members = jnp.maximum(count, 1.0)
    mean = total / members
    spread = jnp.sqrt(jnp.maximum(square / members - mean * mean, 0.0))
    own_mean = lax.optimization_barrier(jnp.sum(onehot * mean[None, :], axis=1))
    own_spread = lax.optimization_barrier(jnp.sum(onehot * spread[None, :], axis=1))
    return (rewards - own_mean) / jnp.maximum(own_spread, 0.5)

def group_advantage(rewards, group_ids):
    onehot = (group_ids[:, None] == jnp.arange(NADV, dtype=jnp.int32)[None, :]).astype(jnp.float32)
    count = lax.optimization_barrier(jnp.sum(onehot, axis=0))
    total = lax.optimization_barrier(jnp.sum(onehot * rewards[:, None], axis=0))
    square = lax.optimization_barrier(jnp.sum(onehot * (rewards * rewards)[:, None], axis=0))
    return from_sums(rewards, onehot, count, total, square)

def reference(prompt_states, response_states, queries, grad_output, key_weight, value_weight, rewards, lengths, group_ids):
    prompt_len = PSHARD * N_PROMPT
    width = KV_HEADS * HEAD_DIM
    grad_wk = jnp.zeros((D, width), jnp.float32)
    grad_wv = jnp.zeros((D, width), jnp.float32)
    query_grads = []
    for group in range(N_GRP):
        states = prompt_states[group]
        prompt_positions = jnp.arange(prompt_len, dtype=jnp.int32)
        prompt_raw = jnp.dot(states, key_weight, preferred_element_type=jnp.float32)
        prompt_keys = finish_keys(prompt_raw, prompt_positions).astype(jnp.bfloat16)
        prompt_values = jnp.dot(states, value_weight, preferred_element_type=jnp.float32).astype(jnp.bfloat16)
        advantage = group_advantage(rewards[group], group_ids[group])

        def one_response(carry, item):
            sum_k, sum_v, acc_wk, acc_wv = carry
            own_states, query, probe, length, weight = item
            positions = prompt_len + jnp.arange(RLEN, dtype=jnp.int32)
            own_raw = jnp.dot(own_states, key_weight, preferred_element_type=jnp.float32)
            own_keys = finish_keys(own_raw, positions).astype(jnp.bfloat16)
            own_values = jnp.dot(own_states, value_weight, preferred_element_type=jnp.float32).astype(jnp.bfloat16)
            keys = jnp.concatenate([prompt_keys, own_keys], axis=0)
            values = jnp.concatenate([prompt_values, own_values], axis=0)
            live = jnp.arange(RLEN, dtype=jnp.int32) < length
            coef = jnp.where(live, weight / length.astype(jnp.float32), jnp.float32(0.0))
            dout = (probe.astype(jnp.float32) * coef[:, None]).astype(jnp.bfloat16)
            grad_q, grad_k, grad_v = attend(query, dout, keys, values, 0, prompt_len)
            own_dk = keys_backward(grad_k[prompt_len:], own_raw, positions).astype(jnp.bfloat16)
            own_dv = grad_v[prompt_len:].astype(jnp.bfloat16)
            acc_wk = acc_wk + jnp.dot(own_states.T, own_dk, preferred_element_type=jnp.float32)
            acc_wv = acc_wv + jnp.dot(own_states.T, own_dv, preferred_element_type=jnp.float32)
            return ((sum_k + grad_k[:prompt_len], sum_v + grad_v[:prompt_len], acc_wk, acc_wv), grad_q)
        start = (jnp.zeros((prompt_len, width), jnp.float32), jnp.zeros((prompt_len, width), jnp.float32), jnp.zeros((D, width), jnp.float32), jnp.zeros((D, width), jnp.float32))
        items = (response_states[group], queries[group], grad_output[group], lengths[group], advantage)
        (sum_k, sum_v, acc_wk, acc_wv), grad_q = lax.scan(one_response, start, items)
        query_grads.append(grad_q)
        prompt_dk = keys_backward(sum_k, prompt_raw, prompt_positions).astype(jnp.bfloat16)
        prompt_dv = sum_v.astype(jnp.bfloat16)
        grad_wk = grad_wk + acc_wk + jnp.dot(states.T, prompt_dk, preferred_element_type=jnp.float32)
        grad_wv = grad_wv + acc_wv + jnp.dot(states.T, prompt_dv, preferred_element_type=jnp.float32)
    return (jnp.stack(query_grads, axis=0), grad_wk, grad_wv)
```

```python
import functools
import math

import jax
import jax.numpy as jnp
from jax import lax
from jax.experimental import pallas as pl
from jax.experimental.pallas import tpu as pltpu
from jax.sharding import PartitionSpec as P

HEAD_DIM = 128
NADV = 8
THETA = 1000000.0
EPS = 1e-06
STATE_BOUND = 6.0
QROWS = 128
CALLS = (2, 2)
VMEM = 58 * 1024 * 1024
MARK = 16
PROJECT_BLOCK = 1024

BF16 = jnp.bfloat16
FREE = pl.CostEstimate(flops=1, bytes_accessed=1, transcendentals=0)
F32 = jnp.float32
BY_ROWS = (((0,), (0,)), ((), ()))
BY_COLS = (((1,), (1,)), ((), ()))


def exchange(value, steps):
    names = tuple(name for name, step in steps if step)
    sizes = [lax.axis_size(name) for name in names]
    mask = 0
    for (name, step), size in zip([s for s in steps if s[1]], sizes):
        mask = mask * size + step
    total = math.prod(sizes)
    return lax.ppermute(value, names, [(j, j ^ mask) for j in range(total)])


def rotary_tables(positions):
    lane = jnp.arange(HEAD_DIM, dtype=jnp.int32)
    half = HEAD_DIM // 2
    steps = (lane % half).astype(F32)
    freq = THETA ** (-2.0 * steps / HEAD_DIM)
    angle = positions.astype(F32)[:, None] * freq[None, :]
    sign = jnp.where(lane < half, -1.0, 1.0).astype(F32)
    return jnp.cos(angle), jnp.sin(angle) * sign[None, :]


def project_kernel(groups, counts, place_ref, p_hbm, r_hbm, wk_hbm, wv_hbm, cos_ref, sin_ref, *refs):
    n_grp, n_chip, n_core, n_resp, block = counts
    p_raw, p_both, r_raw, r_both = refs[:4]
    selected = refs[4:-7]
    x_ref, wk_ref, wv_ref, acc_k, acc_v, sems, out_sems = refs[-7:]
    depth, width = wk_ref.shape
    shard = p_raw.shape[0]
    rows = r_raw.shape[0]
    steps = depth // PROJECT_BLOCK
    copies = []
    for k in range(steps):
        part = slice(k * PROJECT_BLOCK, (k + 1) * PROJECT_BLOCK)
        pairs = (
            (wk_hbm.at[part, :], wk_ref.at[part, :]),
            (p_hbm.at[:, part], x_ref.at[:shard, part]),
            (r_hbm.at[:, part], x_ref.at[shard:, part]),
            (wv_hbm.at[part, :], wv_ref.at[part, :]),
        )
        copies.append([pltpu.make_async_copy(src, dst, sems.at[k, i]) for i, (src, dst) in enumerate(pairs)])
        for copy in copies[-1]:
            copy.start()
    leaving = []
    for k in range(steps):
        part = slice(k * PROJECT_BLOCK, (k + 1) * PROJECT_BLOCK)
        for copy in copies[k]:
            copy.wait()
        if k == steps - 1:
            sub = shard // n_resp
            own = pl.ds(pl.multiple_of(place_ref[3] * sub, sub), sub)
            for i, (e, c) in enumerate(groups if selected else ()):
                for d in range(n_chip):
                    for r in range(n_resp):
                        chip = place_ref[1] ^ d
                        core = place_ref[2] ^ c
                        index = ((chip * n_core + core) * n_resp + r) * n_grp + (place_ref[0] ^ e)
                        source = pl.ds(pl.multiple_of(index * block, block), block)
                        j = d * n_resp + r
                        target = slice(j * block, (j + 1) * block)
                        pairs = (
                            (x_ref.at[shard:, source], selected[i].at[:rows, target]),
                            (x_ref.at[own, source], selected[i].at[rows:, target]),
                        )
                        for m, (src, dst) in enumerate(pairs):
                            leaving.append(pltpu.make_async_copy(src, dst, out_sems.at[i, j, m]))
                            leaving[-1].start()
        for acc, w_ref in ((acc_k, wk_ref), (acc_v, wv_ref)):
            share = jnp.dot(x_ref[:, part], w_ref[part, :], preferred_element_type=F32)
            if k:
                acc[...] += share
            else:
                acc[...] = share
    for place, raw_ref, both_ref in (
        (slice(0, shard), p_raw, p_both),
        (slice(shard, shard + rows), r_raw, r_both),
    ):
        both_ref[:, width:] = acc_v[place, :].astype(BF16)
        raw_ref[...] = acc_k[place, :]
        cosine = cos_ref[place, :]
        sine = sin_ref[place, :]
        for head in range(width // HEAD_DIM):
            cols = slice(head * HEAD_DIM, (head + 1) * HEAD_DIM)
            x = acc_k[place, cols]
            factor = lax.rsqrt(jnp.mean(x * x, axis=-1, keepdims=True) + EPS)
            normed = x * factor
            turned = normed * cosine + pltpu.roll(normed, HEAD_DIM // 2, 1) * sine
            both_ref[:, cols] = turned.astype(BF16)
    for copy in leaving:
        copy.wait()


def project(prompt, response, key_weight, value_weight, cosine, sine, place, groups, counts):
    depth, width = key_weight.shape
    shard, rows = prompt.shape[0], response.shape[0]
    n_grp, n_chip, n_core, n_resp, block = counts
    direct = block % HEAD_DIM == 0
    blocks = n_chip * n_resp
    part = jax.ShapeDtypeStruct((rows + shard // n_resp, blocks * block), BF16)
    any_spec = pl.BlockSpec(memory_space=pl.ANY)
    vmem = pl.BlockSpec(memory_space=pltpu.VMEM)
    out = pl.pallas_call(
        functools.partial(project_kernel, groups, counts),
        in_specs=[pl.BlockSpec(memory_space=pltpu.SMEM)] + [any_spec] * 4 + [vmem] * 2,
        out_specs=[vmem] * 4 + ([any_spec] * len(groups) if direct else []),
        out_shape=[
            jax.ShapeDtypeStruct((count, scale * width), kind)
            for count in (shard, rows)
            for scale, kind in ((1, F32), (2, BF16))
        ]
        + ([part] * len(groups) if direct else []),
        scratch_shapes=[pltpu.VMEM((shard + rows, depth), BF16)]
        + [pltpu.VMEM((depth, width), BF16)] * 2
        + [pltpu.VMEM((shard + rows, width), F32)] * 2
        + [
            pltpu.SemaphoreType.DMA((depth // PROJECT_BLOCK, 4)),
            pltpu.SemaphoreType.DMA((len(groups), blocks, 2)),
        ],
        compiler_params=pltpu.CompilerParams(vmem_limit_bytes=VMEM),
        cost_estimate=FREE,
        name="project",
    )(place, prompt, response, key_weight, value_weight, cosine, sine)
    if direct:
        return out[:4], out[4:]
    own = lax.dynamic_slice_in_dim(prompt, place[3] * (shard // n_resp), shard // n_resp, 0)
    split = jnp.concatenate([response, own]).reshape(-1, n_chip, n_core, n_resp, n_grp, block)
    parts = []
    for e, c in groups:
        piece = lax.dynamic_index_in_dim(split, place[0] ^ e, 4, keepdims=False)
        piece = lax.dynamic_index_in_dim(piece, place[2] ^ c, 2, keepdims=False)
        pieces = [lax.dynamic_index_in_dim(piece, place[1] ^ d, 1, keepdims=False) for d in range(n_chip)]
        parts.append(jnp.stack(pieces, axis=1).reshape(part.shape))
    return out, parts


def tied(value, *others):
    return pl.pallas_call(
        lambda *refs: None,
        in_specs=[pl.BlockSpec(memory_space=pl.ANY)] * (1 + len(others)),
        out_specs=pl.BlockSpec(memory_space=pl.ANY),
        out_shape=jax.ShapeDtypeStruct(value.shape, value.dtype),
        input_output_aliases={0: 0},
        cost_estimate=FREE,
        name="tied",
    )(value, *others)


def attend_kernel(parts, fold, coef_ref, ints_ref, q_ref, go_ref, *refs):
    prompt_k = refs[:parts]
    prompt_v = refs[parts : 2 * parts]
    own_k, own_v, raw_ref, cos_ref, sin_ref = refs[2 * parts : 2 * parts + 5]
    gq_ref, sum_ref, g_ref, k_all, v_all, k_turned, acc_k, acc_v = refs[-8:]
    rows = q_ref.shape[0]
    shard = prompt_k[0].shape[0]
    prompt_len = parts * shard
    scale = HEAD_DIM ** (-0.5)
    length = ints_ref[0]
    coef = coef_ref[0]
    prompt = ints_ref[1]
    for d in range(parts):
        place = pl.ds(pl.multiple_of((prompt ^ d) * shard, shard), shard)
        k_all[place, :] = prompt_k[d][...]
        v_all[place, :] = prompt_v[d][...]
    k_all[prompt_len:, :] = own_k[...]
    v_all[prompt_len:, :] = own_v[...]
    k_turned[...] = k_all[...].T
    acc_k[...] = jnp.zeros_like(acc_k)
    acc_v[...] = jnp.zeros_like(acc_v)
    def one_block(first):
        seen = prompt_len + first + QROWS
        width = fold * QROWS
        position = first + lax.broadcasted_iota(jnp.int32, (QROWS, HEAD_DIM), 0)
        factor = jnp.where(position < length, coef, 0.0)
        parts_q = []
        parts_d = []
        for f in range(fold):
            cols = slice(f * HEAD_DIM, (f + 1) * HEAD_DIM)
            parts_q.append(q_ref[first : first + QROWS, cols])
            parts_d.append((go_ref[first : first + QROWS, cols].astype(F32) * factor).astype(BF16))
        query = jnp.concatenate(parts_q, axis=0)
        dout = jnp.concatenate(parts_d, axis=0)
        scores = lax.dot_general(k_all[:seen, :], query, BY_COLS, preferred_element_type=F32)
        key = lax.broadcasted_iota(jnp.int32, (QROWS, width), 0)
        row = lax.broadcasted_iota(jnp.int32, (QROWS, width), 1) % QROWS
        tail = jnp.where(key <= row, scores[seen - QROWS :, :], -jnp.inf)
        scores = jnp.concatenate([scores[: seen - QROWS, :], tail], axis=0)
        peak = jnp.max(scores, axis=0, keepdims=True)
        expo = jnp.exp2((scores - peak) * (scale * math.log2(math.e)))
        probs = expo * (1.0 / jnp.sum(expo, axis=0, keepdims=True))
        probs_b = probs.astype(BF16)
        dprobs = lax.dot_general(v_all[:seen, :], dout, BY_COLS, preferred_element_type=F32)
        delta = jnp.sum(probs_b.astype(F32) * dprobs, axis=0, keepdims=True)
        dscores = (probs * (dprobs - delta)).astype(BF16)
        grad_q = jnp.dot(k_turned[:, :seen], dscores, preferred_element_type=F32) * scale
        for f in range(fold):
            gq_ref[first : first + QROWS, f * HEAD_DIM : (f + 1) * HEAD_DIM] = (
                grad_q[:, f * QROWS : (f + 1) * QROWS].T.astype(BF16)
            )
        acc_k[:seen, :] += jnp.dot(dscores, query, preferred_element_type=F32)
        acc_v[:seen, :] += jnp.dot(probs_b, dout, preferred_element_type=F32)

    for start in range(0, rows, 2 * QROWS):

        @pl.when(start < length)
        def _(start=start):
            one_block(start)
            one_block(start + QROWS)

        @pl.when(start >= length)
        def _(start=start):
            gq_ref[start : start + 2 * QROWS, :] = jnp.zeros((2 * QROWS, gq_ref.shape[1]), BF16)

    sum_ref[:, :HEAD_DIM] = acc_k[:prompt_len, :] * scale
    sum_ref[:, HEAD_DIM:] = acc_v[:prompt_len, :]
    x = raw_ref[...]
    factor = lax.rsqrt(jnp.mean(x * x, axis=-1, keepdims=True) + EPS)
    normed = x * factor
    grad = acc_k[prompt_len:, :] * scale
    unturned = grad * cos_ref[...] - pltpu.roll(grad, HEAD_DIM // 2, 1) * sin_ref[...]
    inner = jnp.mean(unturned * normed, axis=-1, keepdims=True)
    g_ref[0, 0] = (factor * (unturned - normed * inner)).T.astype(BF16)
    g_ref[0, 1] = acc_v[prompt_len:, :].T.astype(BF16)


def attend(first, per, offset, chunk_heads, coef, ints, query, grad_output, prompt_both, own_both, raw, cosine, sine, before, after):
    rows, query_width = query.shape
    width = raw.shape[1]
    heads = width // HEAD_DIM
    fold = query_width // width
    parts = len(prompt_both)
    shard = prompt_both[0].shape[0]
    prompt_len = parts * shard
    total = prompt_len + rows
    here = lambda h: (0, first + h)
    there = lambda h: (0, heads + first + h)
    scalar = pl.BlockSpec(memory_space=pltpu.SMEM)
    table = pl.BlockSpec((rows, HEAD_DIM), lambda h: (0, 0))
    wide = pl.BlockSpec((rows, fold * HEAD_DIM), here)
    in_specs = [scalar, scalar, wide, wide]
    in_specs += [pl.BlockSpec((shard, HEAD_DIM), here)] * parts + [pl.BlockSpec((shard, HEAD_DIM), there)] * parts
    in_specs += [pl.BlockSpec((rows, HEAD_DIM), here), pl.BlockSpec((rows, HEAD_DIM), there)]
    in_specs += [pl.BlockSpec((rows, HEAD_DIM), here), table, table]
    operands = [coef, ints, query, grad_output, *prompt_both, *prompt_both, own_both, own_both, raw, cosine, sine]
    aliases = {}
    for i, value in enumerate(before):
        if value is not None:
            aliases[len(operands)] = i
            in_specs.append(pl.BlockSpec(memory_space=pl.ANY))
            operands.append(value)
    in_specs += [pl.BlockSpec(memory_space=pl.ANY)] * len(after)
    operands += after
    return pl.pallas_call(
        functools.partial(attend_kernel, parts, fold),
        grid=(per,),
        in_specs=in_specs,
        out_specs=[
            wide,
            pl.BlockSpec((prompt_len, 2 * HEAD_DIM), lambda h: (0, offset + h)),
            pl.BlockSpec((1, 2, HEAD_DIM, rows), lambda h: (h, 0, 0, 0)),
        ],
        out_shape=[
            jax.ShapeDtypeStruct((rows, query_width), BF16),
            jax.ShapeDtypeStruct((prompt_len, 2 * chunk_heads * HEAD_DIM), F32),
            jax.ShapeDtypeStruct((per, 2, HEAD_DIM, rows), BF16),
        ],
        scratch_shapes=[
            pltpu.VMEM((total, HEAD_DIM), BF16),
            pltpu.VMEM((total, HEAD_DIM), BF16),
            pltpu.VMEM((HEAD_DIM, total), BF16),
            pltpu.VMEM((total, HEAD_DIM), F32),
            pltpu.VMEM((total, HEAD_DIM), F32),
        ],
        input_output_aliases=aliases,
        compiler_params=pltpu.CompilerParams(vmem_limit_bytes=VMEM),
        cost_estimate=FREE,
        name="attend",
    )(*operands)


def everyone(value, names):
    return lax.all_to_all(value, names, split_axis=0, concat_axis=0, tiled=True)


def weight_kernel(parts, count, *refs):
    states = refs[:parts]
    grads = refs[parts : parts + count]
    tokens_ref = refs[parts + count]
    out_ref, scale_ref = refs[-2:]
    rows = grads[0].shape[1]
    total_rows = parts * states[0].shape[0]

    @pl.when(pl.program_id(0) == 0)
    def _():
        peak = jnp.max(jnp.abs(tokens_ref[...].astype(F32)), axis=0, keepdims=True)
        peak = jnp.max(peak, axis=1, keepdims=True)
        highest = jnp.zeros((1, rows), F32)
        for grad in grads:
            highest = jnp.maximum(highest, jnp.max(jnp.abs(grad[...]), axis=0, keepdims=True).astype(F32))
        peak = jnp.maximum(peak, jnp.max(highest, axis=1, keepdims=True))
        reach = jnp.maximum(peak * (STATE_BOUND * total_rows), 1e-30)
        exponent = jnp.clip(jnp.ceil(jnp.log2(reach)), -90.0, 120.0)
        scale_ref[...] = jnp.broadcast_to(exponent, scale_ref.shape)

    exponent = scale_ref[:1, :1]
    scale = jnp.exp2(14.0 - exponent)
    prompt = jnp.concatenate([part[rows:, :] for part in states], axis=0)
    first = 0
    for call in range(count // parts):
        rest = first + grads[call * parts].shape[0]
        total = lax.dot_general(tokens_ref[:, first:rest], prompt, BY_ROWS, preferred_element_type=F32)
        for d in range(parts):
            total = total + jnp.dot(grads[call * parts + d][...], states[d][:rows, :], preferred_element_type=F32)
        out_ref[first:rest, :] = total * scale
        first = rest
    out_ref[first:, :] = jnp.broadcast_to(exponent, (MARK, out_ref.shape[1]))


def weight_shares(states, grads, tokens):
    parts = len(states)
    rows, depth = states[0].shape
    columns = tokens.shape[1]
    step = 2 * HEAD_DIM
    return pl.pallas_call(
        functools.partial(weight_kernel, parts, len(grads)),
        grid=(depth // step,),
        in_specs=[pl.BlockSpec((rows, step), lambda j: (0, j))] * parts
        + [pl.BlockSpec(x.shape, lambda j: (0, 0)) for x in (*grads, tokens)],
        out_specs=pl.BlockSpec((columns + MARK, step), lambda j: (0, j)),
        out_shape=jax.ShapeDtypeStruct((columns + MARK, depth), F32),
        scratch_shapes=[pltpu.VMEM((8, HEAD_DIM), F32)],
        compiler_params=pltpu.CompilerParams(vmem_limit_bytes=VMEM),
        cost_estimate=FREE,
        name="weight_shares",
    )(*states, *grads, tokens)


def rows_kernel(sums_ref, raw_ref, cos_ref, sin_ref, *refs):
    out_ref = refs[-1]
    cosine = cos_ref[...]
    sine = sin_ref[...]
    for head in range(raw_ref.shape[1] // HEAD_DIM):
        cols = slice(head * HEAD_DIM, (head + 1) * HEAD_DIM)
        both = jnp.sum(sums_ref[:, :, 2 * head * HEAD_DIM : 2 * (head + 1) * HEAD_DIM], axis=0)
        grad = both[:, :HEAD_DIM]
        raw = raw_ref[:, cols]
        factor = lax.rsqrt(jnp.mean(raw * raw, axis=-1, keepdims=True) + EPS)
        normed = raw * factor
        unturned = grad * cosine - pltpu.roll(grad, HEAD_DIM // 2, 1) * sine
        inner = jnp.mean(unturned * normed, axis=-1, keepdims=True)
        start = 2 * head * HEAD_DIM
        out_ref[:, start : start + HEAD_DIM] = (factor * (unturned - normed * inner)).astype(BF16)
        out_ref[:, start + HEAD_DIM : start + 2 * HEAD_DIM] = both[:, HEAD_DIM:].astype(BF16)


def row_grads(sums, raw, cosine, sine, after):
    return pl.pallas_call(
        rows_kernel,
        in_specs=[pl.BlockSpec(memory_space=pltpu.VMEM)] * 4 + [pl.BlockSpec(memory_space=pl.ANY)] * len(after),
        out_shape=jax.ShapeDtypeStruct((raw.shape[0], 2 * raw.shape[1]), BF16),
        compiler_params=pltpu.CompilerParams(vmem_limit_bytes=VMEM),
        cost_estimate=FREE,
        name="row_grads",
    )(sums, raw, cosine, sine, *after)


def advantage_of(rewards, group_ids):
    onehot = (group_ids[:, None] == jnp.arange(NADV, dtype=jnp.int32)[None, :]).astype(F32)
    sums = jnp.stack(
        [
            jnp.sum(onehot, axis=0),
            jnp.sum(onehot * rewards[:, None], axis=0),
            jnp.sum(onehot * (rewards * rewards)[:, None], axis=0),
        ]
    )
    names = ("chip", "core", "resp")
    peers = lax.axis_size(names)
    sums = jnp.sum(everyone(jnp.broadcast_to(sums[None], (peers,) + sums.shape), names), axis=0)
    members = jnp.maximum(sums[0], 1.0)
    mean = sums[1] / members
    spread = jnp.sqrt(jnp.maximum(sums[2] / members - mean * mean, 0.0))
    own_mean = jnp.sum(onehot * mean[None, :], axis=1)
    own_spread = jnp.sum(onehot * spread[None, :], axis=1)
    return (rewards - own_mean) / jnp.maximum(own_spread, 0.5)


def exponent_of(payload):
    return payload[-MARK : 1 - MARK, :1].astype(F32)


def values_of(payload, exponent):
    return payload[:-MARK].astype(F32) * jnp.exp2(exponent)


def body(prompt_states, response_states, queries, grad_output, key_weight, value_weight, rewards, lengths, group_ids):
    depth, width = key_weight.shape
    shard = prompt_states.shape[1]
    rows = response_states.shape[2]
    n_grp = lax.axis_size("grp")
    n_chip = lax.axis_size("chip")
    n_core = lax.axis_size("core")
    n_resp = lax.axis_size("resp")
    n_prompt = n_chip * n_core
    grp = lax.axis_index("grp")
    chip = lax.axis_index("chip")
    core = lax.axis_index("core")
    resp = lax.axis_index("resp")
    prompt = chip * n_core + core
    prompt_len = shard * n_prompt
    block = depth // (n_prompt * n_resp * n_grp)
    sub = shard // n_resp
    states = response_states[0, 0]
    own_prompt = prompt_states[0]

    advantage = advantage_of(rewards[0], group_ids[0])
    length = lengths[0]
    coef = advantage / length.astype(F32)
    ints = jnp.stack([length[0], prompt.astype(jnp.int32)])

    prompt_cos, prompt_sin = rotary_tables(prompt * shard + jnp.arange(shard, dtype=jnp.int32))
    own_cos, own_sin = rotary_tables(prompt_len + jnp.arange(rows, dtype=jnp.int32))
    groups = [(e, c) for e in range(n_grp) for c in range(n_core)]
    place = jnp.stack([grp, chip, core, resp]).astype(jnp.int32)
    (prompt_raw, mine, own_raw, own_both), parts = project(
        own_prompt,
        states,
        key_weight,
        value_weight,
        jnp.concatenate([prompt_cos, own_cos]),
        jnp.concatenate([prompt_sin, own_sin]),
        place,
        groups,
        (n_grp, n_chip, n_core, n_resp, block),
    )
    prompt_both = [mine]
    for d in range(1, n_prompt):
        prompt_both.append(exchange(mine, [("chip", d // n_core), ("core", d % n_core)]))
    parts = [exchange(x, [("grp", e), ("core", c)]) if e or c else x for x, (e, c) in zip(parts, groups)]

    sub_raw = lax.dynamic_slice_in_dim(prompt_raw, resp * sub, sub, 0)
    sub_cos = lax.dynamic_slice_in_dim(prompt_cos, resp * sub, sub, 0)
    sub_sin = lax.dynamic_slice_in_dim(prompt_sin, resp * sub, sub, 0)

    def gather_rows(row_g):
        held = jnp.concatenate([row_g] + [exchange(row_g, [("core", c)]) for c in range(1, n_core)])
        return jnp.concatenate([held] + [exchange(held, [("grp", e)]) for e in range(1, n_grp)])

    def run(first, per, chunk_first, chunk_heads, grads, sums, after):
        grads, sums, own_g = attend(
            first, per, first - chunk_first, chunk_heads, coef, ints, queries[0, 0], grad_output[0, 0],
            prompt_both, own_both, own_raw, own_cos, own_sin, [grads, sums], after,
        )
        return grads, sums, own_g.reshape(-1, rows)

    def across(own_g):
        return [exchange(own_g, [("grp", e)]) for e in range(1, n_grp)]

    def everywhere(own_g, hops):
        held = [own_g] + hops
        return [exchange(held[e], [("core", c)]) if c else held[e] for e, c in groups]

    def row_tokens(sums, chunk_first, after):
        sums = everyone(sums.reshape(n_prompt * n_resp, sub, -1), ("chip", "core", "resp"))
        raw = lax.slice_in_dim(sub_raw, chunk_first * HEAD_DIM, chunk_first * HEAD_DIM + sums.shape[2] // 2, axis=1)
        own = row_grads(sums, raw, sub_cos, sub_sin, after)
        held = jnp.concatenate([own] + [exchange(own, [("core", c)]) for c in range(1, n_core)])
        return jnp.concatenate([held] + [exchange(held, [("grp", e)]) for e in range(1, n_grp)])

    def summed(shares):
        wide = n_resp * block
        kept = shares[:, :wide]
        sent = [
            exchange(shares[:, d * wide : (d + 1) * wide].astype(jnp.float16), [("chip", d)]) for d in range(1, n_chip)
        ]
        exponents = [exponent_of(x) for x in [kept] + sent]
        top = functools.reduce(jnp.maximum, exponents) + math.ceil(math.log2(n_chip))
        total = values_of(kept, exponents[0] - top)
        for payload, exponent in zip(sent, exponents[1:]):
            total = total + values_of(payload, exponent - top)
        tail = jnp.broadcast_to(top, (MARK, wide))
        payload = jnp.concatenate([total, tail], axis=0).astype(jnp.float16)
        half = lax.dynamic_slice_in_dim(total, resp * block, block, 1) * jnp.exp2(top - 14.0)
        for d in range(1, n_resp):
            part = lax.dynamic_slice_in_dim(payload, (resp ^ d) * block, block, 1)
            part = exchange(part, [("resp", d)])
            half = half + values_of(part, exponent_of(part) - 14.0)
        return half, exchange(half, [("grp", 1)])

    early, late = CALLS
    grads, sums_early, g_early = run(0, early, 0, early, None, None, [])
    hops_early = across(g_early)
    grads, sums_late, g_late = run(early, late, early, late, grads, None, parts[1:])
    hops_early = [tied(x, g_late) for x in hops_early]
    hops_late = across(g_late)
    tokens = row_tokens(sums_early, 0, [g_late])
    shares_early = weight_shares(parts, everywhere(g_early, hops_early), tokens)
    tokens = row_tokens(sums_late, early, [])
    shares_late = weight_shares(parts, everywhere(g_late, hops_late), tokens)
    finished = [summed(shares_early), summed(shares_late)]

    mine = jnp.concatenate([pair[0] for pair in finished], axis=0)
    theirs = jnp.concatenate([pair[1] for pair in finished], axis=0)
    low = jnp.where(grp == 0, mine, theirs)
    high = jnp.where(grp == 0, theirs, mine)
    both = jnp.concatenate([low, high], axis=1).reshape(width // HEAD_DIM, 2, HEAD_DIM, n_grp * block)
    sides = [both[:, side].reshape(width, n_grp * block).T for side in range(2)]
    return (grads[None, None], sides[0], sides[1])


def solution(mesh):
    devices = mesh.devices
    n_grp, n_prompt, n_resp = devices.shape
    split = jax.sharding.Mesh(
        devices.reshape(n_grp, n_prompt // 2, 2, n_resp), ("grp", "chip", "core", "resp")
    )
    prompt = ("chip", "core")
    owner = ("chip", "core", "resp")
    placed = (
        P("grp", prompt, None),
        P("grp", owner, None, None),
        P("grp", owner, None, None),
        P("grp", owner, None, None),
        P(),
        P(),
        P("grp", owner),
        P("grp", owner),
        P("grp", owner),
    )
    return jax.shard_map(
        body,
        mesh=split,
        in_specs=placed,
        out_specs=(
            P("grp", owner, None, None),
            P(owner, None),
            P(owner, None),
        ),
        check_vma=False,
    )
```

```python
import functools
import math

import jax
import jax.numpy as jnp
from jax import lax
from jax.experimental import pallas as pl
from jax.experimental.pallas import tpu as pltpu
from jax.sharding import PartitionSpec as P

HEAD_DIM = 128
NADV = 8
THETA = 1000000.0
EPS = 1e-06
STATE_BOUND = 6.0
QROWS = 128
CALLS = (2, 2)
VMEM = 58 * 1024 * 1024
MARK = 16
PROJECT_BLOCK = 1024

BF16 = jnp.bfloat16
FREE = pl.CostEstimate(flops=1, bytes_accessed=1, transcendentals=0)
F32 = jnp.float32
BY_ROWS = (((0,), (0,)), ((), ()))
BY_COLS = (((1,), (1,)), ((), ()))


def exchange(value, steps):
    names = tuple(name for name, step in steps if step)
    sizes = [lax.axis_size(name) for name in names]
    mask = 0
    for (name, step), size in zip([s for s in steps if s[1]], sizes):
        mask = mask * size + step
    total = math.prod(sizes)
    return lax.ppermute(value, names, [(j, j ^ mask) for j in range(total)])


def rotary_tables(positions):
    lane = jnp.arange(HEAD_DIM, dtype=jnp.int32)
    half = HEAD_DIM // 2
    steps = (lane % half).astype(F32)
    freq = THETA ** (-2.0 * steps / HEAD_DIM)
    angle = positions.astype(F32)[:, None] * freq[None, :]
    sign = jnp.where(lane < half, -1.0, 1.0).astype(F32)
    return jnp.cos(angle), jnp.sin(angle) * sign[None, :]


def column_copies(groups, counts, place_ref, source_ref, first, sub_ref, targets, sems):
    n_grp, n_chip, n_core, n_resp, block = counts
    rows = source_ref.shape[0] - first
    sub = targets[0].shape[0] - rows
    own = pl.ds(pl.multiple_of(place_ref[3] * sub, sub), sub)
    copies = []
    for i, (e, c) in enumerate(groups):
        copies.append([])
        for d in range(n_chip):
            for r in range(n_resp):
                chip = place_ref[1] ^ d
                core = place_ref[2] ^ c
                index = ((chip * n_core + core) * n_resp + r) * n_grp + (place_ref[0] ^ e)
                source = pl.ds(pl.multiple_of(index * block, block), block)
                j = d * n_resp + r
                target = slice(j * block, (j + 1) * block)
                pairs = (
                    (source_ref.at[first:, source], targets[i].at[:rows, target]),
                    (sub_ref.at[own, source], targets[i].at[rows:, target]),
                )
                for m, (src, dst) in enumerate(pairs):
                    copies[-1].append(pltpu.make_async_copy(src, dst, sems.at[i, j, m]))
                    copies[-1][-1].start()
    return copies


def select_kernel(groups, counts, place_ref, states_ref, prompt_ref, *refs):
    beside, across, held, sems, out_sems = refs
    outs = [beside, across.at[0], across.at[1]]
    targets = [held.at[i] for i in range(len(groups))]
    copies = column_copies(groups, counts, place_ref, states_ref, 0, prompt_ref, targets, sems)
    leaving = []
    for i, arriving in enumerate(copies):
        for copy in arriving:
            copy.wait()
        leaving.append(pltpu.make_async_copy(held.at[i], outs[i], out_sems.at[i]))
        leaving[-1].start()
    for copy in leaving:
        copy.wait()


def select_columns(states, prompt, place, groups, counts):
    n_grp, n_chip, n_core, n_resp, block = counts
    sub = prompt.shape[0] // n_resp
    rows = states.shape[0] + sub
    width = n_chip * n_resp * block
    if block % HEAD_DIM:
        own = lax.dynamic_slice_in_dim(prompt, place[3] * sub, sub, 0)
        split = jnp.concatenate([states, own]).reshape(rows, n_chip, n_core, n_resp, n_grp, block)
        out = []
        for e, c in groups:
            part = lax.dynamic_index_in_dim(split, place[0] ^ e, 4, keepdims=False)
            part = lax.dynamic_index_in_dim(part, place[2] ^ c, 2, keepdims=False)
            parts = [lax.dynamic_index_in_dim(part, place[1] ^ d, 1, keepdims=False) for d in range(n_chip)]
            out.append(jnp.stack(parts, axis=1).reshape(rows, width))
        return out if len(out) == 1 else (out[0], jnp.stack(out[1:]))
    return pl.pallas_call(
        functools.partial(select_kernel, groups, counts),
        in_specs=[pl.BlockSpec(memory_space=pltpu.SMEM)] + [pl.BlockSpec(memory_space=pl.ANY)] * 2,
        out_specs=[pl.BlockSpec(memory_space=pl.ANY)] * 2,
        out_shape=[
            jax.ShapeDtypeStruct((rows, width), states.dtype),
            jax.ShapeDtypeStruct((2, rows, width), states.dtype),
        ],
        scratch_shapes=[
            pltpu.VMEM((len(groups), rows, width), states.dtype),
            pltpu.SemaphoreType.DMA((len(groups), n_chip * n_resp, 2)),
            pltpu.SemaphoreType.DMA((len(groups),)),
        ],
        compiler_params=pltpu.CompilerParams(vmem_limit_bytes=VMEM),
        cost_estimate=FREE,
        name="select_columns",
    )(place, states, prompt)


def project_kernel(groups, counts, place_ref, p_hbm, r_hbm, wk_hbm, wv_hbm, cos_ref, sin_ref, after_ref, *refs):
    p_raw, p_both, r_raw, r_both = refs[:4]
    selected = refs[4:-7]
    x_ref, wk_ref, wv_ref, acc_k, acc_v, sems, out_sems = refs[-7:]
    depth, width = wk_ref.shape
    shard = p_raw.shape[0]
    rows = r_raw.shape[0]
    steps = depth // PROJECT_BLOCK
    copies = []
    for k in range(steps):
        part = slice(k * PROJECT_BLOCK, (k + 1) * PROJECT_BLOCK)
        pairs = (
            (wk_hbm.at[part, :], wk_ref.at[part, :]),
            (p_hbm.at[:, part], x_ref.at[:shard, part]),
            (r_hbm.at[:, part], x_ref.at[shard:, part]),
            (wv_hbm.at[part, :], wv_ref.at[part, :]),
        )
        copies.append([pltpu.make_async_copy(src, dst, sems.at[k, i]) for i, (src, dst) in enumerate(pairs)])
        for copy in copies[-1]:
            copy.start()
    leaving = []
    for k in range(steps):
        part = slice(k * PROJECT_BLOCK, (k + 1) * PROJECT_BLOCK)
        for copy in copies[k]:
            copy.wait()
        if k == steps - 1 and selected:
            leaving = column_copies(groups, counts, place_ref, x_ref, shard, x_ref, selected, out_sems)
        for acc, w_ref in ((acc_k, wk_ref), (acc_v, wv_ref)):
            share = jnp.dot(x_ref[:, part], w_ref[part, :], preferred_element_type=F32)
            if k:
                acc[...] += share
            else:
                acc[...] = share
    for place, raw_ref, both_ref in (
        (slice(0, shard), p_raw, p_both),
        (slice(shard, shard + rows), r_raw, r_both),
    ):
        both_ref[:, width:] = acc_v[place, :].astype(BF16)
        raw_ref[...] = acc_k[place, :]
        cosine = cos_ref[place, :]
        sine = sin_ref[place, :]
        for head in range(width // HEAD_DIM):
            cols = slice(head * HEAD_DIM, (head + 1) * HEAD_DIM)
            x = acc_k[place, cols]
            factor = lax.rsqrt(jnp.mean(x * x, axis=-1, keepdims=True) + EPS)
            normed = x * factor
            turned = normed * cosine + pltpu.roll(normed, HEAD_DIM // 2, 1) * sine
            both_ref[:, cols] = turned.astype(BF16)
    for copy in sum(leaving, []):
        copy.wait()


def project(prompt, response, key_weight, value_weight, cosine, sine, place, groups, counts, after):
    depth, width = key_weight.shape
    shard, rows = prompt.shape[0], response.shape[0]
    n_grp, n_chip, n_core, n_resp, block = counts
    direct = block % HEAD_DIM == 0
    blocks = n_chip * n_resp
    part = jax.ShapeDtypeStruct((rows + shard // n_resp, blocks * block), BF16)
    any_spec = pl.BlockSpec(memory_space=pl.ANY)
    vmem = pl.BlockSpec(memory_space=pltpu.VMEM)
    out = pl.pallas_call(
        functools.partial(project_kernel, groups, counts),
        in_specs=[pl.BlockSpec(memory_space=pltpu.SMEM)] + [any_spec] * 4 + [vmem] * 2 + [any_spec],
        out_specs=[vmem] * 4 + ([any_spec] * len(groups) if direct else []),
        out_shape=[
            jax.ShapeDtypeStruct((count, scale * width), kind)
            for count in (shard, rows)
            for scale, kind in ((1, F32), (2, BF16))
        ]
        + ([part] * len(groups) if direct else []),
        scratch_shapes=[pltpu.VMEM((shard + rows, depth), BF16)]
        + [pltpu.VMEM((depth, width), BF16)] * 2
        + [pltpu.VMEM((shard + rows, width), F32)] * 2
        + [
            pltpu.SemaphoreType.DMA((depth // PROJECT_BLOCK, 4)),
            pltpu.SemaphoreType.DMA((len(groups), blocks, 2)),
        ],
        compiler_params=pltpu.CompilerParams(vmem_limit_bytes=VMEM),
        cost_estimate=FREE,
        name="project",
    )(place, prompt, response, key_weight, value_weight, cosine, sine, after)
    if direct:
        return out[:4], out[4:]
    return out, select_columns(response, prompt, place, groups, counts)


def tied(value, *others):
    return pl.pallas_call(
        lambda *refs: None,
        in_specs=[pl.BlockSpec(memory_space=pl.ANY)] * (1 + len(others)),
        out_specs=pl.BlockSpec(memory_space=pl.ANY),
        out_shape=jax.ShapeDtypeStruct(value.shape, value.dtype),
        input_output_aliases={0: 0},
        cost_estimate=FREE,
        name="tied",
    )(value, *others)


def attend_kernel(parts, fold, coef_ref, ints_ref, q_ref, go_ref, *refs):
    prompt_k = refs[:parts]
    prompt_v = refs[parts : 2 * parts]
    own_k, own_v, raw_ref, cos_ref, sin_ref = refs[2 * parts : 2 * parts + 5]
    gq_ref, sum_ref, g_ref, k_all, v_all, k_turned, acc_k, acc_v = refs[-8:]
    rows = q_ref.shape[0]
    shard = prompt_k[0].shape[0]
    prompt_len = parts * shard
    scale = HEAD_DIM ** (-0.5)
    length = ints_ref[0]
    coef = coef_ref[0]
    prompt = ints_ref[1]
    for d in range(parts):
        place = pl.ds(pl.multiple_of((prompt ^ d) * shard, shard), shard)
        k_all[place, :] = prompt_k[d][...]
        v_all[place, :] = prompt_v[d][...]
    k_all[prompt_len:, :] = own_k[...]
    v_all[prompt_len:, :] = own_v[...]
    k_turned[...] = k_all[...].T
    acc_k[...] = jnp.zeros_like(acc_k)
    acc_v[...] = jnp.zeros_like(acc_v)
    def one_block(first):
        seen = prompt_len + first + QROWS
        width = fold * QROWS
        position = first + lax.broadcasted_iota(jnp.int32, (QROWS, HEAD_DIM), 0)
        factor = jnp.where(position < length, coef, 0.0)
        parts_q = []
        parts_d = []
        for f in range(fold):
            cols = slice(f * HEAD_DIM, (f + 1) * HEAD_DIM)
            parts_q.append(q_ref[first : first + QROWS, cols])
            parts_d.append((go_ref[first : first + QROWS, cols].astype(F32) * factor).astype(BF16))
        query = jnp.concatenate(parts_q, axis=0)
        dout = jnp.concatenate(parts_d, axis=0)
        scores = lax.dot_general(k_all[:seen, :], query, BY_COLS, preferred_element_type=F32)
        key = lax.broadcasted_iota(jnp.int32, (QROWS, width), 0)
        row = lax.broadcasted_iota(jnp.int32, (QROWS, width), 1) % QROWS
        tail = jnp.where(key <= row, scores[seen - QROWS :, :], -jnp.inf)
        scores = jnp.concatenate([scores[: seen - QROWS, :], tail], axis=0)
        peak = jnp.max(scores, axis=0, keepdims=True)
        expo = jnp.exp2((scores - peak) * (scale * math.log2(math.e)))
        probs = expo * (1.0 / jnp.sum(expo, axis=0, keepdims=True))
        probs_b = probs.astype(BF16)
        dprobs = lax.dot_general(v_all[:seen, :], dout, BY_COLS, preferred_element_type=F32)
        delta = jnp.sum(probs_b.astype(F32) * dprobs, axis=0, keepdims=True)
        dscores = (probs * (dprobs - delta)).astype(BF16)
        grad_q = jnp.dot(k_turned[:, :seen], dscores, preferred_element_type=F32) * scale
        for f in range(fold):
            gq_ref[first : first + QROWS, f * HEAD_DIM : (f + 1) * HEAD_DIM] = (
                grad_q[:, f * QROWS : (f + 1) * QROWS].T.astype(BF16)
            )
        acc_k[:seen, :] += jnp.dot(dscores, query, preferred_element_type=F32)
        acc_v[:seen, :] += jnp.dot(probs_b, dout, preferred_element_type=F32)

    for start in range(0, rows, 2 * QROWS):

        @pl.when(start < length)
        def _(start=start):
            one_block(start)
            one_block(start + QROWS)

        @pl.when(start >= length)
        def _(start=start):
            gq_ref[start : start + 2 * QROWS, :] = jnp.zeros((2 * QROWS, gq_ref.shape[1]), BF16)

    sum_ref[:, :HEAD_DIM] = acc_k[:prompt_len, :] * scale
    sum_ref[:, HEAD_DIM:] = acc_v[:prompt_len, :]
    x = raw_ref[...]
    factor = lax.rsqrt(jnp.mean(x * x, axis=-1, keepdims=True) + EPS)
    normed = x * factor
    grad = acc_k[prompt_len:, :] * scale
    unturned = grad * cos_ref[...] - pltpu.roll(grad, HEAD_DIM // 2, 1) * sin_ref[...]
    inner = jnp.mean(unturned * normed, axis=-1, keepdims=True)
    g_ref[0, 0] = (factor * (unturned - normed * inner)).T.astype(BF16)
    g_ref[0, 1] = acc_v[prompt_len:, :].T.astype(BF16)


def attend(first, per, offset, chunk_heads, coef, ints, query, grad_output, prompt_both, own_both, raw, cosine, sine, before, after):
    rows, query_width = query.shape
    width = raw.shape[1]
    heads = width // HEAD_DIM
    fold = query_width // width
    parts = len(prompt_both)
    shard = prompt_both[0].shape[0]
    prompt_len = parts * shard
    total = prompt_len + rows
    here = lambda h: (0, first + h)
    there = lambda h: (0, heads + first + h)
    scalar = pl.BlockSpec(memory_space=pltpu.SMEM)
    table = pl.BlockSpec((rows, HEAD_DIM), lambda h: (0, 0))
    wide = pl.BlockSpec((rows, fold * HEAD_DIM), here)
    in_specs = [scalar, scalar, wide, wide]
    in_specs += [pl.BlockSpec((shard, HEAD_DIM), here)] * parts + [pl.BlockSpec((shard, HEAD_DIM), there)] * parts
    in_specs += [pl.BlockSpec((rows, HEAD_DIM), here), pl.BlockSpec((rows, HEAD_DIM), there)]
    in_specs += [pl.BlockSpec((rows, HEAD_DIM), here), table, table]
    operands = [coef, ints, query, grad_output, *prompt_both, *prompt_both, own_both, own_both, raw, cosine, sine]
    aliases = {}
    for i, value in enumerate(before):
        if value is not None:
            aliases[len(operands)] = i
            in_specs.append(pl.BlockSpec(memory_space=pl.ANY))
            operands.append(value)
    in_specs += [pl.BlockSpec(memory_space=pl.ANY)] * len(after)
    operands += after
    return pl.pallas_call(
        functools.partial(attend_kernel, parts, fold),
        grid=(per,),
        in_specs=in_specs,
        out_specs=[
            wide,
            pl.BlockSpec((prompt_len, 2 * HEAD_DIM), lambda h: (0, offset + h)),
            pl.BlockSpec((1, 2, HEAD_DIM, rows), lambda h: (h, 0, 0, 0)),
        ],
        out_shape=[
            jax.ShapeDtypeStruct((rows, query_width), BF16),
            jax.ShapeDtypeStruct((prompt_len, 2 * chunk_heads * HEAD_DIM), F32),
            jax.ShapeDtypeStruct((per, 2, HEAD_DIM, rows), BF16),
        ],
        scratch_shapes=[
            pltpu.VMEM((total, HEAD_DIM), BF16),
            pltpu.VMEM((total, HEAD_DIM), BF16),
            pltpu.VMEM((HEAD_DIM, total), BF16),
            pltpu.VMEM((total, HEAD_DIM), F32),
            pltpu.VMEM((total, HEAD_DIM), F32),
        ],
        input_output_aliases=aliases,
        compiler_params=pltpu.CompilerParams(vmem_limit_bytes=VMEM),
        cost_estimate=FREE,
        name="attend",
    )(*operands)


def everyone(value, names):
    return lax.all_to_all(value, names, split_axis=0, concat_axis=0, tiled=True)


def weight_kernel(parts, tokens_count, *refs):
    states = refs[:parts]
    grads = refs[parts : 2 * parts]
    tokens = refs[2 * parts : 2 * parts + tokens_count]
    out_ref, scale_ref, side_ref = refs[-3:]
    columns, rows = grads[0].shape
    total_rows = parts * states[0].shape[-2]

    @pl.when(pl.program_id(0) == 0)
    def _():
        highest = jnp.zeros((1, rows), F32)
        for d, grad in enumerate(grads):
            value = grad[...]
            side_ref[:, d * rows : (d + 1) * rows] = value
            highest = jnp.maximum(highest, jnp.max(jnp.abs(value), axis=0, keepdims=True).astype(F32))
        peak = jnp.max(highest, axis=1, keepdims=True)
        for token in tokens:
            highest = jnp.max(jnp.abs(token[...].astype(F32)), axis=0, keepdims=True)
            peak = jnp.maximum(peak, jnp.max(highest, axis=1, keepdims=True))
        reach = jnp.maximum(peak * (STATE_BOUND * total_rows), 1e-30)
        exponent = jnp.clip(jnp.ceil(jnp.log2(reach)), -90.0, 120.0)
        scale_ref[...] = jnp.broadcast_to(exponent, scale_ref.shape)

    exponent = scale_ref[:1, :1]
    response = jnp.concatenate([part[:rows, :] for part in states], axis=0)
    prompt = jnp.concatenate([part[rows:, :] for part in states], axis=0)
    token = jnp.concatenate([token[...] for token in tokens], axis=0)
    total = jnp.dot(side_ref[...], response, preferred_element_type=F32)
    total = total + lax.dot_general(token, prompt, BY_ROWS, preferred_element_type=F32)
    out_ref[:columns, :] = total * jnp.exp2(14.0 - exponent)
    out_ref[columns:, :] = jnp.broadcast_to(exponent, (MARK, out_ref.shape[1]))


def weight_shares(states, grads, tokens):
    parts = len(states)
    rows, depth = states[0][0].shape
    columns = grads[0].shape[0]
    step = 2 * HEAD_DIM
    return pl.pallas_call(
        functools.partial(weight_kernel, parts, len(tokens)),
        grid=(depth // step,),
        in_specs=[
            pl.BlockSpec((rows, step), lambda j: (0, j))
            if index is None
            else pl.BlockSpec((None, rows, step), lambda j, index=index: (index, 0, j))
            for _, index in states
        ]
        + [pl.BlockSpec(x.shape, lambda j: (0, 0)) for x in (*grads, *tokens)],
        out_specs=pl.BlockSpec((columns + MARK, step), lambda j: (0, j)),
        out_shape=jax.ShapeDtypeStruct((columns + MARK, depth), F32),
        scratch_shapes=[pltpu.VMEM((8, HEAD_DIM), F32), pltpu.VMEM((columns, parts * grads[0].shape[1]), BF16)],
        compiler_params=pltpu.CompilerParams(vmem_limit_bytes=VMEM),
        cost_estimate=FREE,
        name="weight_shares",
    )(*[array for array, _ in states], *grads, *tokens)


def rows_kernel(first, place_ref, sums_ref, raw_ref, cos_ref, sin_ref, *refs):
    out_ref = refs[-1]
    sub = sums_ref.shape[1]
    own = pl.ds(pl.multiple_of(place_ref[3] * sub, sub), sub)
    cosine = cos_ref[own, :]
    sine = sin_ref[own, :]
    for head in range(out_ref.shape[1] // (2 * HEAD_DIM)):
        start = 2 * head * HEAD_DIM
        both = jnp.sum(sums_ref[:, :, start : start + 2 * HEAD_DIM], axis=0)
        grad = both[:, :HEAD_DIM]
        raw = raw_ref[own, (first + head) * HEAD_DIM : (first + head + 1) * HEAD_DIM]
        factor = lax.rsqrt(jnp.mean(raw * raw, axis=-1, keepdims=True) + EPS)
        normed = raw * factor
        unturned = grad * cosine - pltpu.roll(grad, HEAD_DIM // 2, 1) * sine
        inner = jnp.mean(unturned * normed, axis=-1, keepdims=True)
        out_ref[:, start : start + HEAD_DIM] = (factor * (unturned - normed * inner)).astype(BF16)
        out_ref[:, start + HEAD_DIM : start + 2 * HEAD_DIM] = both[:, HEAD_DIM:].astype(BF16)


def row_grads(first, place, sums, raw, cosine, sine, after):
    return pl.pallas_call(
        functools.partial(rows_kernel, first),
        in_specs=[pl.BlockSpec(memory_space=pltpu.SMEM)]
        + [pl.BlockSpec(memory_space=pltpu.VMEM)] * 4
        + [pl.BlockSpec(memory_space=pl.ANY)] * len(after),
        out_shape=jax.ShapeDtypeStruct(sums.shape[1:], BF16),
        compiler_params=pltpu.CompilerParams(vmem_limit_bytes=VMEM),
        cost_estimate=FREE,
        name="row_grads",
    )(place, sums, raw, cosine, sine, *after)


def advantage_of(rewards, group_ids):
    onehot = (group_ids[:, None] == jnp.arange(NADV, dtype=jnp.int32)[None, :]).astype(F32)
    sums = jnp.stack(
        [
            jnp.sum(onehot, axis=0),
            jnp.sum(onehot * rewards[:, None], axis=0),
            jnp.sum(onehot * (rewards * rewards)[:, None], axis=0),
        ]
    )
    names = ("chip", "core", "resp")
    peers = lax.axis_size(names)
    sums = jnp.sum(everyone(jnp.broadcast_to(sums[None], (peers,) + sums.shape), names), axis=0)
    members = jnp.maximum(sums[0], 1.0)
    mean = sums[1] / members
    spread = jnp.sqrt(jnp.maximum(sums[2] / members - mean * mean, 0.0))
    own_mean = jnp.sum(onehot * mean[None, :], axis=1)
    own_spread = jnp.sum(onehot * spread[None, :], axis=1)
    return (rewards - own_mean) / jnp.maximum(own_spread, 0.5)


def exponent_of(payload):
    return payload[-MARK : 1 - MARK].astype(F32)


def values_of(payload, exponent):
    return payload[:-MARK].astype(F32) * jnp.exp2(exponent)


def body(prompt_states, response_states, queries, grad_output, key_weight, value_weight, rewards, lengths, group_ids):
    depth, width = key_weight.shape
    shard = prompt_states.shape[1]
    rows = response_states.shape[2]
    n_grp = lax.axis_size("grp")
    n_chip = lax.axis_size("chip")
    n_core = lax.axis_size("core")
    n_resp = lax.axis_size("resp")
    n_prompt = n_chip * n_core
    grp = lax.axis_index("grp")
    chip = lax.axis_index("chip")
    core = lax.axis_index("core")
    resp = lax.axis_index("resp")
    prompt = chip * n_core + core
    prompt_len = shard * n_prompt
    block = depth // (n_prompt * n_resp * n_grp)
    sub = shard // n_resp
    states = response_states[0, 0]
    own_prompt = prompt_states[0]

    groups = [(e, c) for e in range(n_grp) for c in range(n_core)]
    counts = (n_grp, n_chip, n_core, n_resp, block)
    place = jnp.stack([grp, chip, core, resp]).astype(jnp.int32)
    beside, across_grp = select_columns(states, own_prompt, place, groups[1:], counts)
    chosen = across_grp
    beside = exchange(beside, [("core", 1)])
    across_grp = exchange(across_grp, [("grp", 1)])

    advantage = advantage_of(rewards[0], group_ids[0])
    length = lengths[0]
    coef = advantage / length.astype(F32)
    ints = jnp.stack([length[0], prompt.astype(jnp.int32)])

    prompt_cos, prompt_sin = rotary_tables(prompt * shard + jnp.arange(shard, dtype=jnp.int32))
    own_cos, own_sin = rotary_tables(prompt_len + jnp.arange(rows, dtype=jnp.int32))
    (prompt_raw, mine, own_raw, own_both), parts = project(
        own_prompt,
        states,
        key_weight,
        value_weight,
        jnp.concatenate([prompt_cos, own_cos]),
        jnp.concatenate([prompt_sin, own_sin]),
        place,
        groups[:1],
        counts,
        chosen,
    )
    prompt_both = [mine]
    for d in range(1, n_prompt):
        prompt_both.append(exchange(mine, [("chip", d // n_core), ("core", d % n_core)]))

    def run(first, per, chunk_first, chunk_heads, grads, sums, after):
        grads, sums, own_g = attend(
            first, per, first - chunk_first, chunk_heads, coef, ints, queries[0, 0], grad_output[0, 0],
            prompt_both, own_both, own_raw, own_cos, own_sin, [grads, sums], after,
        )
        return grads, sums, own_g.reshape(-1, rows)

    def across(own_g):
        return [exchange(own_g, [("grp", e)]) for e in range(1, n_grp)]

    def everywhere(own_g, hops):
        held = [own_g] + hops
        return [exchange(held[e], [("core", c)]) if c else held[e] for e, c in groups]

    def row_tokens(sums, chunk_first, after):
        sums = everyone(sums.reshape(n_prompt * n_resp, sub, -1), ("chip", "core", "resp"))
        own = row_grads(chunk_first, place, sums, prompt_raw, prompt_cos, prompt_sin, after)
        held = jnp.concatenate([own] + [exchange(own, [("core", c)]) for c in range(1, n_core)])
        return [held] + [exchange(held, [("grp", e)]) for e in range(1, n_grp)]

    wide = n_resp * block

    def chip_terms(shares):
        return [exchange(shares[:, d * wide : (d + 1) * wide].astype(jnp.float16), [("chip", d)]) for d in range(1, n_chip)]

    def resp_terms(kept, sent):
        exponents = [exponent_of(x) for x in [kept] + sent]
        top = functools.reduce(jnp.maximum, exponents) + math.ceil(math.log2(n_chip))
        total = values_of(kept, exponents[0] - top)
        for payload, exponent in zip(sent, exponents[1:]):
            total = total + values_of(payload, exponent - top)
        payload = jnp.concatenate([total, jnp.broadcast_to(top, (MARK, wide))], axis=0).astype(jnp.float16)
        half = lax.dynamic_slice_in_dim(total * jnp.exp2(top - 14.0), resp * block, block, 1)
        pieces = []
        for d in range(1, n_resp):
            part = lax.dynamic_slice_in_dim(payload, (resp ^ d) * block, block, 1)
            pieces.append(exchange(part, [("resp", d)]))
        return half, pieces

    def finish(half, pieces):
        for part in pieces:
            half = half + values_of(part, exponent_of(part) - 14.0)
        return half, exchange(half, [("grp", 1)])

    early, late = CALLS
    grads, sums_early, g_early = run(0, early, 0, early, None, None, [])
    hops_early = across(g_early)
    across_grp = tied(across_grp, g_early)
    grads, sums_late, g_late = run(early, late, early, late, grads, None, [beside, across_grp])
    parts = [(parts[0], None), (beside, None), (across_grp, 0), (exchange(across_grp, [("core", 1)]), 1)]
    hops_early = [tied(x, g_late) for x in hops_early]
    g_late = tied(g_late, *hops_early)
    sums_late = tied(sums_late, *hops_early)
    hops_late = across(g_late)
    tokens = row_tokens(sums_early, 0, [g_late])
    shares_early = weight_shares(parts, everywhere(g_early, hops_early), tokens)
    tokens = row_tokens(sums_late, early, [])
    shares_late = weight_shares(parts, everywhere(g_late, hops_late), tokens)
    sent_early = chip_terms(shares_early)
    sent_late = chip_terms(shares_late)
    half_early, pieces_early = resp_terms(shares_early[:, :wide], sent_early)
    done_early = finish(half_early, pieces_early)
    sent_late = [lax.optimization_barrier((x, done_early[0]))[0] for x in sent_late]
    half_late, pieces_late = resp_terms(shares_late[:, :wide], sent_late)
    finished = [done_early, finish(half_late, pieces_late)]

    mine = jnp.concatenate([pair[0] for pair in finished], axis=0)
    theirs = jnp.concatenate([pair[1] for pair in finished], axis=0)
    low = jnp.where(grp == 0, mine, theirs)
    high = jnp.where(grp == 0, theirs, mine)
    both = jnp.concatenate([low, high], axis=1).reshape(width // HEAD_DIM, 2, HEAD_DIM, n_grp * block)
    sides = [both[:, side].reshape(width, n_grp * block).T for side in range(2)]
    return (grads[None, None], sides[0], sides[1])


def solution(mesh):
    devices = mesh.devices
    n_grp, n_prompt, n_resp = devices.shape
    split = jax.sharding.Mesh(
        devices.reshape(n_grp, n_prompt // 2, 2, n_resp), ("grp", "chip", "core", "resp")
    )
    prompt = ("chip", "core")
    owner = ("chip", "core", "resp")
    placed = (
        P("grp", prompt, None),
        P("grp", owner, None, None),
        P("grp", owner, None, None),
        P("grp", owner, None, None),
        P(),
        P(),
        P("grp", owner),
        P("grp", owner),
        P("grp", owner),
    )
    return jax.shard_map(
        body,
        mesh=split,
        in_specs=placed,
        out_specs=(
            P("grp", owner, None, None),
            P(owner, None),
            P(owner, None),
        ),
        check_vma=False,
    )
```

```python
import functools
import math

import jax
import jax.numpy as jnp
from jax import lax
from jax.experimental import pallas as pl
from jax.experimental.pallas import tpu as pltpu
from jax.sharding import PartitionSpec as P

HEAD_DIM = 128
NADV = 8
THETA = 1000000.0
EPS = 1e-06
STATE_BOUND = 6.0
QROWS = 128
CALLS = (2, 2)
VMEM = 58 * 1024 * 1024
MARK = 16
PROJECT_BLOCK = 1024
WEIGHT_BLOCK = 256

BF16 = jnp.bfloat16
FREE = pl.CostEstimate(flops=1, bytes_accessed=1, transcendentals=0)
F32 = jnp.float32
BY_ROWS = (((0,), (0,)), ((), ()))
BY_COLS = (((1,), (1,)), ((), ()))


def exchange(value, steps):
    names = tuple(name for name, step in steps if step)
    sizes = [lax.axis_size(name) for name in names]
    mask = 0
    for (name, step), size in zip([s for s in steps if s[1]], sizes):
        mask = mask * size + step
    total = math.prod(sizes)
    return lax.ppermute(value, names, [(j, j ^ mask) for j in range(total)])


def rotary_tables(positions):
    lane = jnp.arange(HEAD_DIM, dtype=jnp.int32)
    half = HEAD_DIM // 2
    steps = (lane % half).astype(F32)
    freq = THETA ** (-2.0 * steps / HEAD_DIM)
    angle = positions.astype(F32)[:, None] * freq[None, :]
    sign = jnp.where(lane < half, -1.0, 1.0).astype(F32)
    return jnp.cos(angle), jnp.sin(angle) * sign[None, :]


def column_copies(groups, counts, place_ref, source_ref, rows, sub_ref, first, targets, sems):
    n_grp, n_chip, n_core, n_resp, block = counts
    sub = targets[0].shape[0] - rows
    own = pl.ds(pl.multiple_of(first + place_ref[3] * sub, sub), sub)
    copies = []
    for i, (e, c) in enumerate(groups):
        copies.append([])
        for d in range(n_chip):
            for r in range(n_resp):
                chip = place_ref[1] ^ d
                core = place_ref[2] ^ c
                index = ((chip * n_core + core) * n_resp + r) * n_grp + (place_ref[0] ^ e)
                source = pl.ds(pl.multiple_of(index * block, block), block)
                j = d * n_resp + r
                target = slice(j * block, (j + 1) * block)
                pairs = (
                    (source_ref.at[:rows, source], targets[i].at[:rows, target]),
                    (sub_ref.at[own, source], targets[i].at[rows:, target]),
                )
                for m, (src, dst) in enumerate(pairs):
                    copies[-1].append(pltpu.make_async_copy(src, dst, sems.at[i, j, m]))
                    copies[-1][-1].start()
    return copies


def select_kernel(groups, counts, place_ref, states_ref, prompt_ref, *refs):
    beside, across, held, sems, out_sems = refs
    outs = [beside, across.at[0], across.at[1]]
    targets = [held.at[i] for i in range(len(groups))]
    copies = column_copies(groups, counts, place_ref, states_ref, states_ref.shape[0], prompt_ref, 0, targets, sems)
    leaving = []
    for i, arriving in enumerate(copies):
        for copy in arriving:
            copy.wait()
        leaving.append(pltpu.make_async_copy(held.at[i], outs[i], out_sems.at[i]))
        leaving[-1].start()
    for copy in leaving:
        copy.wait()


def select_columns(states, prompt, place, groups, counts):
    n_grp, n_chip, n_core, n_resp, block = counts
    sub = prompt.shape[0] // n_resp
    rows = states.shape[0] + sub
    width = n_chip * n_resp * block
    if block % HEAD_DIM:
        own = lax.dynamic_slice_in_dim(prompt, place[3] * sub, sub, 0)
        split = jnp.concatenate([states, own]).reshape(rows, n_chip, n_core, n_resp, n_grp, block)
        out = []
        for e, c in groups:
            part = lax.dynamic_index_in_dim(split, place[0] ^ e, 4, keepdims=False)
            part = lax.dynamic_index_in_dim(part, place[2] ^ c, 2, keepdims=False)
            parts = [lax.dynamic_index_in_dim(part, place[1] ^ d, 1, keepdims=False) for d in range(n_chip)]
            out.append(jnp.stack(parts, axis=1).reshape(rows, width))
        return out if len(out) == 1 else (out[0], jnp.stack(out[1:]))
    return pl.pallas_call(
        functools.partial(select_kernel, groups, counts),
        in_specs=[pl.BlockSpec(memory_space=pltpu.SMEM)] + [pl.BlockSpec(memory_space=pl.ANY)] * 2,
        out_specs=[pl.BlockSpec(memory_space=pl.ANY)] * 2,
        out_shape=[
            jax.ShapeDtypeStruct((rows, width), states.dtype),
            jax.ShapeDtypeStruct((2, rows, width), states.dtype),
        ],
        scratch_shapes=[
            pltpu.VMEM((len(groups), rows, width), states.dtype),
            pltpu.SemaphoreType.DMA((len(groups), n_chip * n_resp, 2)),
            pltpu.SemaphoreType.DMA((len(groups),)),
        ],
        compiler_params=pltpu.CompilerParams(vmem_limit_bytes=VMEM),
        cost_estimate=FREE,
        name="select_columns",
    )(place, states, prompt)


def project_kernel(groups, counts, place_ref, p_hbm, r_hbm, wk_hbm, wv_hbm, cos_ref, sin_ref, after_ref, *refs):
    p_raw, p_both, r_raw, r_both = refs[:4]
    selected = refs[4:-7]
    x_ref, wk_ref, wv_ref, acc_k, acc_v, sems, out_sems = refs[-7:]
    depth, width = wk_ref.shape
    shard = p_raw.shape[0]
    rows = r_raw.shape[0]
    steps = depth // PROJECT_BLOCK
    copies = []
    for k in range(steps):
        part = slice(k * PROJECT_BLOCK, (k + 1) * PROJECT_BLOCK)
        pairs = (
            (wk_hbm.at[part, :], wk_ref.at[part, :]),
            (p_hbm.at[:, part], x_ref.at[rows:, part]),
            (r_hbm.at[:, part], x_ref.at[:rows, part]),
            (wv_hbm.at[part, :], wv_ref.at[part, :]),
        )
        copies.append([pltpu.make_async_copy(src, dst, sems.at[k, i]) for i, (src, dst) in enumerate(pairs)])
        for copy in copies[-1]:
            copy.start()
    leaving = []
    for k in range(steps):
        part = slice(k * PROJECT_BLOCK, (k + 1) * PROJECT_BLOCK)
        for copy in copies[k]:
            copy.wait()
        if k == steps - 1 and selected:
            leaving = column_copies(groups, counts, place_ref, x_ref, rows, x_ref, rows, selected, out_sems)
        for acc, w_ref in ((acc_k, wk_ref), (acc_v, wv_ref)):
            share = jnp.dot(x_ref[:, part], w_ref[part, :], preferred_element_type=F32)
            if k:
                acc[...] += share
            else:
                acc[...] = share
    for place, raw_ref, both_ref in (
        (slice(rows, rows + shard), p_raw, p_both),
        (slice(0, rows), r_raw, r_both),
    ):
        both_ref[:, width:] = acc_v[place, :].astype(BF16)
        raw_ref[...] = acc_k[place, :]
        cosine = cos_ref[place, :]
        sine = sin_ref[place, :]
        for head in range(width // HEAD_DIM):
            cols = slice(head * HEAD_DIM, (head + 1) * HEAD_DIM)
            x = acc_k[place, cols]
            factor = lax.rsqrt(jnp.mean(x * x, axis=-1, keepdims=True) + EPS)
            normed = x * factor
            turned = normed * cosine + pltpu.roll(normed, HEAD_DIM // 2, 1) * sine
            both_ref[:, cols] = turned.astype(BF16)
    for copy in sum(leaving, []):
        copy.wait()


def project(prompt, response, key_weight, value_weight, cosine, sine, place, groups, counts, after):
    depth, width = key_weight.shape
    shard, rows = prompt.shape[0], response.shape[0]
    n_grp, n_chip, n_core, n_resp, block = counts
    direct = block % HEAD_DIM == 0
    blocks = n_chip * n_resp
    part = jax.ShapeDtypeStruct((rows + shard // n_resp, blocks * block), BF16)
    any_spec = pl.BlockSpec(memory_space=pl.ANY)
    vmem = pl.BlockSpec(memory_space=pltpu.VMEM)
    out = pl.pallas_call(
        functools.partial(project_kernel, groups, counts),
        in_specs=[pl.BlockSpec(memory_space=pltpu.SMEM)] + [any_spec] * 4 + [vmem] * 2 + [any_spec],
        out_specs=[vmem] * 4 + ([any_spec] * len(groups) if direct else []),
        out_shape=[
            jax.ShapeDtypeStruct((count, scale * width), kind)
            for count in (shard, rows)
            for scale, kind in ((1, F32), (2, BF16))
        ]
        + ([part] * len(groups) if direct else []),
        scratch_shapes=[pltpu.VMEM((shard + rows, depth), BF16)]
        + [pltpu.VMEM((depth, width), BF16)] * 2
        + [pltpu.VMEM((shard + rows, width), F32)] * 2
        + [
            pltpu.SemaphoreType.DMA((depth // PROJECT_BLOCK, 4)),
            pltpu.SemaphoreType.DMA((len(groups), blocks, 2)),
        ],
        compiler_params=pltpu.CompilerParams(vmem_limit_bytes=VMEM),
        cost_estimate=FREE,
        name="project",
    )(place, prompt, response, key_weight, value_weight, cosine, sine, after)
    if direct:
        return out[:4], out[4:]
    return out, select_columns(response, prompt, place, groups, counts)


def tied(value, *others):
    return pl.pallas_call(
        lambda *refs: None,
        in_specs=[pl.BlockSpec(memory_space=pl.ANY)] * (1 + len(others)),
        out_specs=pl.BlockSpec(memory_space=pl.ANY),
        out_shape=jax.ShapeDtypeStruct(value.shape, value.dtype),
        input_output_aliases={0: 0},
        cost_estimate=FREE,
        name="tied",
    )(value, *others)


def attend_kernel(parts, fold, coef_ref, ints_ref, q_ref, go_ref, *refs):
    prompt_k = refs[:parts]
    prompt_v = refs[parts : 2 * parts]
    own_k, own_v, raw_ref, cos_ref, sin_ref = refs[2 * parts : 2 * parts + 5]
    gq_ref, sum_ref, g_ref, k_all, v_all, k_turned, acc_k, acc_v = refs[-8:]
    rows = q_ref.shape[0]
    shard = prompt_k[0].shape[0]
    prompt_len = parts * shard
    scale = HEAD_DIM ** (-0.5)
    length = ints_ref[0]
    coef = coef_ref[0]
    prompt = ints_ref[1]
    for d in range(parts):
        place = pl.ds(pl.multiple_of((prompt ^ d) * shard, shard), shard)
        k_all[place, :] = prompt_k[d][...]
        v_all[place, :] = prompt_v[d][...]
    k_all[prompt_len:, :] = own_k[...]
    v_all[prompt_len:, :] = own_v[...]
    k_turned[...] = k_all[...].T
    acc_k[...] = jnp.zeros_like(acc_k)
    acc_v[...] = jnp.zeros_like(acc_v)
    def one_block(first):
        seen = prompt_len + first + QROWS
        width = fold * QROWS
        position = first + lax.broadcasted_iota(jnp.int32, (QROWS, HEAD_DIM), 0)
        factor = jnp.where(position < length, coef, 0.0)
        parts_q = []
        parts_d = []
        for f in range(fold):
            cols = slice(f * HEAD_DIM, (f + 1) * HEAD_DIM)
            parts_q.append(q_ref[first : first + QROWS, cols])
            parts_d.append((go_ref[first : first + QROWS, cols].astype(F32) * factor).astype(BF16))
        query = jnp.concatenate(parts_q, axis=0)
        dout = jnp.concatenate(parts_d, axis=0)
        scores = lax.dot_general(k_all[:seen, :], query, BY_COLS, preferred_element_type=F32)
        key = lax.broadcasted_iota(jnp.int32, (QROWS, width), 0)
        row = lax.broadcasted_iota(jnp.int32, (QROWS, width), 1) % QROWS
        tail = jnp.where(key <= row, scores[seen - QROWS :, :], -jnp.inf)
        scores = jnp.concatenate([scores[: seen - QROWS, :], tail], axis=0)
        peak = jnp.max(scores, axis=0, keepdims=True)
        expo = jnp.exp2((scores - peak) * (scale * math.log2(math.e)))
        probs = expo * (1.0 / jnp.sum(expo, axis=0, keepdims=True))
        probs_b = probs.astype(BF16)
        dprobs = lax.dot_general(v_all[:seen, :], dout, BY_COLS, preferred_element_type=F32)
        delta = jnp.sum(probs_b.astype(F32) * dprobs, axis=0, keepdims=True)
        dscores = (probs * (dprobs - delta)).astype(BF16)
        grad_q = jnp.dot(k_turned[:, :seen], dscores, preferred_element_type=F32) * scale
        for f in range(fold):
            gq_ref[first : first + QROWS, f * HEAD_DIM : (f + 1) * HEAD_DIM] = (
                grad_q[:, f * QROWS : (f + 1) * QROWS].T.astype(BF16)
            )
        acc_k[:seen, :] += jnp.dot(dscores, query, preferred_element_type=F32)
        acc_v[:seen, :] += jnp.dot(probs_b, dout, preferred_element_type=F32)

    for start in range(0, rows, 2 * QROWS):

        @pl.when(start < length)
        def _(start=start):
            one_block(start)
            one_block(start + QROWS)

        @pl.when(start >= length)
        def _(start=start):
            gq_ref[start : start + 2 * QROWS, :] = jnp.zeros((2 * QROWS, gq_ref.shape[1]), BF16)

    sum_ref[:, :HEAD_DIM] = acc_k[:prompt_len, :] * scale
    sum_ref[:, HEAD_DIM:] = acc_v[:prompt_len, :]
    x = raw_ref[...]
    factor = lax.rsqrt(jnp.mean(x * x, axis=-1, keepdims=True) + EPS)
    normed = x * factor
    grad = acc_k[prompt_len:, :] * scale
    unturned = grad * cos_ref[...] - pltpu.roll(grad, HEAD_DIM // 2, 1) * sin_ref[...]
    inner = jnp.mean(unturned * normed, axis=-1, keepdims=True)
    g_ref[0, 0] = (factor * (unturned - normed * inner)).T.astype(BF16)
    g_ref[0, 1] = acc_v[prompt_len:, :].T.astype(BF16)


def attend(first, per, offset, chunk_heads, coef, ints, query, grad_output, prompt_both, own_both, raw, cosine, sine, before, after):
    rows, query_width = query.shape
    width = raw.shape[1]
    heads = width // HEAD_DIM
    fold = query_width // width
    parts = len(prompt_both)
    shard = prompt_both[0].shape[0]
    prompt_len = parts * shard
    total = prompt_len + rows
    here = lambda h: (0, first + h)
    there = lambda h: (0, heads + first + h)
    scalar = pl.BlockSpec(memory_space=pltpu.SMEM)
    table = pl.BlockSpec((rows, HEAD_DIM), lambda h: (0, 0))
    wide = pl.BlockSpec((rows, fold * HEAD_DIM), here)
    in_specs = [scalar, scalar, wide, wide]
    in_specs += [pl.BlockSpec((shard, HEAD_DIM), here)] * parts + [pl.BlockSpec((shard, HEAD_DIM), there)] * parts
    in_specs += [pl.BlockSpec((rows, HEAD_DIM), here), pl.BlockSpec((rows, HEAD_DIM), there)]
    in_specs += [pl.BlockSpec((rows, HEAD_DIM), here), table, table]
    operands = [coef, ints, query, grad_output, *prompt_both, *prompt_both, own_both, own_both, raw, cosine, sine]
    aliases = {}
    for i, value in enumerate(before):
        if value is not None:
            aliases[len(operands)] = i
            in_specs.append(pl.BlockSpec(memory_space=pl.ANY))
            operands.append(value)
    in_specs += [pl.BlockSpec(memory_space=pl.ANY)] * len(after)
    operands += after
    return pl.pallas_call(
        functools.partial(attend_kernel, parts, fold),
        grid=(per,),
        in_specs=in_specs,
        out_specs=[
            wide,
            pl.BlockSpec((prompt_len, 2 * HEAD_DIM), lambda h: (0, offset + h)),
            pl.BlockSpec((1, 2, HEAD_DIM, rows), lambda h: (h, 0, 0, 0)),
        ],
        out_shape=[
            jax.ShapeDtypeStruct((rows, query_width), BF16),
            jax.ShapeDtypeStruct((prompt_len, 2 * chunk_heads * HEAD_DIM), F32),
            jax.ShapeDtypeStruct((per, 2, HEAD_DIM, rows), BF16),
        ],
        scratch_shapes=[
            pltpu.VMEM((total, HEAD_DIM), BF16),
            pltpu.VMEM((total, HEAD_DIM), BF16),
            pltpu.VMEM((HEAD_DIM, total), BF16),
            pltpu.VMEM((total, HEAD_DIM), F32),
            pltpu.VMEM((total, HEAD_DIM), F32),
        ],
        input_output_aliases=aliases,
        compiler_params=pltpu.CompilerParams(vmem_limit_bytes=VMEM),
        cost_estimate=FREE,
        name="attend",
    )(*operands)


def everyone(value, names):
    return lax.all_to_all(value, names, split_axis=0, concat_axis=0, tiled=True)


def weight_kernel(places, tokens_count, *refs):
    parts = len(places)
    states = [ref if index is None else ref.at[index] for ref, index in zip(refs, places)]
    grads = refs[parts : 2 * parts]
    tokens = refs[2 * parts : 2 * parts + tokens_count]
    out_ref, held, side, result, sems, side_sems, out_sems = refs[2 * parts + tokens_count :]
    columns, rows = grads[0].shape
    depth = out_ref.shape[1]
    total_rows = parts * held.shape[1]
    steps = depth // WEIGHT_BLOCK
    arriving = []
    for d in range(parts):
        arriving.append(pltpu.make_async_copy(grads[d], side.at[:, d * rows : (d + 1) * rows], side_sems.at[d]))
        arriving[-1].start()
    pieces = []
    for j in range(steps):
        lanes = slice(j * WEIGHT_BLOCK, (j + 1) * WEIGHT_BLOCK)
        pieces.append([])
        for d in range(parts):
            pieces[-1].append(pltpu.make_async_copy(states[d].at[:, lanes], held.at[d, :, lanes], sems.at[j, d]))
            pieces[-1][-1].start()
    for copy in arriving:
        copy.wait()
    token = jnp.concatenate([token[...] for token in tokens], axis=0)
    highest = jnp.max(jnp.abs(token.astype(F32)), axis=0, keepdims=True)
    peak = jnp.max(highest, axis=1, keepdims=True)
    highest = jnp.max(jnp.abs(side[...]), axis=0, keepdims=True).astype(F32)
    peak = jnp.maximum(peak, jnp.max(highest, axis=1, keepdims=True))
    reach = jnp.maximum(peak * (STATE_BOUND * total_rows), 1e-30)
    exponent = jnp.clip(jnp.ceil(jnp.log2(reach)), -90.0, 120.0)
    scale = jnp.exp2(14.0 - exponent)
    leaving = []
    for j in range(steps):
        lanes = slice(j * WEIGHT_BLOCK, (j + 1) * WEIGHT_BLOCK)
        for copy in pieces[j]:
            copy.wait()
        response = jnp.concatenate([held[d, :rows, lanes] for d in range(parts)], axis=0)
        prompt = jnp.concatenate([held[d, rows:, lanes] for d in range(parts)], axis=0)
        total = jnp.dot(side[...], response, preferred_element_type=F32)
        total = total + lax.dot_general(token, prompt, BY_ROWS, preferred_element_type=F32)
        result[:columns, lanes] = total * scale
        result[columns:, lanes] = jnp.broadcast_to(exponent, (MARK, WEIGHT_BLOCK))
        leaving.append(pltpu.make_async_copy(result.at[:, lanes], out_ref.at[:, lanes], out_sems.at[j]))
        leaving[-1].start()
    for copy in leaving:
        copy.wait()


def weight_shares(states, grads, tokens):
    parts = len(states)
    rows, depth = states[0][0].shape
    columns = grads[0].shape[0]
    steps = depth // WEIGHT_BLOCK
    out = jax.ShapeDtypeStruct((columns + MARK, depth), F32)
    return pl.pallas_call(
        functools.partial(weight_kernel, [index for _, index in states], len(tokens)),
        in_specs=[pl.BlockSpec(memory_space=pl.ANY)] * (2 * parts)
        + [pl.BlockSpec(memory_space=pltpu.VMEM)] * len(tokens),
        out_specs=pl.BlockSpec(memory_space=pl.ANY),
        out_shape=out,
        scratch_shapes=[
            pltpu.VMEM((parts, rows, depth), BF16),
            pltpu.VMEM((columns, parts * grads[0].shape[1]), BF16),
            pltpu.VMEM(out.shape, F32),
            pltpu.SemaphoreType.DMA((steps, parts)),
            pltpu.SemaphoreType.DMA((parts,)),
            pltpu.SemaphoreType.DMA((steps,)),
        ],
        compiler_params=pltpu.CompilerParams(vmem_limit_bytes=VMEM),
        cost_estimate=FREE,
        name="weight_shares",
    )(*[array for array, _ in states], *grads, *tokens)


def rows_kernel(first, place_ref, sums_ref, raw_ref, cos_ref, sin_ref, *refs):
    out_ref = refs[-1]
    sub = sums_ref.shape[1]
    own = pl.ds(pl.multiple_of(place_ref[3] * sub, sub), sub)
    turn = pl.ds(pl.multiple_of(cos_ref.shape[0] - raw_ref.shape[0] + place_ref[3] * sub, sub), sub)
    cosine = cos_ref[turn, :]
    sine = sin_ref[turn, :]
    for head in range(out_ref.shape[1] // (2 * HEAD_DIM)):
        start = 2 * head * HEAD_DIM
        both = jnp.sum(sums_ref[:, :, start : start + 2 * HEAD_DIM], axis=0)
        grad = both[:, :HEAD_DIM]
        raw = raw_ref[own, (first + head) * HEAD_DIM : (first + head + 1) * HEAD_DIM]
        factor = lax.rsqrt(jnp.mean(raw * raw, axis=-1, keepdims=True) + EPS)
        normed = raw * factor
        unturned = grad * cosine - pltpu.roll(grad, HEAD_DIM // 2, 1) * sine
        inner = jnp.mean(unturned * normed, axis=-1, keepdims=True)
        out_ref[:, start : start + HEAD_DIM] = (factor * (unturned - normed * inner)).astype(BF16)
        out_ref[:, start + HEAD_DIM : start + 2 * HEAD_DIM] = both[:, HEAD_DIM:].astype(BF16)


def row_grads(first, place, sums, raw, cosine, sine, after):
    return pl.pallas_call(
        functools.partial(rows_kernel, first),
        in_specs=[pl.BlockSpec(memory_space=pltpu.SMEM)]
        + [pl.BlockSpec(memory_space=pltpu.VMEM)] * 4
        + [pl.BlockSpec(memory_space=pl.ANY)] * len(after),
        out_shape=jax.ShapeDtypeStruct(sums.shape[1:], BF16),
        compiler_params=pltpu.CompilerParams(vmem_limit_bytes=VMEM),
        cost_estimate=FREE,
        name="row_grads",
    )(place, sums, raw, cosine, sine, *after)


def advantage_of(rewards, group_ids):
    onehot = (group_ids[:, None] == jnp.arange(NADV, dtype=jnp.int32)[None, :]).astype(F32)
    sums = jnp.stack(
        [
            jnp.sum(onehot, axis=0),
            jnp.sum(onehot * rewards[:, None], axis=0),
            jnp.sum(onehot * (rewards * rewards)[:, None], axis=0),
        ]
    )
    names = ("chip", "core", "resp")
    peers = lax.axis_size(names)
    sums = jnp.sum(everyone(jnp.broadcast_to(sums[None], (peers,) + sums.shape), names), axis=0)
    members = jnp.maximum(sums[0], 1.0)
    mean = sums[1] / members
    spread = jnp.sqrt(jnp.maximum(sums[2] / members - mean * mean, 0.0))
    own_mean = jnp.sum(onehot * mean[None, :], axis=1)
    own_spread = jnp.sum(onehot * spread[None, :], axis=1)
    return (rewards - own_mean) / jnp.maximum(own_spread, 0.5)


def exponent_of(payload):
    return payload[-MARK : 1 - MARK].astype(F32)


def values_of(payload, exponent):
    return payload[:-MARK].astype(F32) * jnp.exp2(exponent)


def body(prompt_states, response_states, queries, grad_output, key_weight, value_weight, rewards, lengths, group_ids):
    depth, width = key_weight.shape
    shard = prompt_states.shape[1]
    rows = response_states.shape[2]
    n_grp = lax.axis_size("grp")
    n_chip = lax.axis_size("chip")
    n_core = lax.axis_size("core")
    n_resp = lax.axis_size("resp")
    n_prompt = n_chip * n_core
    grp = lax.axis_index("grp")
    chip = lax.axis_index("chip")
    core = lax.axis_index("core")
    resp = lax.axis_index("resp")
    prompt = chip * n_core + core
    prompt_len = shard * n_prompt
    block = depth // (n_prompt * n_resp * n_grp)
    sub = shard // n_resp
    states = response_states[0, 0]
    own_prompt = prompt_states[0]

    groups = [(e, c) for e in range(n_grp) for c in range(n_core)]
    counts = (n_grp, n_chip, n_core, n_resp, block)
    place = jnp.stack([grp, chip, core, resp]).astype(jnp.int32)
    beside, across_grp = select_columns(states, own_prompt, place, groups[1:], counts)
    chosen = across_grp
    beside = exchange(beside, [("core", 1)])
    across_grp = exchange(across_grp, [("grp", 1)])

    advantage = advantage_of(rewards[0], group_ids[0])
    length = lengths[0]
    coef = advantage / length.astype(F32)
    ints = jnp.stack([length[0], prompt.astype(jnp.int32)])

    line = jnp.arange(rows + shard, dtype=jnp.int32)
    cosine, sine = rotary_tables(jnp.where(line < rows, prompt_len + line, prompt * shard + line - rows))
    (prompt_raw, mine, own_raw, own_both), parts = project(
        own_prompt,
        states,
        key_weight,
        value_weight,
        cosine,
        sine,
        place,
        groups[:1],
        counts,
        chosen,
    )
    prompt_both = [mine]
    for d in range(1, n_prompt):
        prompt_both.append(exchange(mine, [("chip", d // n_core), ("core", d % n_core)]))

    def run(first, per, chunk_first, chunk_heads, grads, sums, after):
        grads, sums, own_g = attend(
            first, per, first - chunk_first, chunk_heads, coef, ints, queries[0, 0], grad_output[0, 0],
            prompt_both, own_both, own_raw, cosine, sine, [grads, sums], after,
        )
        return grads, sums, own_g.reshape(-1, rows)

    def across(own_g):
        return [exchange(own_g, [("grp", e)]) for e in range(1, n_grp)]

    def everywhere(own_g, hops):
        held = [own_g] + hops
        return [exchange(held[e], [("core", c)]) if c else held[e] for e, c in groups]

    def row_tokens(sums, chunk_first, after):
        sums = everyone(sums.reshape(n_prompt * n_resp, sub, -1), ("chip", "core", "resp"))
        own = row_grads(chunk_first, place, sums, prompt_raw, cosine, sine, after)
        held = jnp.concatenate([own] + [exchange(own, [("core", c)]) for c in range(1, n_core)])
        return [held] + across(held)

    wide = n_resp * block

    def chip_terms(shares):
        return [exchange(shares[:, d * wide : (d + 1) * wide].astype(jnp.float16), [("chip", d)]) for d in range(1, n_chip)]

    def resp_terms(kept, sent):
        exponents = [exponent_of(x) for x in [kept] + sent]
        top = functools.reduce(jnp.maximum, exponents) + math.ceil(math.log2(n_chip))
        total = values_of(kept, exponents[0] - top)
        for payload, exponent in zip(sent, exponents[1:]):
            total = total + values_of(payload, exponent - top)
        payload = jnp.concatenate([total, jnp.broadcast_to(top, (MARK, wide))], axis=0).astype(jnp.float16)
        half = lax.dynamic_slice_in_dim(total * jnp.exp2(top - 14.0), resp * block, block, 1)
        pieces = []
        for d in range(1, n_resp):
            part = lax.dynamic_slice_in_dim(payload, (resp ^ d) * block, block, 1)
            pieces.append(exchange(part, [("resp", d)]))
        return half, pieces

    def finish(half, pieces):
        for part in pieces:
            half = half + values_of(part, exponent_of(part) - 14.0)
        return half, exchange(half, [("grp", 1)])

    early, late = CALLS
    grads, sums_early, g_early = run(0, early, 0, early, None, None, [])
    hops_early = across(g_early)
    across_grp = tied(across_grp, g_early)
    grads, sums_late, g_late = run(early, late, early, late, grads, None, [beside, across_grp])
    parts = [(parts[0], None), (beside, None), (across_grp, 0), (exchange(across_grp, [("core", 1)]), 1)]
    hops_early = [tied(x, g_late) for x in hops_early]
    g_late = tied(g_late, *hops_early)
    sums_late = tied(sums_late, *hops_early)
    tokens = row_tokens(sums_early, 0, [g_late])
    g_late = tied(g_late, *tokens[1:])
    hops_late = across(g_late)
    shares_early = weight_shares(parts, everywhere(g_early, hops_early), tokens)
    tokens = row_tokens(sums_late, early, [])
    shares_late = weight_shares(parts, everywhere(g_late, hops_late), tokens)
    sent_early = chip_terms(shares_early)
    sent_late = chip_terms(shares_late)
    half_early, pieces_early = resp_terms(shares_early[:, :wide], sent_early)
    done_early = finish(half_early, pieces_early)
    sent_late = [lax.optimization_barrier((x, done_early[0]))[0] for x in sent_late]
    half_late, pieces_late = resp_terms(shares_late[:, :wide], sent_late)
    finished = [done_early, finish(half_late, pieces_late)]

    mine = jnp.concatenate([pair[0] for pair in finished], axis=0)
    theirs = jnp.concatenate([pair[1] for pair in finished], axis=0)
    low = jnp.where(grp == 0, mine, theirs)
    high = jnp.where(grp == 0, theirs, mine)
    both = jnp.concatenate([low, high], axis=1).reshape(width // HEAD_DIM, 2, HEAD_DIM, n_grp * block)
    sides = [both[:, side].reshape(width, n_grp * block).T for side in range(2)]
    return (grads[None, None], sides[0], sides[1])


def solution(mesh):
    devices = mesh.devices
    n_grp, n_prompt, n_resp = devices.shape
    split = jax.sharding.Mesh(
        devices.reshape(n_grp, n_prompt // 2, 2, n_resp), ("grp", "chip", "core", "resp")
    )
    prompt = ("chip", "core")
    owner = ("chip", "core", "resp")
    placed = (
        P("grp", prompt, None),
        P("grp", owner, None, None),
        P("grp", owner, None, None),
        P("grp", owner, None, None),
        P(),
        P(),
        P("grp", owner),
        P("grp", owner),
        P("grp", owner),
    )
    return jax.shard_map(
        body,
        mesh=split,
        in_specs=placed,
        out_specs=(
            P("grp", owner, None, None),
            P(owner, None),
            P(owner, None),
        ),
        check_vma=False,
    )
```

```python
import functools
import math

import jax
import jax.numpy as jnp
from jax import lax
from jax.experimental import pallas as pl
from jax.experimental.pallas import tpu as pltpu
from jax.sharding import PartitionSpec as P

HEAD_DIM = 128
NADV = 8
THETA = 1000000.0
EPS = 1e-06
STATE_BOUND = 6.0
QROWS = 128
CALLS = (2, 2)
VMEM = 58 * 1024 * 1024
MARK = 16
PROJECT_BLOCK = 1024

BF16 = jnp.bfloat16
FREE = pl.CostEstimate(flops=1, bytes_accessed=1, transcendentals=0)
F32 = jnp.float32
BY_ROWS = (((0,), (0,)), ((), ()))
BY_COLS = (((1,), (1,)), ((), ()))


def exchange(value, steps):
    names = tuple(name for name, step in steps if step)
    sizes = [lax.axis_size(name) for name in names]
    mask = 0
    for (name, step), size in zip([s for s in steps if s[1]], sizes):
        mask = mask * size + step
    total = math.prod(sizes)
    return lax.ppermute(value, names, [(j, j ^ mask) for j in range(total)])


def rotary_tables(positions):
    lane = jnp.arange(HEAD_DIM, dtype=jnp.int32)
    half = HEAD_DIM // 2
    steps = (lane % half).astype(F32)
    freq = THETA ** (-2.0 * steps / HEAD_DIM)
    angle = positions.astype(F32)[:, None] * freq[None, :]
    sign = jnp.where(lane < half, -1.0, 1.0).astype(F32)
    return jnp.cos(angle), jnp.sin(angle) * sign[None, :]


def column_copies(groups, counts, place_ref, source_ref, rows, sub_ref, first, targets, sems):
    n_grp, n_chip, n_core, n_resp, block = counts
    sub = targets[0].shape[0] - rows
    own = pl.ds(pl.multiple_of(first + place_ref[3] * sub, sub), sub)
    copies = []
    for i, (e, c) in enumerate(groups):
        copies.append([])
        for d in range(n_chip):
            for r in range(n_resp):
                chip = place_ref[1] ^ d
                core = place_ref[2] ^ c
                index = ((chip * n_core + core) * n_resp + r) * n_grp + (place_ref[0] ^ e)
                source = pl.ds(pl.multiple_of(index * block, block), block)
                j = d * n_resp + r
                target = slice(j * block, (j + 1) * block)
                pairs = (
                    (source_ref.at[:rows, source], targets[i].at[:rows, target]),
                    (sub_ref.at[own, source], targets[i].at[rows:, target]),
                )
                for m, (src, dst) in enumerate(pairs):
                    copies[-1].append(pltpu.make_async_copy(src, dst, sems.at[i, j, m]))
                    copies[-1][-1].start()
    return copies


def select_kernel(groups, counts, place_ref, states_ref, prompt_ref, *refs):
    beside, across, held, sems, out_sems = refs
    outs = [beside, across.at[0], across.at[1]]
    targets = [held.at[i] for i in range(len(groups))]
    copies = column_copies(groups, counts, place_ref, states_ref, states_ref.shape[0], prompt_ref, 0, targets, sems)
    leaving = []
    for i, arriving in enumerate(copies):
        for copy in arriving:
            copy.wait()
        leaving.append(pltpu.make_async_copy(held.at[i], outs[i], out_sems.at[i]))
        leaving[-1].start()
    for copy in leaving:
        copy.wait()


def select_columns(states, prompt, place, groups, counts):
    n_grp, n_chip, n_core, n_resp, block = counts
    sub = prompt.shape[0] // n_resp
    rows = states.shape[0] + sub
    width = n_chip * n_resp * block
    if block % HEAD_DIM:
        own = lax.dynamic_slice_in_dim(prompt, place[3] * sub, sub, 0)
        split = jnp.concatenate([states, own]).reshape(rows, n_chip, n_core, n_resp, n_grp, block)
        out = []
        for e, c in groups:
            part = lax.dynamic_index_in_dim(split, place[0] ^ e, 4, keepdims=False)
            part = lax.dynamic_index_in_dim(part, place[2] ^ c, 2, keepdims=False)
            parts = [lax.dynamic_index_in_dim(part, place[1] ^ d, 1, keepdims=False) for d in range(n_chip)]
            out.append(jnp.stack(parts, axis=1).reshape(rows, width))
        return out if len(out) == 1 else (out[0], jnp.stack(out[1:]))
    return pl.pallas_call(
        functools.partial(select_kernel, groups, counts),
        in_specs=[pl.BlockSpec(memory_space=pltpu.SMEM)] + [pl.BlockSpec(memory_space=pl.ANY)] * 2,
        out_specs=[pl.BlockSpec(memory_space=pl.ANY)] * 2,
        out_shape=[
            jax.ShapeDtypeStruct((rows, width), states.dtype),
            jax.ShapeDtypeStruct((2, rows, width), states.dtype),
        ],
        scratch_shapes=[
            pltpu.VMEM((len(groups), rows, width), states.dtype),
            pltpu.SemaphoreType.DMA((len(groups), n_chip * n_resp, 2)),
            pltpu.SemaphoreType.DMA((len(groups),)),
        ],
        compiler_params=pltpu.CompilerParams(vmem_limit_bytes=VMEM),
        cost_estimate=FREE,
        name="select_columns",
    )(place, states, prompt)


def project_kernel(groups, counts, place_ref, p_hbm, r_hbm, wk_hbm, wv_hbm, cos_ref, sin_ref, after_ref, *refs):
    p_raw, p_both, r_raw, r_both = refs[:4]
    selected = refs[4:-7]
    x_ref, wk_ref, wv_ref, acc_k, acc_v, sems, out_sems = refs[-7:]
    depth, width = wk_ref.shape
    shard = p_raw.shape[0]
    rows = r_raw.shape[0]
    steps = depth // PROJECT_BLOCK
    copies = []
    for k in range(steps):
        part = slice(k * PROJECT_BLOCK, (k + 1) * PROJECT_BLOCK)
        pairs = (
            (wk_hbm.at[part, :], wk_ref.at[part, :]),
            (p_hbm.at[:, part], x_ref.at[rows:, part]),
            (r_hbm.at[:, part], x_ref.at[:rows, part]),
            (wv_hbm.at[part, :], wv_ref.at[part, :]),
        )
        copies.append([pltpu.make_async_copy(src, dst, sems.at[k, i]) for i, (src, dst) in enumerate(pairs)])
        for copy in copies[-1]:
            copy.start()
    leaving = []
    for k in range(steps):
        part = slice(k * PROJECT_BLOCK, (k + 1) * PROJECT_BLOCK)
        for copy in copies[k]:
            copy.wait()
        if k == steps - 1 and selected:
            leaving = column_copies(groups, counts, place_ref, x_ref, rows, x_ref, rows, selected, out_sems)
        for acc, w_ref in ((acc_k, wk_ref), (acc_v, wv_ref)):
            share = jnp.dot(x_ref[:, part], w_ref[part, :], preferred_element_type=F32)
            if k:
                acc[...] += share
            else:
                acc[...] = share
    for place, raw_ref, both_ref in (
        (slice(rows, rows + shard), p_raw, p_both),
        (slice(0, rows), r_raw, r_both),
    ):
        both_ref[:, width:] = acc_v[place, :].astype(BF16)
        raw_ref[...] = acc_k[place, :]
        cosine = cos_ref[place, :]
        sine = sin_ref[place, :]
        for head in range(width // HEAD_DIM):
            cols = slice(head * HEAD_DIM, (head + 1) * HEAD_DIM)
            x = acc_k[place, cols]
            factor = lax.rsqrt(jnp.mean(x * x, axis=-1, keepdims=True) + EPS)
            normed = x * factor
            turned = normed * cosine + pltpu.roll(normed, HEAD_DIM // 2, 1) * sine
            both_ref[:, cols] = turned.astype(BF16)
    for copy in sum(leaving, []):
        copy.wait()


def project(prompt, response, key_weight, value_weight, cosine, sine, place, groups, counts, after):
    depth, width = key_weight.shape
    shard, rows = prompt.shape[0], response.shape[0]
    n_grp, n_chip, n_core, n_resp, block = counts
    direct = block % HEAD_DIM == 0
    blocks = n_chip * n_resp
    part = jax.ShapeDtypeStruct((rows + shard // n_resp, blocks * block), BF16)
    any_spec = pl.BlockSpec(memory_space=pl.ANY)
    vmem = pl.BlockSpec(memory_space=pltpu.VMEM)
    out = pl.pallas_call(
        functools.partial(project_kernel, groups, counts),
        in_specs=[pl.BlockSpec(memory_space=pltpu.SMEM)] + [any_spec] * 4 + [vmem] * 2 + [any_spec],
        out_specs=[vmem] * 4 + ([any_spec] * len(groups) if direct else []),
        out_shape=[
            jax.ShapeDtypeStruct((count, scale * width), kind)
            for count in (shard, rows)
            for scale, kind in ((1, F32), (2, BF16))
        ]
        + ([part] * len(groups) if direct else []),
        scratch_shapes=[pltpu.VMEM((shard + rows, depth), BF16)]
        + [pltpu.VMEM((depth, width), BF16)] * 2
        + [pltpu.VMEM((shard + rows, width), F32)] * 2
        + [
            pltpu.SemaphoreType.DMA((depth // PROJECT_BLOCK, 4)),
            pltpu.SemaphoreType.DMA((len(groups), blocks, 2)),
        ],
        compiler_params=pltpu.CompilerParams(vmem_limit_bytes=VMEM),
        cost_estimate=FREE,
        name="project",
    )(place, prompt, response, key_weight, value_weight, cosine, sine, after)
    if direct:
        return out[:4], out[4:]
    return out, select_columns(response, prompt, place, groups, counts)


def tied(value, *others):
    return pl.pallas_call(
        lambda *refs: None,
        in_specs=[pl.BlockSpec(memory_space=pl.ANY)] * (1 + len(others)),
        out_specs=pl.BlockSpec(memory_space=pl.ANY),
        out_shape=jax.ShapeDtypeStruct(value.shape, value.dtype),
        input_output_aliases={0: 0},
        cost_estimate=FREE,
        name="tied",
    )(value, *others)


def attend_kernel(parts, fold, coef_ref, ints_ref, q_ref, go_ref, *refs):
    prompt_k = refs[:parts]
    prompt_v = refs[parts : 2 * parts]
    own_k, own_v, raw_ref, cos_ref, sin_ref = refs[2 * parts : 2 * parts + 5]
    gq_ref, sum_ref, g_ref, k_all, v_all, k_turned, acc_k, acc_v = refs[-8:]
    rows = q_ref.shape[0]
    shard = prompt_k[0].shape[0]
    prompt_len = parts * shard
    scale = HEAD_DIM ** (-0.5)
    length = ints_ref[0]
    coef = coef_ref[0]
    prompt = ints_ref[1]
    for d in range(parts):
        place = pl.ds(pl.multiple_of((prompt ^ d) * shard, shard), shard)
        k_all[place, :] = prompt_k[d][...]
        v_all[place, :] = prompt_v[d][...]
    k_all[prompt_len:, :] = own_k[...]
    v_all[prompt_len:, :] = own_v[...]
    k_turned[...] = k_all[...].T
    acc_k[...] = jnp.zeros_like(acc_k)
    acc_v[...] = jnp.zeros_like(acc_v)
    def one_block(first):
        seen = prompt_len + first + QROWS
        width = fold * QROWS
        position = first + lax.broadcasted_iota(jnp.int32, (QROWS, HEAD_DIM), 0)
        factor = jnp.where(position < length, coef, 0.0)
        parts_q = []
        parts_d = []
        for f in range(fold):
            cols = slice(f * HEAD_DIM, (f + 1) * HEAD_DIM)
            parts_q.append(q_ref[first : first + QROWS, cols])
            parts_d.append((go_ref[first : first + QROWS, cols].astype(F32) * factor).astype(BF16))
        query = jnp.concatenate(parts_q, axis=0)
        dout = jnp.concatenate(parts_d, axis=0)
        scores = lax.dot_general(k_all[:seen, :], query, BY_COLS, preferred_element_type=F32)
        key = lax.broadcasted_iota(jnp.int32, (QROWS, width), 0)
        row = lax.broadcasted_iota(jnp.int32, (QROWS, width), 1) % QROWS
        tail = jnp.where(key <= row, scores[seen - QROWS :, :], -jnp.inf)
        scores = jnp.concatenate([scores[: seen - QROWS, :], tail], axis=0)
        peak = jnp.max(scores, axis=0, keepdims=True)
        expo = jnp.exp2((scores - peak) * (scale * math.log2(math.e)))
        probs = expo * (1.0 / jnp.sum(expo, axis=0, keepdims=True))
        probs_b = probs.astype(BF16)
        dprobs = lax.dot_general(v_all[:seen, :], dout, BY_COLS, preferred_element_type=F32)
        delta = jnp.sum(probs_b.astype(F32) * dprobs, axis=0, keepdims=True)
        dscores = (probs * (dprobs - delta)).astype(BF16)
        grad_q = jnp.dot(k_turned[:, :seen], dscores, preferred_element_type=F32) * scale
        for f in range(fold):
            gq_ref[first : first + QROWS, f * HEAD_DIM : (f + 1) * HEAD_DIM] = (
                grad_q[:, f * QROWS : (f + 1) * QROWS].T.astype(BF16)
            )
        acc_k[:seen, :] += jnp.dot(dscores, query, preferred_element_type=F32)
        acc_v[:seen, :] += jnp.dot(probs_b, dout, preferred_element_type=F32)

    for start in range(0, rows, 2 * QROWS):

        @pl.when(start < length)
        def _(start=start):
            one_block(start)
            one_block(start + QROWS)

        @pl.when(start >= length)
        def _(start=start):
            gq_ref[start : start + 2 * QROWS, :] = jnp.zeros((2 * QROWS, gq_ref.shape[1]), BF16)

    sum_ref[:, :HEAD_DIM] = acc_k[:prompt_len, :] * scale
    sum_ref[:, HEAD_DIM:] = acc_v[:prompt_len, :]
    x = raw_ref[...]
    factor = lax.rsqrt(jnp.mean(x * x, axis=-1, keepdims=True) + EPS)
    normed = x * factor
    grad = acc_k[prompt_len:, :] * scale
    unturned = grad * cos_ref[...] - pltpu.roll(grad, HEAD_DIM // 2, 1) * sin_ref[...]
    inner = jnp.mean(unturned * normed, axis=-1, keepdims=True)
    g_ref[0, 0] = (factor * (unturned - normed * inner)).T.astype(BF16)
    g_ref[0, 1] = acc_v[prompt_len:, :].T.astype(BF16)


def attend(first, per, coef, ints, query, grad_output, prompt_both, own_both, raw, cosine, sine, before, after):
    rows, query_width = query.shape
    width = raw.shape[1]
    heads = width // HEAD_DIM
    fold = query_width // width
    parts = len(prompt_both)
    shard = prompt_both[0].shape[0]
    prompt_len = parts * shard
    total = prompt_len + rows
    here = lambda h: (0, first + h)
    there = lambda h: (0, heads + first + h)
    scalar = pl.BlockSpec(memory_space=pltpu.SMEM)
    table = pl.BlockSpec((rows, HEAD_DIM), lambda h: (0, 0))
    wide = pl.BlockSpec((rows, fold * HEAD_DIM), here)
    in_specs = [scalar, scalar, wide, wide]
    in_specs += [pl.BlockSpec((shard, HEAD_DIM), here)] * parts + [pl.BlockSpec((shard, HEAD_DIM), there)] * parts
    in_specs += [pl.BlockSpec((rows, HEAD_DIM), here), pl.BlockSpec((rows, HEAD_DIM), there)]
    in_specs += [pl.BlockSpec((rows, HEAD_DIM), here), table, table]
    operands = [coef, ints, query, grad_output, *prompt_both, *prompt_both, own_both, own_both, raw, cosine, sine]
    aliases = {}
    for i, value in enumerate(before):
        if value is not None:
            aliases[len(operands)] = i
            in_specs.append(pl.BlockSpec(memory_space=pl.ANY))
            operands.append(value)
    in_specs += [pl.BlockSpec(memory_space=pl.ANY)] * len(after)
    operands += after
    return pl.pallas_call(
        functools.partial(attend_kernel, parts, fold),
        grid=(per,),
        in_specs=in_specs,
        out_specs=[
            wide,
            pl.BlockSpec((prompt_len, 2 * HEAD_DIM), here),
            pl.BlockSpec((1, 2, HEAD_DIM, rows), lambda h: (h, 0, 0, 0)),
        ],
        out_shape=[
            jax.ShapeDtypeStruct((rows, query_width), BF16),
            jax.ShapeDtypeStruct((prompt_len, 2 * width), F32),
            jax.ShapeDtypeStruct((per, 2, HEAD_DIM, rows), BF16),
        ],
        scratch_shapes=[
            pltpu.VMEM((total, HEAD_DIM), BF16),
            pltpu.VMEM((total, HEAD_DIM), BF16),
            pltpu.VMEM((HEAD_DIM, total), BF16),
            pltpu.VMEM((total, HEAD_DIM), F32),
            pltpu.VMEM((total, HEAD_DIM), F32),
        ],
        input_output_aliases=aliases,
        compiler_params=pltpu.CompilerParams(vmem_limit_bytes=VMEM),
        cost_estimate=FREE,
        name="attend",
    )(*operands)


def everyone(value, names):
    return lax.all_to_all(value, names, split_axis=0, concat_axis=0, tiled=True)


def weight_kernel(parts, *refs):
    states = refs[:parts]
    grads = refs[parts : 2 * parts]
    out_ref, peak_ref, side_ref = refs[-3:]
    rows = grads[0].shape[1]

    @pl.when(pl.program_id(0) == 0)
    def _():
        highest = jnp.zeros((1, rows), F32)
        for d, grad in enumerate(grads):
            value = grad[...]
            side_ref[:, d * rows : (d + 1) * rows] = value
            highest = jnp.maximum(highest, jnp.max(jnp.abs(value), axis=0, keepdims=True).astype(F32))
        peak_ref[...] = jnp.broadcast_to(jnp.max(highest, axis=1, keepdims=True), peak_ref.shape)

    response = jnp.concatenate([part[...] for part in states], axis=0)
    out_ref[...] = jnp.dot(side_ref[...], response, preferred_element_type=F32)


def weight_shares(states, grads, after):
    parts = len(states)
    depth = states[0][0].shape[1]
    columns, rows = grads[0].shape
    step = 2 * HEAD_DIM
    return pl.pallas_call(
        functools.partial(weight_kernel, parts),
        grid=(depth // step,),
        in_specs=[
            pl.BlockSpec((rows, step), lambda j: (0, j))
            if index is None
            else pl.BlockSpec((None, rows, step), lambda j, index=index: (index, 0, j))
            for _, index in states
        ]
        + [pl.BlockSpec(grad.shape, lambda j: (0, 0)) for grad in grads]
        + [pl.BlockSpec(memory_space=pl.ANY)] * len(after),
        out_specs=[pl.BlockSpec((columns, step), lambda j: (0, j)), pl.BlockSpec((8, HEAD_DIM), lambda j: (0, 0))],
        out_shape=[jax.ShapeDtypeStruct((columns, depth), F32), jax.ShapeDtypeStruct((8, HEAD_DIM), F32)],
        scratch_shapes=[pltpu.VMEM((columns, parts * rows), BF16)],
        compiler_params=pltpu.CompilerParams(vmem_limit_bytes=VMEM),
        cost_estimate=FREE,
        name="weight_shares",
    )(*[array for array, _ in states], *grads, *after)


def rows_kernel(place_ref, sums_ref, raw_ref, cos_ref, sin_ref, *refs):
    out_ref = refs[-1]
    sub = sums_ref.shape[1]
    own = pl.ds(pl.multiple_of(place_ref[3] * sub, sub), sub)
    turn = pl.ds(pl.multiple_of(cos_ref.shape[0] - raw_ref.shape[0] + place_ref[3] * sub, sub), sub)
    cosine = cos_ref[turn, :]
    sine = sin_ref[turn, :]
    for head in range(out_ref.shape[1] // (2 * HEAD_DIM)):
        start = 2 * head * HEAD_DIM
        both = jnp.sum(sums_ref[:, :, start : start + 2 * HEAD_DIM], axis=0)
        grad = both[:, :HEAD_DIM]
        raw = raw_ref[own, head * HEAD_DIM : (head + 1) * HEAD_DIM]
        factor = lax.rsqrt(jnp.mean(raw * raw, axis=-1, keepdims=True) + EPS)
        normed = raw * factor
        unturned = grad * cosine - pltpu.roll(grad, HEAD_DIM // 2, 1) * sine
        inner = jnp.mean(unturned * normed, axis=-1, keepdims=True)
        out_ref[:, start : start + HEAD_DIM] = (factor * (unturned - normed * inner)).astype(BF16)
        out_ref[:, start + HEAD_DIM : start + 2 * HEAD_DIM] = both[:, HEAD_DIM:].astype(BF16)


def row_grads(place, sums, raw, cosine, sine, after):
    return pl.pallas_call(
        rows_kernel,
        in_specs=[pl.BlockSpec(memory_space=pltpu.SMEM)]
        + [pl.BlockSpec(memory_space=pltpu.VMEM)] * 4
        + [pl.BlockSpec(memory_space=pl.ANY)] * len(after),
        out_shape=jax.ShapeDtypeStruct(sums.shape[1:], BF16),
        compiler_params=pltpu.CompilerParams(vmem_limit_bytes=VMEM),
        cost_estimate=FREE,
        name="row_grads",
    )(place, sums, raw, cosine, sine, *after)


def advantage_of(rewards, group_ids):
    onehot = (group_ids[:, None] == jnp.arange(NADV, dtype=jnp.int32)[None, :]).astype(F32)
    sums = jnp.stack(
        [
            jnp.sum(onehot, axis=0),
            jnp.sum(onehot * rewards[:, None], axis=0),
            jnp.sum(onehot * (rewards * rewards)[:, None], axis=0),
        ]
    )
    names = ("chip", "core", "resp")
    peers = lax.axis_size(names)
    sums = jnp.sum(everyone(jnp.broadcast_to(sums[None], (peers,) + sums.shape), names), axis=0)
    members = jnp.maximum(sums[0], 1.0)
    mean = sums[1] / members
    spread = jnp.sqrt(jnp.maximum(sums[2] / members - mean * mean, 0.0))
    own_mean = jnp.sum(onehot * mean[None, :], axis=1)
    own_spread = jnp.sum(onehot * spread[None, :], axis=1)
    return (rewards - own_mean) / jnp.maximum(own_spread, 0.5)


def exponent_of(payload):
    return payload[-MARK : 1 - MARK].astype(F32)


def values_of(payload, exponent):
    return payload[:-MARK].astype(F32) * jnp.exp2(exponent)


def body(prompt_states, response_states, queries, grad_output, key_weight, value_weight, rewards, lengths, group_ids):
    depth, width = key_weight.shape
    shard = prompt_states.shape[1]
    rows = response_states.shape[2]
    n_grp = lax.axis_size("grp")
    n_chip = lax.axis_size("chip")
    n_core = lax.axis_size("core")
    n_resp = lax.axis_size("resp")
    n_prompt = n_chip * n_core
    grp = lax.axis_index("grp")
    chip = lax.axis_index("chip")
    core = lax.axis_index("core")
    resp = lax.axis_index("resp")
    prompt = chip * n_core + core
    prompt_len = shard * n_prompt
    block = depth // (n_prompt * n_resp * n_grp)
    sub = shard // n_resp
    states = response_states[0, 0]
    own_prompt = prompt_states[0]

    groups = [(e, c) for e in range(n_grp) for c in range(n_core)]
    counts = (n_grp, n_chip, n_core, n_resp, block)
    place = jnp.stack([grp, chip, core, resp]).astype(jnp.int32)
    beside, across_grp = select_columns(states, own_prompt, place, groups[1:], counts)
    chosen = across_grp
    beside = exchange(beside, [("core", 1)])
    across_grp = exchange(across_grp, [("grp", 1)])

    advantage = advantage_of(rewards[0], group_ids[0])
    length = lengths[0]
    coef = advantage / length.astype(F32)
    ints = jnp.stack([length[0], prompt.astype(jnp.int32)])

    line = jnp.arange(rows + shard, dtype=jnp.int32)
    cosine, sine = rotary_tables(jnp.where(line < rows, prompt_len + line, prompt * shard + line - rows))
    (prompt_raw, mine, own_raw, own_both), parts = project(
        own_prompt,
        states,
        key_weight,
        value_weight,
        cosine,
        sine,
        place,
        groups[:1],
        counts,
        chosen,
    )
    prompt_both = [mine]
    for d in range(1, n_prompt):
        prompt_both.append(exchange(mine, [("chip", d // n_core), ("core", d % n_core)]))

    def run(first, per, before, after):
        grads, sums, own_g = attend(
            first, per, coef, ints, queries[0, 0], grad_output[0, 0],
            prompt_both, own_both, own_raw, cosine, sine, before, after,
        )
        return [grads, sums], own_g.reshape(-1, rows)

    def across(own_g):
        return [exchange(own_g, [("grp", e)]) for e in range(1, n_grp)]

    def everywhere(own_g, hops):
        held = [own_g] + hops
        return [exchange(held[e], [("core", c)]) if c else held[e] for e, c in groups]

    wide = n_resp * block

    def chip_terms(shares, peak, token):
        peak = jnp.maximum(peak[0, 0], jnp.max(jnp.abs(token.astype(F32))))
        reach = jnp.maximum(peak * (STATE_BOUND * len(groups) * (rows + sub)), 1e-30)
        exponent = jnp.clip(jnp.ceil(jnp.log2(reach)), -90.0, 120.0)
        total = shares + lax.dot_general(token, prompt_part, BY_ROWS, preferred_element_type=F32)
        total = total * jnp.exp2(14.0 - exponent)
        tail = jnp.full((MARK, wide), exponent, F32)
        sent = []
        for d in range(1, n_chip):
            payload = jnp.concatenate([total[:, d * wide : (d + 1) * wide], tail], axis=0).astype(jnp.float16)
            sent.append(exchange(payload, [("chip", d)]))
        return total[:, :wide], exponent, sent

    def resp_terms(kept, exponent, sent):
        exponents = [exponent_of(x) for x in sent]
        top = functools.reduce(jnp.maximum, exponents, exponent) + math.ceil(math.log2(n_chip))
        total = kept * jnp.exp2(exponent - top)
        for payload, other in zip(sent, exponents):
            total = total + values_of(payload, other - top)
        payload = jnp.concatenate([total, jnp.broadcast_to(top, (MARK, wide))], axis=0).astype(jnp.float16)
        half = lax.dynamic_slice_in_dim(total * jnp.exp2(top - 14.0), resp * block, block, 1)
        pieces = []
        for d in range(1, n_resp):
            part = lax.dynamic_slice_in_dim(payload, (resp ^ d) * block, block, 1)
            pieces.append(exchange(part, [("resp", d)]))
        return half, pieces

    def finish(half, pieces):
        for part in pieces:
            half = half + values_of(part, exponent_of(part) - 14.0)
        return half, exchange(half, [("grp", 1)])

    early, late = CALLS
    before, g_early = run(0, early, [None, None], [])
    hops_early = across(g_early)
    across_grp = tied(across_grp, g_early)
    (grads, sums), g_late = run(early, late, before, [beside, across_grp])
    parts = [(parts[0], None), (beside, None), (across_grp, 0), (exchange(across_grp, [("core", 1)]), 1)]
    prompt_part = jnp.concatenate([x[rows:] if i is None else x[i, rows:] for x, i in parts], axis=0)
    hops_early = [tied(x, g_late) for x in hops_early]
    g_late = tied(g_late, *hops_early)
    sums = tied(sums, *hops_early)
    hops_late = across(g_late)

    sums = everyone(sums.reshape(n_prompt * n_resp, sub, 2 * width), ("chip", "core", "resp"))
    shares_early, peak_early = weight_shares(parts, everywhere(g_early, hops_early), [])
    own = row_grads(place, sums, prompt_raw, cosine, sine, [peak_early])
    held = jnp.concatenate([own] + [exchange(own, [("core", c)]) for c in range(1, n_core)])
    tokens = jnp.concatenate([held] + across(held))
    cut = 2 * early * HEAD_DIM
    kept_early, exponent_early, sent_early = chip_terms(shares_early, peak_early, tokens[:, :cut])
    hops_late = [tied(x, peak_early) for x in hops_late]
    shares_late, peak_late = weight_shares(parts, everywhere(g_late, hops_late), [kept_early])
    kept_late, exponent_late, sent_late = chip_terms(shares_late, peak_late, tokens[:, cut:])
    half_early, pieces_early = resp_terms(kept_early, exponent_early, sent_early)
    done_early = finish(half_early, pieces_early)
    sent_late = [lax.optimization_barrier((x, done_early[0]))[0] for x in sent_late]
    half_late, pieces_late = resp_terms(kept_late, exponent_late, sent_late)
    finished = [done_early, finish(half_late, pieces_late)]

    mine = jnp.concatenate([pair[0] for pair in finished], axis=0)
    theirs = jnp.concatenate([pair[1] for pair in finished], axis=0)
    low = jnp.where(grp == 0, mine, theirs)
    high = jnp.where(grp == 0, theirs, mine)
    both = jnp.concatenate([low, high], axis=1).reshape(width // HEAD_DIM, 2, HEAD_DIM, n_grp * block)
    sides = [both[:, side].reshape(width, n_grp * block).T for side in range(2)]
    return (grads[None, None], sides[0], sides[1])


def solution(mesh):
    devices = mesh.devices
    n_grp, n_prompt, n_resp = devices.shape
    split = jax.sharding.Mesh(
        devices.reshape(n_grp, n_prompt // 2, 2, n_resp), ("grp", "chip", "core", "resp")
    )
    prompt = ("chip", "core")
    owner = ("chip", "core", "resp")
    placed = (
        P("grp", prompt, None),
        P("grp", owner, None, None),
        P("grp", owner, None, None),
        P("grp", owner, None, None),
        P(),
        P(),
        P("grp", owner),
        P("grp", owner),
        P("grp", owner),
    )
    return jax.shard_map(
        body,
        mesh=split,
        in_specs=placed,
        out_specs=(
            P("grp", owner, None, None),
            P(owner, None),
            P(owner, None),
        ),
        check_vma=False,
    )
```

```python
import functools
import math

import jax
import jax.numpy as jnp
from jax import lax
from jax.experimental import pallas as pl
from jax.experimental.pallas import tpu as pltpu
from jax.sharding import PartitionSpec as P

HEAD_DIM = 128
NADV = 8
THETA = 1000000.0
EPS = 1e-06
STATE_BOUND = 6.0
QROWS = 128
CALLS = (2, 2)
VMEM = 58 * 1024 * 1024
MARK = 16
PROJECT_BLOCK = 1024

BF16 = jnp.bfloat16
FREE = pl.CostEstimate(flops=1, bytes_accessed=1, transcendentals=0)
F32 = jnp.float32
BY_ROWS = (((0,), (0,)), ((), ()))
BY_COLS = (((1,), (1,)), ((), ()))


def exchange(value, steps):
    names = tuple(name for name, step in steps if step)
    sizes = [lax.axis_size(name) for name in names]
    mask = 0
    for (name, step), size in zip([s for s in steps if s[1]], sizes):
        mask = mask * size + step
    total = math.prod(sizes)
    return lax.ppermute(value, names, [(j, j ^ mask) for j in range(total)])


def rotary_tables(positions):
    lane = jnp.arange(HEAD_DIM, dtype=jnp.int32)
    half = HEAD_DIM // 2
    steps = (lane % half).astype(F32)
    freq = THETA ** (-2.0 * steps / HEAD_DIM)
    angle = positions.astype(F32)[:, None] * freq[None, :]
    sign = jnp.where(lane < half, -1.0, 1.0).astype(F32)
    return jnp.cos(angle), jnp.sin(angle) * sign[None, :]


def column_copies(groups, counts, place_ref, source_ref, rows, sub_ref, first, targets, sems):
    n_grp, n_chip, n_core, n_resp, block = counts
    sub = targets[0].shape[0] - rows
    own = pl.ds(pl.multiple_of(first + place_ref[3] * sub, sub), sub)
    copies = []
    for i, (e, c) in enumerate(groups):
        copies.append([])
        for d in range(n_chip):
            for r in range(n_resp):
                chip = place_ref[1] ^ d
                core = place_ref[2] ^ c
                index = ((chip * n_core + core) * n_resp + r) * n_grp + (place_ref[0] ^ e)
                source = pl.ds(pl.multiple_of(index * block, block), block)
                j = d * n_resp + r
                target = slice(j * block, (j + 1) * block)
                pairs = (
                    (source_ref.at[:rows, source], targets[i].at[:rows, target]),
                    (sub_ref.at[own, source], targets[i].at[rows:, target]),
                )
                for m, (src, dst) in enumerate(pairs):
                    copies[-1].append(pltpu.make_async_copy(src, dst, sems.at[i, j, m]))
                    copies[-1][-1].start()
    return copies


def select_kernel(groups, counts, place_ref, states_ref, prompt_ref, *refs):
    beside, across, held, sems, out_sems = refs
    outs = [beside, across.at[0], across.at[1]]
    targets = [held.at[i] for i in range(len(groups))]
    copies = column_copies(groups, counts, place_ref, states_ref, states_ref.shape[0], prompt_ref, 0, targets, sems)
    leaving = []
    for i, arriving in enumerate(copies):
        for copy in arriving:
            copy.wait()
        leaving.append(pltpu.make_async_copy(held.at[i], outs[i], out_sems.at[i]))
        leaving[-1].start()
    for copy in leaving:
        copy.wait()


def select_columns(states, prompt, place, groups, counts):
    n_grp, n_chip, n_core, n_resp, block = counts
    sub = prompt.shape[0] // n_resp
    rows = states.shape[0] + sub
    width = n_chip * n_resp * block
    if block % HEAD_DIM:
        own = lax.dynamic_slice_in_dim(prompt, place[3] * sub, sub, 0)
        split = jnp.concatenate([states, own]).reshape(rows, n_chip, n_core, n_resp, n_grp, block)
        out = []
        for e, c in groups:
            part = lax.dynamic_index_in_dim(split, place[0] ^ e, 4, keepdims=False)
            part = lax.dynamic_index_in_dim(part, place[2] ^ c, 2, keepdims=False)
            parts = [lax.dynamic_index_in_dim(part, place[1] ^ d, 1, keepdims=False) for d in range(n_chip)]
            out.append(jnp.stack(parts, axis=1).reshape(rows, width))
        return out if len(out) == 1 else (out[0], jnp.stack(out[1:]))
    return pl.pallas_call(
        functools.partial(select_kernel, groups, counts),
        in_specs=[pl.BlockSpec(memory_space=pltpu.SMEM)] + [pl.BlockSpec(memory_space=pl.ANY)] * 2,
        out_specs=[pl.BlockSpec(memory_space=pl.ANY)] * 2,
        out_shape=[
            jax.ShapeDtypeStruct((rows, width), states.dtype),
            jax.ShapeDtypeStruct((2, rows, width), states.dtype),
        ],
        scratch_shapes=[
            pltpu.VMEM((len(groups), rows, width), states.dtype),
            pltpu.SemaphoreType.DMA((len(groups), n_chip * n_resp, 2)),
            pltpu.SemaphoreType.DMA((len(groups),)),
        ],
        compiler_params=pltpu.CompilerParams(vmem_limit_bytes=VMEM),
        cost_estimate=FREE,
        name="select_columns",
    )(place, states, prompt)


def project_kernel(groups, counts, place_ref, p_hbm, r_hbm, wk_hbm, wv_hbm, cos_ref, sin_ref, after_ref, *refs):
    p_raw, p_both, r_raw, r_both = refs[:4]
    selected = refs[4:-7]
    x_ref, wk_ref, wv_ref, acc_k, acc_v, sems, out_sems = refs[-7:]
    depth, width = wk_ref.shape
    shard = p_raw.shape[0]
    rows = r_raw.shape[0]
    steps = depth // PROJECT_BLOCK
    copies = []
    for k in range(steps):
        part = slice(k * PROJECT_BLOCK, (k + 1) * PROJECT_BLOCK)
        pairs = (
            (wk_hbm.at[part, :], wk_ref.at[part, :]),
            (p_hbm.at[:, part], x_ref.at[rows:, part]),
            (r_hbm.at[:, part], x_ref.at[:rows, part]),
            (wv_hbm.at[part, :], wv_ref.at[part, :]),
        )
        copies.append([pltpu.make_async_copy(src, dst, sems.at[k, i]) for i, (src, dst) in enumerate(pairs)])
        for copy in copies[-1]:
            copy.start()
    leaving = []
    for k in range(steps):
        part = slice(k * PROJECT_BLOCK, (k + 1) * PROJECT_BLOCK)
        for copy in copies[k]:
            copy.wait()
        if k == steps - 1 and selected:
            leaving = column_copies(groups, counts, place_ref, x_ref, rows, x_ref, rows, selected, out_sems)
        for acc, w_ref in ((acc_k, wk_ref), (acc_v, wv_ref)):
            share = jnp.dot(x_ref[:, part], w_ref[part, :], preferred_element_type=F32)
            if k:
                acc[...] += share
            else:
                acc[...] = share
    for place, raw_ref, both_ref in (
        (slice(rows, rows + shard), p_raw, p_both),
        (slice(0, rows), r_raw, r_both),
    ):
        both_ref[:, width:] = acc_v[place, :].astype(BF16)
        raw_ref[...] = acc_k[place, :]
        cosine = cos_ref[place, :]
        sine = sin_ref[place, :]
        for head in range(width // HEAD_DIM):
            cols = slice(head * HEAD_DIM, (head + 1) * HEAD_DIM)
            x = acc_k[place, cols]
            factor = lax.rsqrt(jnp.mean(x * x, axis=-1, keepdims=True) + EPS)
            normed = x * factor
            turned = normed * cosine + pltpu.roll(normed, HEAD_DIM // 2, 1) * sine
            both_ref[:, cols] = turned.astype(BF16)
    for copy in sum(leaving, []):
        copy.wait()


def project(prompt, response, key_weight, value_weight, cosine, sine, place, groups, counts, after):
    depth, width = key_weight.shape
    shard, rows = prompt.shape[0], response.shape[0]
    n_grp, n_chip, n_core, n_resp, block = counts
    direct = block % HEAD_DIM == 0
    blocks = n_chip * n_resp
    part = jax.ShapeDtypeStruct((rows + shard // n_resp, blocks * block), BF16)
    any_spec = pl.BlockSpec(memory_space=pl.ANY)
    vmem = pl.BlockSpec(memory_space=pltpu.VMEM)
    out = pl.pallas_call(
        functools.partial(project_kernel, groups, counts),
        in_specs=[pl.BlockSpec(memory_space=pltpu.SMEM)] + [any_spec] * 4 + [vmem] * 2 + [any_spec],
        out_specs=[vmem] * 4 + ([any_spec] * len(groups) if direct else []),
        out_shape=[
            jax.ShapeDtypeStruct((count, scale * width), kind)
            for count in (shard, rows)
            for scale, kind in ((1, F32), (2, BF16))
        ]
        + ([part] * len(groups) if direct else []),
        scratch_shapes=[pltpu.VMEM((shard + rows, depth), BF16)]
        + [pltpu.VMEM((depth, width), BF16)] * 2
        + [pltpu.VMEM((shard + rows, width), F32)] * 2
        + [
            pltpu.SemaphoreType.DMA((depth // PROJECT_BLOCK, 4)),
            pltpu.SemaphoreType.DMA((len(groups), blocks, 2)),
        ],
        compiler_params=pltpu.CompilerParams(vmem_limit_bytes=VMEM),
        cost_estimate=FREE,
        name="project",
    )(place, prompt, response, key_weight, value_weight, cosine, sine, after)
    if direct:
        return out[:4], out[4:]
    return out, select_columns(response, prompt, place, groups, counts)


def tied(value, *others):
    return pl.pallas_call(
        lambda *refs: None,
        in_specs=[pl.BlockSpec(memory_space=pl.ANY)] * (1 + len(others)),
        out_specs=pl.BlockSpec(memory_space=pl.ANY),
        out_shape=jax.ShapeDtypeStruct(value.shape, value.dtype),
        input_output_aliases={0: 0},
        cost_estimate=FREE,
        name="tied",
    )(value, *others)


def attend_kernel(parts, fold, coef_ref, ints_ref, q_ref, go_ref, *refs):
    prompt_k = refs[:parts]
    prompt_v = refs[parts : 2 * parts]
    own_k, own_v, raw_ref, cos_ref, sin_ref = refs[2 * parts : 2 * parts + 5]
    gq_ref, sum_ref, g_ref, k_all, v_all, k_turned, acc_k, acc_v = refs[-8:]
    rows = q_ref.shape[0]
    shard = prompt_k[0].shape[0]
    prompt_len = parts * shard
    scale = HEAD_DIM ** (-0.5)
    length = ints_ref[0]
    coef = coef_ref[0]
    prompt = ints_ref[1]
    for d in range(parts):
        place = pl.ds(pl.multiple_of((prompt ^ d) * shard, shard), shard)
        k_all[place, :] = prompt_k[d][...]
        v_all[place, :] = prompt_v[d][...]
    k_all[prompt_len:, :] = own_k[...]
    v_all[prompt_len:, :] = own_v[...]
    k_turned[...] = k_all[...].T
    acc_k[...] = jnp.zeros_like(acc_k)
    acc_v[...] = jnp.zeros_like(acc_v)
    def one_block(first):
        seen = prompt_len + first + QROWS
        width = fold * QROWS
        position = first + lax.broadcasted_iota(jnp.int32, (QROWS, HEAD_DIM), 0)
        factor = jnp.where(position < length, coef, 0.0)
        parts_q = []
        parts_d = []
        for f in range(fold):
            cols = slice(f * HEAD_DIM, (f + 1) * HEAD_DIM)
            parts_q.append(q_ref[first : first + QROWS, cols])
            parts_d.append((go_ref[first : first + QROWS, cols].astype(F32) * factor).astype(BF16))
        query = jnp.concatenate(parts_q, axis=0)
        dout = jnp.concatenate(parts_d, axis=0)
        scores = lax.dot_general(k_all[:seen, :], query, BY_COLS, preferred_element_type=F32)
        key = lax.broadcasted_iota(jnp.int32, (QROWS, width), 0)
        row = lax.broadcasted_iota(jnp.int32, (QROWS, width), 1) % QROWS
        tail = jnp.where(key <= row, scores[seen - QROWS :, :], -jnp.inf)
        scores = jnp.concatenate([scores[: seen - QROWS, :], tail], axis=0)
        peak = jnp.max(scores, axis=0, keepdims=True)
        expo = jnp.exp2((scores - peak) * (scale * math.log2(math.e)))
        probs = expo * (1.0 / jnp.sum(expo, axis=0, keepdims=True))
        probs_b = probs.astype(BF16)
        dprobs = lax.dot_general(v_all[:seen, :], dout, BY_COLS, preferred_element_type=F32)
        delta = jnp.sum(probs_b.astype(F32) * dprobs, axis=0, keepdims=True)
        dscores = (probs * (dprobs - delta)).astype(BF16)
        grad_q = jnp.dot(k_turned[:, :seen], dscores, preferred_element_type=F32) * scale
        for f in range(fold):
            gq_ref[first : first + QROWS, f * HEAD_DIM : (f + 1) * HEAD_DIM] = (
                grad_q[:, f * QROWS : (f + 1) * QROWS].T.astype(BF16)
            )
        acc_k[:seen, :] += jnp.dot(dscores, query, preferred_element_type=F32)
        acc_v[:seen, :] += jnp.dot(probs_b, dout, preferred_element_type=F32)

    for start in range(0, rows, 2 * QROWS):

        @pl.when(start < length)
        def _(start=start):
            one_block(start)
            one_block(start + QROWS)

        @pl.when(start >= length)
        def _(start=start):
            gq_ref[start : start + 2 * QROWS, :] = jnp.zeros((2 * QROWS, gq_ref.shape[1]), BF16)

    sum_ref[:, :HEAD_DIM] = acc_k[:prompt_len, :] * scale
    sum_ref[:, HEAD_DIM:] = acc_v[:prompt_len, :]
    x = raw_ref[...]
    factor = lax.rsqrt(jnp.mean(x * x, axis=-1, keepdims=True) + EPS)
    normed = x * factor
    grad = acc_k[prompt_len:, :] * scale
    unturned = grad * cos_ref[...] - pltpu.roll(grad, HEAD_DIM // 2, 1) * sin_ref[...]
    inner = jnp.mean(unturned * normed, axis=-1, keepdims=True)
    g_ref[0, 0] = (factor * (unturned - normed * inner)).T.astype(BF16)
    g_ref[0, 1] = acc_v[prompt_len:, :].T.astype(BF16)


def attend(first, per, offset, chunk_heads, coef, ints, query, grad_output, prompt_both, own_both, raw, cosine, sine, before, after):
    rows, query_width = query.shape
    width = raw.shape[1]
    heads = width // HEAD_DIM
    fold = query_width // width
    parts = len(prompt_both)
    shard = prompt_both[0].shape[0]
    prompt_len = parts * shard
    total = prompt_len + rows
    here = lambda h: (0, first + h)
    there = lambda h: (0, heads + first + h)
    scalar = pl.BlockSpec(memory_space=pltpu.SMEM)
    table = pl.BlockSpec((rows, HEAD_DIM), lambda h: (0, 0))
    wide = pl.BlockSpec((rows, fold * HEAD_DIM), here)
    in_specs = [scalar, scalar, wide, wide]
    in_specs += [pl.BlockSpec((shard, HEAD_DIM), here)] * parts + [pl.BlockSpec((shard, HEAD_DIM), there)] * parts
    in_specs += [pl.BlockSpec((rows, HEAD_DIM), here), pl.BlockSpec((rows, HEAD_DIM), there)]
    in_specs += [pl.BlockSpec((rows, HEAD_DIM), here), table, table]
    operands = [coef, ints, query, grad_output, *prompt_both, *prompt_both, own_both, own_both, raw, cosine, sine]
    aliases = {}
    for i, value in enumerate(before):
        if value is not None:
            aliases[len(operands)] = i
            in_specs.append(pl.BlockSpec(memory_space=pl.ANY))
            operands.append(value)
    in_specs += [pl.BlockSpec(memory_space=pl.ANY)] * len(after)
    operands += after
    return pl.pallas_call(
        functools.partial(attend_kernel, parts, fold),
        grid=(per,),
        in_specs=in_specs,
        out_specs=[
            wide,
            pl.BlockSpec((prompt_len, 2 * HEAD_DIM), lambda h: (0, offset + h)),
            pl.BlockSpec((1, 2, HEAD_DIM, rows), lambda h: (h, 0, 0, 0)),
        ],
        out_shape=[
            jax.ShapeDtypeStruct((rows, query_width), BF16),
            jax.ShapeDtypeStruct((prompt_len, 2 * chunk_heads * HEAD_DIM), F32),
            jax.ShapeDtypeStruct((per, 2, HEAD_DIM, rows), BF16),
        ],
        scratch_shapes=[
            pltpu.VMEM((total, HEAD_DIM), BF16),
            pltpu.VMEM((total, HEAD_DIM), BF16),
            pltpu.VMEM((HEAD_DIM, total), BF16),
            pltpu.VMEM((total, HEAD_DIM), F32),
            pltpu.VMEM((total, HEAD_DIM), F32),
        ],
        input_output_aliases=aliases,
        compiler_params=pltpu.CompilerParams(vmem_limit_bytes=VMEM),
        cost_estimate=FREE,
        name="attend",
    )(*operands)


def everyone(value, names):
    return lax.all_to_all(value, names, split_axis=0, concat_axis=0, tiled=True)


def weight_kernel(parts, tokens_count, *refs):
    states = refs[:parts]
    grads = refs[parts : 2 * parts]
    tokens = refs[2 * parts : 2 * parts + tokens_count]
    out_ref, scale_ref, side_ref = refs[-3:]
    columns, rows = grads[0].shape
    total_rows = parts * states[0].shape[-2]

    @pl.when(pl.program_id(0) == 0)
    def _():
        highest = jnp.zeros((1, rows), F32)
        for d, grad in enumerate(grads):
            value = grad[...]
            side_ref[:, d * rows : (d + 1) * rows] = value
            highest = jnp.maximum(highest, jnp.max(jnp.abs(value), axis=0, keepdims=True).astype(F32))
        peak = jnp.max(highest, axis=1, keepdims=True)
        for token in tokens:
            highest = jnp.max(jnp.abs(token[...].astype(F32)), axis=0, keepdims=True)
            peak = jnp.maximum(peak, jnp.max(highest, axis=1, keepdims=True))
        reach = jnp.maximum(peak * (STATE_BOUND * total_rows), 1e-30)
        exponent = jnp.clip(jnp.ceil(jnp.log2(reach)), -90.0, 120.0)
        scale_ref[...] = jnp.broadcast_to(exponent, scale_ref.shape)

    exponent = scale_ref[:1, :1]
    response = jnp.concatenate([part[:rows, :] for part in states], axis=0)
    prompt = jnp.concatenate([part[rows:, :] for part in states], axis=0)
    token = jnp.concatenate([token[...] for token in tokens], axis=0)
    total = jnp.dot(side_ref[...], response, preferred_element_type=F32)
    total = total + lax.dot_general(token, prompt, BY_ROWS, preferred_element_type=F32)
    out_ref[:columns, :] = total * jnp.exp2(14.0 - exponent)
    out_ref[columns:, :] = jnp.broadcast_to(exponent, (MARK, out_ref.shape[1]))


def weight_shares(states, grads, tokens, after):
    parts = len(states)
    rows, depth = states[0][0].shape
    columns = grads[0].shape[0]
    step = 2 * HEAD_DIM
    return pl.pallas_call(
        functools.partial(weight_kernel, parts, len(tokens)),
        grid=(depth // step,),
        in_specs=[
            pl.BlockSpec((rows, step), lambda j: (0, j))
            if index is None
            else pl.BlockSpec((None, rows, step), lambda j, index=index: (index, 0, j))
            for _, index in states
        ]
        + [pl.BlockSpec(x.shape, lambda j: (0, 0)) for x in (*grads, *tokens)]
        + [pl.BlockSpec(memory_space=pl.ANY)] * len(after),
        out_specs=pl.BlockSpec((columns + MARK, step), lambda j: (0, j)),
        out_shape=jax.ShapeDtypeStruct((columns + MARK, depth), F32),
        scratch_shapes=[pltpu.VMEM((8, HEAD_DIM), F32), pltpu.VMEM((columns, parts * grads[0].shape[1]), BF16)],
        compiler_params=pltpu.CompilerParams(vmem_limit_bytes=VMEM),
        cost_estimate=FREE,
        name="weight_shares",
    )(*[array for array, _ in states], *grads, *tokens, *after)


def rows_kernel(first, place_ref, sums_ref, raw_ref, cos_ref, sin_ref, *refs):
    out_ref = refs[-1]
    sub = sums_ref.shape[1]
    own = pl.ds(pl.multiple_of(place_ref[3] * sub, sub), sub)
    turn = pl.ds(pl.multiple_of(cos_ref.shape[0] - raw_ref.shape[0] + place_ref[3] * sub, sub), sub)
    cosine = cos_ref[turn, :]
    sine = sin_ref[turn, :]
    for head in range(out_ref.shape[1] // (2 * HEAD_DIM)):
        start = 2 * head * HEAD_DIM
        both = jnp.sum(sums_ref[:, :, start : start + 2 * HEAD_DIM], axis=0)
        grad = both[:, :HEAD_DIM]
        raw = raw_ref[own, (first + head) * HEAD_DIM : (first + head + 1) * HEAD_DIM]
        factor = lax.rsqrt(jnp.mean(raw * raw, axis=-1, keepdims=True) + EPS)
        normed = raw * factor
        unturned = grad * cosine - pltpu.roll(grad, HEAD_DIM // 2, 1) * sine
        inner = jnp.mean(unturned * normed, axis=-1, keepdims=True)
        out_ref[:, start : start + HEAD_DIM] = (factor * (unturned - normed * inner)).astype(BF16)
        out_ref[:, start + HEAD_DIM : start + 2 * HEAD_DIM] = both[:, HEAD_DIM:].astype(BF16)


def row_grads(first, place, sums, raw, cosine, sine, after):
    return pl.pallas_call(
        functools.partial(rows_kernel, first),
        in_specs=[pl.BlockSpec(memory_space=pltpu.SMEM)]
        + [pl.BlockSpec(memory_space=pltpu.VMEM)] * 4
        + [pl.BlockSpec(memory_space=pl.ANY)] * len(after),
        out_shape=jax.ShapeDtypeStruct(sums.shape[1:], BF16),
        compiler_params=pltpu.CompilerParams(vmem_limit_bytes=VMEM),
        cost_estimate=FREE,
        name="row_grads",
    )(place, sums, raw, cosine, sine, *after)


def advantage_of(rewards, group_ids):
    onehot = (group_ids[:, None] == jnp.arange(NADV, dtype=jnp.int32)[None, :]).astype(F32)
    sums = jnp.stack(
        [
            jnp.sum(onehot, axis=0),
            jnp.sum(onehot * rewards[:, None], axis=0),
            jnp.sum(onehot * (rewards * rewards)[:, None], axis=0),
        ]
    )
    names = ("chip", "core", "resp")
    peers = lax.axis_size(names)
    sums = jnp.sum(everyone(jnp.broadcast_to(sums[None], (peers,) + sums.shape), names), axis=0)
    members = jnp.maximum(sums[0], 1.0)
    mean = sums[1] / members
    spread = jnp.sqrt(jnp.maximum(sums[2] / members - mean * mean, 0.0))
    own_mean = jnp.sum(onehot * mean[None, :], axis=1)
    own_spread = jnp.sum(onehot * spread[None, :], axis=1)
    return (rewards - own_mean) / jnp.maximum(own_spread, 0.5)


def exponent_of(payload):
    return payload[-MARK : 1 - MARK].astype(F32)


def values_of(payload, exponent):
    return payload[:-MARK].astype(F32) * jnp.exp2(exponent)


def body(prompt_states, response_states, queries, grad_output, key_weight, value_weight, rewards, lengths, group_ids):
    depth, width = key_weight.shape
    shard = prompt_states.shape[1]
    rows = response_states.shape[2]
    n_grp = lax.axis_size("grp")
    n_chip = lax.axis_size("chip")
    n_core = lax.axis_size("core")
    n_resp = lax.axis_size("resp")
    n_prompt = n_chip * n_core
    grp = lax.axis_index("grp")
    chip = lax.axis_index("chip")
    core = lax.axis_index("core")
    resp = lax.axis_index("resp")
    prompt = chip * n_core + core
    prompt_len = shard * n_prompt
    block = depth // (n_prompt * n_resp * n_grp)
    sub = shard // n_resp
    states = response_states[0, 0]
    own_prompt = prompt_states[0]

    groups = [(e, c) for e in range(n_grp) for c in range(n_core)]
    counts = (n_grp, n_chip, n_core, n_resp, block)
    place = jnp.stack([grp, chip, core, resp]).astype(jnp.int32)
    beside, across_grp = select_columns(states, own_prompt, place, groups[1:], counts)
    chosen = across_grp
    beside = exchange(beside, [("core", 1)])
    across_grp = exchange(across_grp, [("grp", 1)])

    advantage = advantage_of(rewards[0], group_ids[0])
    length = lengths[0]
    coef = advantage / length.astype(F32)
    ints = jnp.stack([length[0], prompt.astype(jnp.int32)])

    line = jnp.arange(rows + shard, dtype=jnp.int32)
    cosine, sine = rotary_tables(jnp.where(line < rows, prompt_len + line, prompt * shard + line - rows))
    (prompt_raw, mine, own_raw, own_both), parts = project(
        own_prompt,
        states,
        key_weight,
        value_weight,
        cosine,
        sine,
        place,
        groups[:1],
        counts,
        chosen,
    )
    prompt_both = [mine]
    for d in range(1, n_prompt):
        prompt_both.append(exchange(mine, [("chip", d // n_core), ("core", d % n_core)]))

    def run(first, per, chunk_first, chunk_heads, grads, sums, after):
        grads, sums, own_g = attend(
            first, per, first - chunk_first, chunk_heads, coef, ints, queries[0, 0], grad_output[0, 0],
            prompt_both, own_both, own_raw, cosine, sine, [grads, sums], after,
        )
        return grads, sums, own_g.reshape(-1, rows)

    def across(own_g):
        return [exchange(own_g, [("grp", e)]) for e in range(1, n_grp)]

    def everywhere(own_g, hops):
        held = [own_g] + hops
        return [exchange(held[e], [("core", c)]) if c else held[e] for e, c in groups]

    def row_tokens(sums, chunk_first, after):
        sums = everyone(sums.reshape(n_prompt * n_resp, sub, -1), ("chip", "core", "resp"))
        own = row_grads(chunk_first, place, sums, prompt_raw, cosine, sine, after)
        held = jnp.concatenate([own] + [exchange(own, [("core", c)]) for c in range(1, n_core)])
        return [held] + across(held), own

    wide = n_resp * block

    def chip_terms(shares):
        return [exchange(shares[:, d * wide : (d + 1) * wide].astype(jnp.float16), [("chip", d)]) for d in range(1, n_chip)]

    def resp_terms(kept, sent):
        exponents = [exponent_of(x) for x in [kept] + sent]
        top = functools.reduce(jnp.maximum, exponents) + math.ceil(math.log2(n_chip))
        total = values_of(kept, exponents[0] - top)
        for payload, exponent in zip(sent, exponents[1:]):
            total = total + values_of(payload, exponent - top)
        payload = jnp.concatenate([total, jnp.broadcast_to(top, (MARK, wide))], axis=0).astype(jnp.float16)
        half = lax.dynamic_slice_in_dim(total * jnp.exp2(top - 14.0), resp * block, block, 1)
        pieces = []
        for d in range(1, n_resp):
            part = lax.dynamic_slice_in_dim(payload, (resp ^ d) * block, block, 1)
            pieces.append(exchange(part, [("resp", d)]))
        return half, pieces

    def finish(half, pieces):
        for part in pieces:
            half = half + values_of(part, exponent_of(part) - 14.0)
        return half, exchange(half, [("grp", 1)])

    early, late = CALLS
    grads, sums_early, g_early = run(0, early, 0, early, None, None, [])
    hops_early = across(g_early)
    across_grp = tied(across_grp, g_early)
    grads, sums_late, g_late = run(early, late, early, late, grads, None, [beside, across_grp])
    parts = [(parts[0], None), (beside, None), (across_grp, 0), (exchange(across_grp, [("core", 1)]), 1)]
    hops_early = [tied(x, g_late) for x in hops_early]
    g_late = tied(g_late, *hops_early)
    sums_late = tied(sums_late, *hops_early)
    tokens_early, _ = row_tokens(sums_early, 0, [g_late])
    g_late = tied(g_late, *tokens_early[1:])
    hops_late = across(g_late)
    tokens_late, own_late = row_tokens(sums_late, early, [])
    shares_early = weight_shares(parts, everywhere(g_early, hops_early), tokens_early, [own_late])
    hops_late = [tied(x, shares_early) for x in hops_late]
    shares_late = weight_shares(parts, everywhere(g_late, hops_late), tokens_late, [])
    sent_early = chip_terms(shares_early)
    sent_late = chip_terms(shares_late)
    half_early, pieces_early = resp_terms(shares_early[:, :wide], sent_early)
    done_early = finish(half_early, pieces_early)
    sent_late = [lax.optimization_barrier((x, done_early[0]))[0] for x in sent_late]
    half_late, pieces_late = resp_terms(shares_late[:, :wide], sent_late)
    finished = [done_early, finish(half_late, pieces_late)]

    mine = jnp.concatenate([pair[0] for pair in finished], axis=0)
    theirs = jnp.concatenate([pair[1] for pair in finished], axis=0)
    low = jnp.where(grp == 0, mine, theirs)
    high = jnp.where(grp == 0, theirs, mine)
    both = jnp.concatenate([low, high], axis=1).reshape(width // HEAD_DIM, 2, HEAD_DIM, n_grp * block)
    sides = [both[:, side].reshape(width, n_grp * block).T for side in range(2)]
    return (grads[None, None], sides[0], sides[1])


def solution(mesh):
    devices = mesh.devices
    n_grp, n_prompt, n_resp = devices.shape
    split = jax.sharding.Mesh(
        devices.reshape(n_grp, n_prompt // 2, 2, n_resp), ("grp", "chip", "core", "resp")
    )
    prompt = ("chip", "core")
    owner = ("chip", "core", "resp")
    placed = (
        P("grp", prompt, None),
        P("grp", owner, None, None),
        P("grp", owner, None, None),
        P("grp", owner, None, None),
        P(),
        P(),
        P("grp", owner),
        P("grp", owner),
        P("grp", owner),
    )
    return jax.shard_map(
        body,
        mesh=split,
        in_specs=placed,
        out_specs=(
            P("grp", owner, None, None),
            P(owner, None),
            P(owner, None),
        ),
        check_vma=False,
    )
```

```python
import functools
import math

import jax
import jax.numpy as jnp
from jax import lax
from jax.experimental import pallas as pl
from jax.experimental.pallas import tpu as pltpu
from jax.sharding import PartitionSpec as P

HEAD_DIM = 128
NADV = 8
THETA = 1000000.0
EPS = 1e-06
STATE_BOUND = 6.0
QROWS = 128
CALLS = (2, 2)
VMEM = 58 * 1024 * 1024
MARK = 16
PROJECT_BLOCK = 1024

BF16 = jnp.bfloat16
FREE = pl.CostEstimate(flops=1, bytes_accessed=1, transcendentals=0)
F32 = jnp.float32
BY_ROWS = (((0,), (0,)), ((), ()))
BY_COLS = (((1,), (1,)), ((), ()))


def exchange(value, steps):
    names = tuple(name for name, step in steps if step)
    sizes = [lax.axis_size(name) for name in names]
    mask = 0
    for (name, step), size in zip([s for s in steps if s[1]], sizes):
        mask = mask * size + step
    total = math.prod(sizes)
    return lax.ppermute(value, names, [(j, j ^ mask) for j in range(total)])


def rotary_tables(positions):
    lane = jnp.arange(HEAD_DIM, dtype=jnp.int32)
    half = HEAD_DIM // 2
    steps = (lane % half).astype(F32)
    freq = THETA ** (-2.0 * steps / HEAD_DIM)
    angle = positions.astype(F32)[:, None] * freq[None, :]
    sign = jnp.where(lane < half, -1.0, 1.0).astype(F32)
    return jnp.cos(angle), jnp.sin(angle) * sign[None, :]


def column_copies(groups, counts, place_ref, source_ref, rows, sub_ref, first, targets, sems):
    n_grp, n_chip, n_core, n_resp, block = counts
    sub = targets[0].shape[0] - rows
    own = pl.ds(pl.multiple_of(first + place_ref[3] * sub, sub), sub)
    copies = []
    for i, (e, c) in enumerate(groups):
        copies.append([])
        for d in range(n_chip):
            for r in range(n_resp):
                chip = place_ref[1] ^ d
                core = place_ref[2] ^ c
                index = ((chip * n_core + core) * n_resp + r) * n_grp + (place_ref[0] ^ e)
                source = pl.ds(pl.multiple_of(index * block, block), block)
                j = d * n_resp + r
                target = slice(j * block, (j + 1) * block)
                pairs = (
                    (source_ref.at[:rows, source], targets[i].at[:rows, target]),
                    (sub_ref.at[own, source], targets[i].at[rows:, target]),
                )
                for m, (src, dst) in enumerate(pairs):
                    copies[-1].append(pltpu.make_async_copy(src, dst, sems.at[i, j, m]))
                    copies[-1][-1].start()
    return copies


def select_kernel(groups, counts, place_ref, states_ref, prompt_ref, *refs):
    beside, across, held, sems, out_sems = refs
    outs = [beside, across.at[0], across.at[1]]
    targets = [held.at[i] for i in range(len(groups))]
    copies = column_copies(groups, counts, place_ref, states_ref, states_ref.shape[0], prompt_ref, 0, targets, sems)
    leaving = []
    for i, arriving in enumerate(copies):
        for copy in arriving:
            copy.wait()
        leaving.append(pltpu.make_async_copy(held.at[i], outs[i], out_sems.at[i]))
        leaving[-1].start()
    for copy in leaving:
        copy.wait()


def select_columns(states, prompt, place, groups, counts):
    n_grp, n_chip, n_core, n_resp, block = counts
    sub = prompt.shape[0] // n_resp
    rows = states.shape[0] + sub
    width = n_chip * n_resp * block
    if block % HEAD_DIM:
        own = lax.dynamic_slice_in_dim(prompt, place[3] * sub, sub, 0)
        split = jnp.concatenate([states, own]).reshape(rows, n_chip, n_core, n_resp, n_grp, block)
        out = []
        for e, c in groups:
            part = lax.dynamic_index_in_dim(split, place[0] ^ e, 4, keepdims=False)
            part = lax.dynamic_index_in_dim(part, place[2] ^ c, 2, keepdims=False)
            parts = [lax.dynamic_index_in_dim(part, place[1] ^ d, 1, keepdims=False) for d in range(n_chip)]
            out.append(jnp.stack(parts, axis=1).reshape(rows, width))
        return out if len(out) == 1 else (out[0], jnp.stack(out[1:]))
    return pl.pallas_call(
        functools.partial(select_kernel, groups, counts),
        in_specs=[pl.BlockSpec(memory_space=pltpu.SMEM)] + [pl.BlockSpec(memory_space=pl.ANY)] * 2,
        out_specs=[pl.BlockSpec(memory_space=pl.ANY)] * 2,
        out_shape=[
            jax.ShapeDtypeStruct((rows, width), states.dtype),
            jax.ShapeDtypeStruct((2, rows, width), states.dtype),
        ],
        scratch_shapes=[
            pltpu.VMEM((len(groups), rows, width), states.dtype),
            pltpu.SemaphoreType.DMA((len(groups), n_chip * n_resp, 2)),
            pltpu.SemaphoreType.DMA((len(groups),)),
        ],
        compiler_params=pltpu.CompilerParams(vmem_limit_bytes=VMEM),
        cost_estimate=FREE,
        name="select_columns",
    )(place, states, prompt)


def project_kernel(groups, counts, place_ref, p_hbm, r_hbm, wk_hbm, wv_hbm, cos_ref, sin_ref, after_ref, *refs):
    p_raw, p_both, r_raw, r_both = refs[:4]
    selected = refs[4:-7]
    x_ref, wk_ref, wv_ref, acc_k, acc_v, sems, out_sems = refs[-7:]
    depth, width = wk_ref.shape
    shard = p_raw.shape[0]
    rows = r_raw.shape[0]
    steps = depth // PROJECT_BLOCK
    copies = []
    for k in range(steps):
        part = slice(k * PROJECT_BLOCK, (k + 1) * PROJECT_BLOCK)
        pairs = (
            (wk_hbm.at[part, :], wk_ref.at[part, :]),
            (p_hbm.at[:, part], x_ref.at[rows:, part]),
            (r_hbm.at[:, part], x_ref.at[:rows, part]),
            (wv_hbm.at[part, :], wv_ref.at[part, :]),
        )
        copies.append([pltpu.make_async_copy(src, dst, sems.at[k, i]) for i, (src, dst) in enumerate(pairs)])
        for copy in copies[-1]:
            copy.start()
    leaving = []
    for k in range(steps):
        part = slice(k * PROJECT_BLOCK, (k + 1) * PROJECT_BLOCK)
        for copy in copies[k]:
            copy.wait()
        if k == steps - 1 and selected:
            leaving = column_copies(groups, counts, place_ref, x_ref, rows, x_ref, rows, selected, out_sems)
        for acc, w_ref in ((acc_k, wk_ref), (acc_v, wv_ref)):
            share = jnp.dot(x_ref[:, part], w_ref[part, :], preferred_element_type=F32)
            if k:
                acc[...] += share
            else:
                acc[...] = share
    for place, raw_ref, both_ref in (
        (slice(rows, rows + shard), p_raw, p_both),
        (slice(0, rows), r_raw, r_both),
    ):
        both_ref[:, width:] = acc_v[place, :].astype(BF16)
        raw_ref[...] = acc_k[place, :]
        cosine = cos_ref[place, :]
        sine = sin_ref[place, :]
        for head in range(width // HEAD_DIM):
            cols = slice(head * HEAD_DIM, (head + 1) * HEAD_DIM)
            x = acc_k[place, cols]
            factor = lax.rsqrt(jnp.mean(x * x, axis=-1, keepdims=True) + EPS)
            normed = x * factor
            turned = normed * cosine + pltpu.roll(normed, HEAD_DIM // 2, 1) * sine
            both_ref[:, cols] = turned.astype(BF16)
    for copy in sum(leaving, []):
        copy.wait()


def project(prompt, response, key_weight, value_weight, cosine, sine, place, groups, counts, after):
    depth, width = key_weight.shape
    shard, rows = prompt.shape[0], response.shape[0]
    n_grp, n_chip, n_core, n_resp, block = counts
    direct = block % HEAD_DIM == 0
    blocks = n_chip * n_resp
    part = jax.ShapeDtypeStruct((rows + shard // n_resp, blocks * block), BF16)
    any_spec = pl.BlockSpec(memory_space=pl.ANY)
    vmem = pl.BlockSpec(memory_space=pltpu.VMEM)
    out = pl.pallas_call(
        functools.partial(project_kernel, groups, counts),
        in_specs=[pl.BlockSpec(memory_space=pltpu.SMEM)] + [any_spec] * 4 + [vmem] * 2 + [any_spec],
        out_specs=[vmem] * 4 + ([any_spec] * len(groups) if direct else []),
        out_shape=[
            jax.ShapeDtypeStruct((count, scale * width), kind)
            for count in (shard, rows)
            for scale, kind in ((1, F32), (2, BF16))
        ]
        + ([part] * len(groups) if direct else []),
        scratch_shapes=[pltpu.VMEM((shard + rows, depth), BF16)]
        + [pltpu.VMEM((depth, width), BF16)] * 2
        + [pltpu.VMEM((shard + rows, width), F32)] * 2
        + [
            pltpu.SemaphoreType.DMA((depth // PROJECT_BLOCK, 4)),
            pltpu.SemaphoreType.DMA((len(groups), blocks, 2)),
        ],
        compiler_params=pltpu.CompilerParams(vmem_limit_bytes=VMEM),
        cost_estimate=FREE,
        name="project",
    )(place, prompt, response, key_weight, value_weight, cosine, sine, after)
    if direct:
        return out[:4], out[4:]
    return out, select_columns(response, prompt, place, groups, counts)


def tied(value, *others):
    return pl.pallas_call(
        lambda *refs: None,
        in_specs=[pl.BlockSpec(memory_space=pl.ANY)] * (1 + len(others)),
        out_specs=pl.BlockSpec(memory_space=pl.ANY),
        out_shape=jax.ShapeDtypeStruct(value.shape, value.dtype),
        input_output_aliases={0: 0},
        cost_estimate=FREE,
        name="tied",
    )(value, *others)


def attend_kernel(parts, fold, coef_ref, ints_ref, q_ref, go_ref, *refs):
    prompt_k = refs[:parts]
    prompt_v = refs[parts : 2 * parts]
    own_k, own_v, raw_ref, cos_ref, sin_ref = refs[2 * parts : 2 * parts + 5]
    gq_ref, sum_ref, g_ref, k_all, v_all, k_turned, acc_k, acc_v = refs[-8:]
    rows = q_ref.shape[0]
    shard = prompt_k[0].shape[0]
    prompt_len = parts * shard
    scale = HEAD_DIM ** (-0.5)
    length = ints_ref[0]
    coef = coef_ref[0]
    prompt = ints_ref[1]
    for d in range(parts):
        place = pl.ds(pl.multiple_of((prompt ^ d) * shard, shard), shard)
        k_all[place, :] = prompt_k[d][...]
        v_all[place, :] = prompt_v[d][...]
    k_all[prompt_len:, :] = own_k[...]
    v_all[prompt_len:, :] = own_v[...]
    k_turned[...] = k_all[...].T
    acc_k[...] = jnp.zeros_like(acc_k)
    acc_v[...] = jnp.zeros_like(acc_v)
    def one_block(first):
        seen = prompt_len + first + QROWS
        width = fold * QROWS
        position = first + lax.broadcasted_iota(jnp.int32, (QROWS, HEAD_DIM), 0)
        factor = jnp.where(position < length, coef, 0.0)
        parts_q = []
        parts_d = []
        for f in range(fold):
            cols = slice(f * HEAD_DIM, (f + 1) * HEAD_DIM)
            parts_q.append(q_ref[first : first + QROWS, cols])
            parts_d.append((go_ref[first : first + QROWS, cols].astype(F32) * factor).astype(BF16))
        query = jnp.concatenate(parts_q, axis=0)
        dout = jnp.concatenate(parts_d, axis=0)
        scores = lax.dot_general(k_all[:seen, :], query, BY_COLS, preferred_element_type=F32)
        key = lax.broadcasted_iota(jnp.int32, (QROWS, width), 0)
        row = lax.broadcasted_iota(jnp.int32, (QROWS, width), 1) % QROWS
        tail = jnp.where(key <= row, scores[seen - QROWS :, :], -jnp.inf)
        scores = jnp.concatenate([scores[: seen - QROWS, :], tail], axis=0)
        peak = jnp.max(scores, axis=0, keepdims=True)
        expo = jnp.exp2((scores - peak) * (scale * math.log2(math.e)))
        probs = expo * (1.0 / jnp.sum(expo, axis=0, keepdims=True))
        probs_b = probs.astype(BF16)
        dprobs = lax.dot_general(v_all[:seen, :], dout, BY_COLS, preferred_element_type=F32)
        delta = jnp.sum(probs_b.astype(F32) * dprobs, axis=0, keepdims=True)
        dscores = (probs * (dprobs - delta)).astype(BF16)
        grad_q = jnp.dot(k_turned[:, :seen], dscores, preferred_element_type=F32) * scale
        for f in range(fold):
            gq_ref[first : first + QROWS, f * HEAD_DIM : (f + 1) * HEAD_DIM] = (
                grad_q[:, f * QROWS : (f + 1) * QROWS].T.astype(BF16)
            )
        acc_k[:seen, :] += jnp.dot(dscores, query, preferred_element_type=F32)
        acc_v[:seen, :] += jnp.dot(probs_b, dout, preferred_element_type=F32)

    for start in range(0, rows, 2 * QROWS):

        @pl.when(start < length)
        def _(start=start):
            one_block(start)
            one_block(start + QROWS)

        @pl.when(start >= length)
        def _(start=start):
            gq_ref[start : start + 2 * QROWS, :] = jnp.zeros((2 * QROWS, gq_ref.shape[1]), BF16)

    sum_ref[:, :HEAD_DIM] = acc_k[:prompt_len, :] * scale
    sum_ref[:, HEAD_DIM:] = acc_v[:prompt_len, :]
    x = raw_ref[...]
    factor = lax.rsqrt(jnp.mean(x * x, axis=-1, keepdims=True) + EPS)
    normed = x * factor
    grad = acc_k[prompt_len:, :] * scale
    unturned = grad * cos_ref[...] - pltpu.roll(grad, HEAD_DIM // 2, 1) * sin_ref[...]
    inner = jnp.mean(unturned * normed, axis=-1, keepdims=True)
    g_ref[0, 0] = (factor * (unturned - normed * inner)).T.astype(BF16)
    g_ref[0, 1] = acc_v[prompt_len:, :].T.astype(BF16)


def attend(first, per, offset, chunk_heads, coef, ints, query, grad_output, prompt_both, own_both, raw, cosine, sine, before, after):
    rows, query_width = query.shape
    width = raw.shape[1]
    heads = width // HEAD_DIM
    fold = query_width // width
    parts = len(prompt_both)
    shard = prompt_both[0].shape[0]
    prompt_len = parts * shard
    total = prompt_len + rows
    here = lambda h: (0, first + h)
    there = lambda h: (0, heads + first + h)
    scalar = pl.BlockSpec(memory_space=pltpu.SMEM)
    table = pl.BlockSpec((rows, HEAD_DIM), lambda h: (0, 0))
    wide = pl.BlockSpec((rows, fold * HEAD_DIM), here)
    in_specs = [scalar, scalar, wide, wide]
    in_specs += [pl.BlockSpec((shard, HEAD_DIM), here)] * parts + [pl.BlockSpec((shard, HEAD_DIM), there)] * parts
    in_specs += [pl.BlockSpec((rows, HEAD_DIM), here), pl.BlockSpec((rows, HEAD_DIM), there)]
    in_specs += [pl.BlockSpec((rows, HEAD_DIM), here), table, table]
    operands = [coef, ints, query, grad_output, *prompt_both, *prompt_both, own_both, own_both, raw, cosine, sine]
    aliases = {}
    for i, value in enumerate(before):
        if value is not None:
            aliases[len(operands)] = i
            in_specs.append(pl.BlockSpec(memory_space=pl.ANY))
            operands.append(value)
    in_specs += [pl.BlockSpec(memory_space=pl.ANY)] * len(after)
    operands += after
    return pl.pallas_call(
        functools.partial(attend_kernel, parts, fold),
        grid=(per,),
        in_specs=in_specs,
        out_specs=[
            wide,
            pl.BlockSpec((prompt_len, 2 * HEAD_DIM), lambda h: (0, offset + h)),
            pl.BlockSpec((1, 2, HEAD_DIM, rows), lambda h: (h, 0, 0, 0)),
        ],
        out_shape=[
            jax.ShapeDtypeStruct((rows, query_width), BF16),
            jax.ShapeDtypeStruct((prompt_len, 2 * chunk_heads * HEAD_DIM), F32),
            jax.ShapeDtypeStruct((per, 2, HEAD_DIM, rows), BF16),
        ],
        scratch_shapes=[
            pltpu.VMEM((total, HEAD_DIM), BF16),
            pltpu.VMEM((total, HEAD_DIM), BF16),
            pltpu.VMEM((HEAD_DIM, total), BF16),
            pltpu.VMEM((total, HEAD_DIM), F32),
            pltpu.VMEM((total, HEAD_DIM), F32),
        ],
        input_output_aliases=aliases,
        compiler_params=pltpu.CompilerParams(vmem_limit_bytes=VMEM),
        cost_estimate=FREE,
        name="attend",
    )(*operands)


def everyone(value, names):
    return lax.all_to_all(value, names, split_axis=0, concat_axis=0, tiled=True)


def weight_kernel(parts, tokens_count, *refs):
    states = refs[:parts]
    grads = refs[parts : 2 * parts]
    tokens = refs[2 * parts : 2 * parts + tokens_count]
    out_ref, scale_ref, side_ref = refs[-3:]
    columns, rows = grads[0].shape
    total_rows = parts * states[0].shape[-2]

    @pl.when(pl.program_id(0) == 0)
    def _():
        highest = jnp.zeros((1, rows), F32)
        for d, grad in enumerate(grads):
            value = grad[...]
            side_ref[:, d * rows : (d + 1) * rows] = value
            highest = jnp.maximum(highest, jnp.max(jnp.abs(value), axis=0, keepdims=True).astype(F32))
        peak = jnp.max(highest, axis=1, keepdims=True)
        for token in tokens:
            highest = jnp.max(jnp.abs(token[...].astype(F32)), axis=0, keepdims=True)
            peak = jnp.maximum(peak, jnp.max(highest, axis=1, keepdims=True))
        reach = jnp.maximum(peak * (STATE_BOUND * total_rows), 1e-30)
        exponent = jnp.clip(jnp.ceil(jnp.log2(reach)), -90.0, 120.0)
        scale_ref[...] = jnp.broadcast_to(exponent, scale_ref.shape)

    exponent = scale_ref[:1, :1]
    response = jnp.concatenate([part[:rows, :] for part in states], axis=0)
    prompt = jnp.concatenate([part[rows:, :] for part in states], axis=0)
    token = jnp.concatenate([token[...] for token in tokens], axis=0)
    total = jnp.dot(side_ref[...], response, preferred_element_type=F32)
    total = total + lax.dot_general(token, prompt, BY_ROWS, preferred_element_type=F32)
    out_ref[:columns, :] = total * jnp.exp2(14.0 - exponent)
    out_ref[columns:, :] = jnp.broadcast_to(exponent, (MARK, out_ref.shape[1]))


def weight_shares(states, grads, tokens):
    parts = len(states)
    rows, depth = states[0][0].shape
    columns = grads[0].shape[0]
    step = 2 * HEAD_DIM
    return pl.pallas_call(
        functools.partial(weight_kernel, parts, len(tokens)),
        grid=(depth // step,),
        in_specs=[
            pl.BlockSpec((rows, step), lambda j: (0, j))
            if index is None
            else pl.BlockSpec((None, rows, step), lambda j, index=index: (index, 0, j))
            for _, index in states
        ]
        + [pl.BlockSpec(x.shape, lambda j: (0, 0)) for x in (*grads, *tokens)],
        out_specs=pl.BlockSpec((columns + MARK, step), lambda j: (0, j)),
        out_shape=jax.ShapeDtypeStruct((columns + MARK, depth), F32),
        scratch_shapes=[pltpu.VMEM((8, HEAD_DIM), F32), pltpu.VMEM((columns, parts * grads[0].shape[1]), BF16)],
        compiler_params=pltpu.CompilerParams(vmem_limit_bytes=VMEM),
        cost_estimate=FREE,
        name="weight_shares",
    )(*[array for array, _ in states], *grads, *tokens)


def rows_kernel(first, place_ref, sums_ref, raw_ref, cos_ref, sin_ref, *refs):
    out_ref = refs[-1]
    sub = sums_ref.shape[1]
    own = pl.ds(pl.multiple_of(place_ref[3] * sub, sub), sub)
    turn = pl.ds(pl.multiple_of(cos_ref.shape[0] - raw_ref.shape[0] + place_ref[3] * sub, sub), sub)
    cosine = cos_ref[turn, :]
    sine = sin_ref[turn, :]
    for head in range(out_ref.shape[1] // (2 * HEAD_DIM)):
        start = 2 * head * HEAD_DIM
        both = jnp.sum(sums_ref[:, :, start : start + 2 * HEAD_DIM], axis=0)
        grad = both[:, :HEAD_DIM]
        raw = raw_ref[own, (first + head) * HEAD_DIM : (first + head + 1) * HEAD_DIM]
        factor = lax.rsqrt(jnp.mean(raw * raw, axis=-1, keepdims=True) + EPS)
        normed = raw * factor
        unturned = grad * cosine - pltpu.roll(grad, HEAD_DIM // 2, 1) * sine
        inner = jnp.mean(unturned * normed, axis=-1, keepdims=True)
        out_ref[:, start : start + HEAD_DIM] = (factor * (unturned - normed * inner)).astype(BF16)
        out_ref[:, start + HEAD_DIM : start + 2 * HEAD_DIM] = both[:, HEAD_DIM:].astype(BF16)


def row_grads(first, place, sums, raw, cosine, sine, after):
    return pl.pallas_call(
        functools.partial(rows_kernel, first),
        in_specs=[pl.BlockSpec(memory_space=pltpu.SMEM)]
        + [pl.BlockSpec(memory_space=pltpu.VMEM)] * 4
        + [pl.BlockSpec(memory_space=pl.ANY)] * len(after),
        out_shape=jax.ShapeDtypeStruct(sums.shape[1:], BF16),
        compiler_params=pltpu.CompilerParams(vmem_limit_bytes=VMEM),
        cost_estimate=FREE,
        name="row_grads",
    )(place, sums, raw, cosine, sine, *after)


def advantage_of(rewards, group_ids):
    onehot = (group_ids[:, None] == jnp.arange(NADV, dtype=jnp.int32)[None, :]).astype(F32)
    sums = jnp.stack(
        [
            jnp.sum(onehot, axis=0),
            jnp.sum(onehot * rewards[:, None], axis=0),
            jnp.sum(onehot * (rewards * rewards)[:, None], axis=0),
        ]
    )
    names = ("chip", "core", "resp")
    peers = lax.axis_size(names)
    sums = jnp.sum(everyone(jnp.broadcast_to(sums[None], (peers,) + sums.shape), names), axis=0)
    members = jnp.maximum(sums[0], 1.0)
    mean = sums[1] / members
    spread = jnp.sqrt(jnp.maximum(sums[2] / members - mean * mean, 0.0))
    own_mean = jnp.sum(onehot * mean[None, :], axis=1)
    own_spread = jnp.sum(onehot * spread[None, :], axis=1)
    return (rewards - own_mean) / jnp.maximum(own_spread, 0.5)


def exponent_of(payload):
    return payload[-MARK : 1 - MARK].astype(F32)


def values_of(payload, exponent):
    return payload[:-MARK].astype(F32) * jnp.exp2(exponent)


def body(prompt_states, response_states, queries, grad_output, key_weight, value_weight, rewards, lengths, group_ids):
    depth, width = key_weight.shape
    shard = prompt_states.shape[1]
    rows = response_states.shape[2]
    n_grp = lax.axis_size("grp")
    n_chip = lax.axis_size("chip")
    n_core = lax.axis_size("core")
    n_resp = lax.axis_size("resp")
    n_prompt = n_chip * n_core
    grp = lax.axis_index("grp")
    chip = lax.axis_index("chip")
    core = lax.axis_index("core")
    resp = lax.axis_index("resp")
    prompt = chip * n_core + core
    prompt_len = shard * n_prompt
    block = depth // (n_prompt * n_resp * n_grp)
    sub = shard // n_resp
    states = response_states[0, 0]
    own_prompt = prompt_states[0]

    groups = [(e, c) for e in range(n_grp) for c in range(n_core)]
    counts = (n_grp, n_chip, n_core, n_resp, block)
    place = jnp.stack([grp, chip, core, resp]).astype(jnp.int32)
    beside, across_grp = select_columns(states, own_prompt, place, groups[1:], counts)
    chosen = across_grp
    beside = exchange(beside, [("core", 1)])
    across_grp = exchange(across_grp, [("grp", 1)])

    advantage = advantage_of(rewards[0], group_ids[0])
    length = lengths[0]
    coef = advantage / length.astype(F32)
    ints = jnp.stack([length[0], prompt.astype(jnp.int32)])

    line = jnp.arange(rows + shard, dtype=jnp.int32)
    cosine, sine = rotary_tables(jnp.where(line < rows, prompt_len + line, prompt * shard + line - rows))
    (prompt_raw, mine, own_raw, own_both), parts = project(
        own_prompt,
        states,
        key_weight,
        value_weight,
        cosine,
        sine,
        place,
        groups[:1],
        counts,
        chosen,
    )
    prompt_both = [mine]
    for d in range(1, n_prompt):
        prompt_both.append(exchange(mine, [("chip", d // n_core), ("core", d % n_core)]))

    def run(first, per, chunk_first, chunk_heads, grads, sums, after):
        grads, sums, own_g = attend(
            first, per, first - chunk_first, chunk_heads, coef, ints, queries[0, 0], grad_output[0, 0],
            prompt_both, own_both, own_raw, cosine, sine, [grads, sums], after,
        )
        return grads, sums, own_g.reshape(-1, rows)

    def across(own_g):
        return [exchange(own_g, [("grp", e)]) for e in range(1, n_grp)]

    def everywhere(own_g, hops):
        held = [own_g] + hops
        return [exchange(held[e], [("core", c)]) if c else held[e] for e, c in groups]

    def row_tokens(sums, chunk_first, after):
        sums = everyone(sums.reshape(n_prompt * n_resp, sub, -1), ("chip", "core", "resp"))
        own = row_grads(chunk_first, place, sums, prompt_raw, cosine, sine, after)
        return [exchange(own, [("grp", e), ("core", c)]) if e or c else own for e, c in groups]

    wide = n_resp * block

    def chip_terms(shares):
        return [exchange(shares[:, d * wide : (d + 1) * wide].astype(jnp.float16), [("chip", d)]) for d in range(1, n_chip)]

    def resp_terms(kept, sent):
        exponents = [exponent_of(x) for x in [kept] + sent]
        top = functools.reduce(jnp.maximum, exponents) + math.ceil(math.log2(n_chip))
        total = values_of(kept, exponents[0] - top)
        for payload, exponent in zip(sent, exponents[1:]):
            total = total + values_of(payload, exponent - top)
        payload = jnp.concatenate([total, jnp.broadcast_to(top, (MARK, wide))], axis=0).astype(jnp.float16)
        half = lax.dynamic_slice_in_dim(total * jnp.exp2(top - 14.0), resp * block, block, 1)
        pieces = []
        for d in range(1, n_resp):
            part = lax.dynamic_slice_in_dim(payload, (resp ^ d) * block, block, 1)
            pieces.append(exchange(part, [("resp", d)]))
        return half, pieces

    def finish(half, pieces):
        for part in pieces:
            half = half + values_of(part, exponent_of(part) - 14.0)
        return half, exchange(half, [("grp", 1)])

    early, late = CALLS
    grads, sums_early, g_early = run(0, early, 0, early, None, None, [])
    hops_early = across(g_early)
    across_grp = tied(across_grp, g_early)
    grads, sums_late, g_late = run(early, late, early, late, grads, None, [beside, across_grp])
    parts = [(parts[0], None), (beside, None), (across_grp, 0), (exchange(across_grp, [("core", 1)]), 1)]
    hops_early = [tied(x, g_late) for x in hops_early]
    g_late = tied(g_late, *hops_early)
    sums_late = tied(sums_late, *hops_early)
    tokens_early = row_tokens(sums_early, 0, [g_late])
    g_late = tied(g_late, *[token for token, (e, c) in zip(tokens_early, groups) if e])
    hops_late = across(g_late)
    shares_early = weight_shares(parts, everywhere(g_early, hops_early), tokens_early)
    hops_late = [tied(x, shares_early) for x in hops_late]
    tokens_late = row_tokens(sums_late, early, [shares_early])
    shares_late = weight_shares(parts, everywhere(g_late, hops_late), tokens_late)
    sent_early = chip_terms(shares_early)
    sent_late = chip_terms(shares_late)
    half_early, pieces_early = resp_terms(shares_early[:, :wide], sent_early)
    done_early = finish(half_early, pieces_early)
    sent_late = [lax.optimization_barrier((x, done_early[0]))[0] for x in sent_late]
    half_late, pieces_late = resp_terms(shares_late[:, :wide], sent_late)
    finished = [done_early, finish(half_late, pieces_late)]

    mine = jnp.concatenate([pair[0] for pair in finished], axis=0)
    theirs = jnp.concatenate([pair[1] for pair in finished], axis=0)
    low = jnp.where(grp == 0, mine, theirs)
    high = jnp.where(grp == 0, theirs, mine)
    both = jnp.concatenate([low, high], axis=1).reshape(width // HEAD_DIM, 2, HEAD_DIM, n_grp * block)
    sides = [both[:, side].reshape(width, n_grp * block).T for side in range(2)]
    return (grads[None, None], sides[0], sides[1])


def solution(mesh):
    devices = mesh.devices
    n_grp, n_prompt, n_resp = devices.shape
    split = jax.sharding.Mesh(
        devices.reshape(n_grp, n_prompt // 2, 2, n_resp), ("grp", "chip", "core", "resp")
    )
    prompt = ("chip", "core")
    owner = ("chip", "core", "resp")
    placed = (
        P("grp", prompt, None),
        P("grp", owner, None, None),
        P("grp", owner, None, None),
        P("grp", owner, None, None),
        P(),
        P(),
        P("grp", owner),
        P("grp", owner),
        P("grp", owner),
    )
    return jax.shard_map(
        body,
        mesh=split,
        in_specs=placed,
        out_specs=(
            P("grp", owner, None, None),
            P(owner, None),
            P(owner, None),
        ),
        check_vma=False,
    )
```

```python
import functools
import math

import jax
import jax.numpy as jnp
from jax import lax
from jax.experimental import pallas as pl
from jax.experimental.pallas import tpu as pltpu
from jax.sharding import PartitionSpec as P

HEAD_DIM = 128
NADV = 8
THETA = 1000000.0
EPS = 1e-06
STATE_BOUND = 6.0
QROWS = 128
CALLS = (2, 2)
VMEM = 58 * 1024 * 1024
MARK = 16
PROJECT_BLOCK = 1024

BF16 = jnp.bfloat16
FREE = pl.CostEstimate(flops=1, bytes_accessed=1, transcendentals=0)
F32 = jnp.float32
BY_ROWS = (((0,), (0,)), ((), ()))
BY_COLS = (((1,), (1,)), ((), ()))


def exchange(value, steps):
    names = tuple(name for name, step in steps if step)
    sizes = [lax.axis_size(name) for name in names]
    mask = 0
    for (name, step), size in zip([s for s in steps if s[1]], sizes):
        mask = mask * size + step
    total = math.prod(sizes)
    return lax.ppermute(value, names, [(j, j ^ mask) for j in range(total)])


def rotary_tables(positions):
    lane = jnp.arange(HEAD_DIM, dtype=jnp.int32)
    half = HEAD_DIM // 2
    steps = (lane % half).astype(F32)
    freq = THETA ** (-2.0 * steps / HEAD_DIM)
    angle = positions.astype(F32)[:, None] * freq[None, :]
    sign = jnp.where(lane < half, -1.0, 1.0).astype(F32)
    return jnp.cos(angle), jnp.sin(angle) * sign[None, :]


def column_copies(groups, counts, place_ref, source_ref, rows, sub_ref, first, targets, sems):
    n_grp, n_chip, n_core, n_resp, block = counts
    sub = targets[0].shape[0] - rows
    own = pl.ds(pl.multiple_of(first + place_ref[3] * sub, sub), sub)
    copies = []
    for i, (e, c) in enumerate(groups):
        copies.append([])
        for d in range(n_chip):
            for r in range(n_resp):
                chip = place_ref[1] ^ d
                core = place_ref[2] ^ c
                index = ((chip * n_core + core) * n_resp + r) * n_grp + (place_ref[0] ^ e)
                source = pl.ds(pl.multiple_of(index * block, block), block)
                j = d * n_resp + r
                target = slice(j * block, (j + 1) * block)
                pairs = (
                    (source_ref.at[:rows, source], targets[i].at[:rows, target]),
                    (sub_ref.at[own, source], targets[i].at[rows:, target]),
                )
                for m, (src, dst) in enumerate(pairs):
                    copies[-1].append(pltpu.make_async_copy(src, dst, sems.at[i, j, m]))
                    copies[-1][-1].start()
    return copies


def select_kernel(groups, counts, place_ref, states_ref, prompt_ref, *refs):
    beside, across, held, sems, out_sems = refs
    outs = [beside, across.at[0], across.at[1]]
    targets = [held.at[i] for i in range(len(groups))]
    copies = column_copies(groups, counts, place_ref, states_ref, states_ref.shape[0], prompt_ref, 0, targets, sems)
    leaving = []
    for i, arriving in enumerate(copies):
        for copy in arriving:
            copy.wait()
        leaving.append(pltpu.make_async_copy(held.at[i], outs[i], out_sems.at[i]))
        leaving[-1].start()
    for copy in leaving:
        copy.wait()


def select_columns(states, prompt, place, groups, counts):
    n_grp, n_chip, n_core, n_resp, block = counts
    sub = prompt.shape[0] // n_resp
    rows = states.shape[0] + sub
    width = n_chip * n_resp * block
    if block % HEAD_DIM:
        own = lax.dynamic_slice_in_dim(prompt, place[3] * sub, sub, 0)
        split = jnp.concatenate([states, own]).reshape(rows, n_chip, n_core, n_resp, n_grp, block)
        out = []
        for e, c in groups:
            part = lax.dynamic_index_in_dim(split, place[0] ^ e, 4, keepdims=False)
            part = lax.dynamic_index_in_dim(part, place[2] ^ c, 2, keepdims=False)
            parts = [lax.dynamic_index_in_dim(part, place[1] ^ d, 1, keepdims=False) for d in range(n_chip)]
            out.append(jnp.stack(parts, axis=1).reshape(rows, width))
        return out if len(out) == 1 else (out[0], jnp.stack(out[1:]))
    return pl.pallas_call(
        functools.partial(select_kernel, groups, counts),
        in_specs=[pl.BlockSpec(memory_space=pltpu.SMEM)] + [pl.BlockSpec(memory_space=pl.ANY)] * 2,
        out_specs=[pl.BlockSpec(memory_space=pl.ANY)] * 2,
        out_shape=[
            jax.ShapeDtypeStruct((rows, width), states.dtype),
            jax.ShapeDtypeStruct((2, rows, width), states.dtype),
        ],
        scratch_shapes=[
            pltpu.VMEM((len(groups), rows, width), states.dtype),
            pltpu.SemaphoreType.DMA((len(groups), n_chip * n_resp, 2)),
            pltpu.SemaphoreType.DMA((len(groups),)),
        ],
        compiler_params=pltpu.CompilerParams(vmem_limit_bytes=VMEM),
        cost_estimate=FREE,
        name="select_columns",
    )(place, states, prompt)


def project_kernel(groups, counts, place_ref, p_hbm, r_hbm, wk_hbm, wv_hbm, cos_ref, sin_ref, after_ref, *refs):
    p_raw, p_both, r_raw, r_both = refs[:4]
    selected = refs[4:-7]
    x_ref, wk_ref, wv_ref, acc_k, acc_v, sems, out_sems = refs[-7:]
    depth, width = wk_ref.shape
    shard = p_raw.shape[0]
    rows = r_raw.shape[0]
    steps = depth // PROJECT_BLOCK
    copies = []
    for k in range(steps):
        part = slice(k * PROJECT_BLOCK, (k + 1) * PROJECT_BLOCK)
        pairs = (
            (wk_hbm.at[part, :], wk_ref.at[part, :]),
            (p_hbm.at[:, part], x_ref.at[rows:, part]),
            (r_hbm.at[:, part], x_ref.at[:rows, part]),
            (wv_hbm.at[part, :], wv_ref.at[part, :]),
        )
        copies.append([pltpu.make_async_copy(src, dst, sems.at[k, i]) for i, (src, dst) in enumerate(pairs)])
        for copy in copies[-1]:
            copy.start()
    leaving = []
    for k in range(steps):
        part = slice(k * PROJECT_BLOCK, (k + 1) * PROJECT_BLOCK)
        for copy in copies[k]:
            copy.wait()
        if k == steps - 1 and selected:
            leaving = column_copies(groups, counts, place_ref, x_ref, rows, x_ref, rows, selected, out_sems)
        for acc, w_ref in ((acc_k, wk_ref), (acc_v, wv_ref)):
            share = jnp.dot(x_ref[:, part], w_ref[part, :], preferred_element_type=F32)
            if k:
                acc[...] += share
            else:
                acc[...] = share
    for place, raw_ref, both_ref in (
        (slice(rows, rows + shard), p_raw, p_both),
        (slice(0, rows), r_raw, r_both),
    ):
        both_ref[:, width:] = acc_v[place, :].astype(BF16)
        raw_ref[...] = acc_k[place, :]
        cosine = cos_ref[place, :]
        sine = sin_ref[place, :]
        for head in range(width // HEAD_DIM):
            cols = slice(head * HEAD_DIM, (head + 1) * HEAD_DIM)
            x = acc_k[place, cols]
            factor = lax.rsqrt(jnp.mean(x * x, axis=-1, keepdims=True) + EPS)
            normed = x * factor
            turned = normed * cosine + pltpu.roll(normed, HEAD_DIM // 2, 1) * sine
            both_ref[:, cols] = turned.astype(BF16)
    for copy in sum(leaving, []):
        copy.wait()


def project(prompt, response, key_weight, value_weight, cosine, sine, place, groups, counts, after):
    depth, width = key_weight.shape
    shard, rows = prompt.shape[0], response.shape[0]
    n_grp, n_chip, n_core, n_resp, block = counts
    direct = block % HEAD_DIM == 0
    blocks = n_chip * n_resp
    part = jax.ShapeDtypeStruct((rows + shard // n_resp, blocks * block), BF16)
    any_spec = pl.BlockSpec(memory_space=pl.ANY)
    vmem = pl.BlockSpec(memory_space=pltpu.VMEM)
    out = pl.pallas_call(
        functools.partial(project_kernel, groups, counts),
        in_specs=[pl.BlockSpec(memory_space=pltpu.SMEM)] + [any_spec] * 4 + [vmem] * 2 + [any_spec],
        out_specs=[vmem] * 4 + ([any_spec] * len(groups) if direct else []),
        out_shape=[
            jax.ShapeDtypeStruct((count, scale * width), kind)
            for count in (shard, rows)
            for scale, kind in ((1, F32), (2, BF16))
        ]
        + ([part] * len(groups) if direct else []),
        scratch_shapes=[pltpu.VMEM((shard + rows, depth), BF16)]
        + [pltpu.VMEM((depth, width), BF16)] * 2
        + [pltpu.VMEM((shard + rows, width), F32)] * 2
        + [
            pltpu.SemaphoreType.DMA((depth // PROJECT_BLOCK, 4)),
            pltpu.SemaphoreType.DMA((len(groups), blocks, 2)),
        ],
        compiler_params=pltpu.CompilerParams(vmem_limit_bytes=VMEM),
        cost_estimate=FREE,
        name="project",
    )(place, prompt, response, key_weight, value_weight, cosine, sine, after)
    if direct:
        return out[:4], out[4:]
    return out, select_columns(response, prompt, place, groups, counts)


def tied(value, *others):
    return pl.pallas_call(
        lambda *refs: None,
        in_specs=[pl.BlockSpec(memory_space=pl.ANY)] * (1 + len(others)),
        out_specs=pl.BlockSpec(memory_space=pl.ANY),
        out_shape=jax.ShapeDtypeStruct(value.shape, value.dtype),
        input_output_aliases={0: 0},
        cost_estimate=FREE,
        name="tied",
    )(value, *others)


def attend_kernel(parts, fold, coef_ref, ints_ref, q_ref, go_ref, *refs):
    prompt_k = refs[:parts]
    prompt_v = refs[parts : 2 * parts]
    own_k, own_v, raw_ref, cos_ref, sin_ref = refs[2 * parts : 2 * parts + 5]
    gq_ref, sum_ref, g_ref, k_all, v_all, k_turned, acc_k, acc_v = refs[-8:]
    rows = q_ref.shape[0]
    shard = prompt_k[0].shape[0]
    prompt_len = parts * shard
    scale = HEAD_DIM ** (-0.5)
    length = ints_ref[0]
    coef = coef_ref[0]
    prompt = ints_ref[1]
    for d in range(parts):
        place = pl.ds(pl.multiple_of((prompt ^ d) * shard, shard), shard)
        k_all[place, :] = prompt_k[d][...]
        v_all[place, :] = prompt_v[d][...]
    k_all[prompt_len:, :] = own_k[...]
    v_all[prompt_len:, :] = own_v[...]
    k_turned[...] = k_all[...].T
    acc_k[...] = jnp.zeros_like(acc_k)
    acc_v[...] = jnp.zeros_like(acc_v)
    width = fold * QROWS
    key = lax.broadcasted_iota(jnp.int32, (QROWS, width), 0)
    row = lax.broadcasted_iota(jnp.int32, (QROWS, width), 1) % QROWS

    def begin(first):
        seen = prompt_len + first + QROWS
        position = first + lax.broadcasted_iota(jnp.int32, (QROWS, HEAD_DIM), 0)
        factor = jnp.where(position < length, coef, 0.0)
        parts_q = []
        parts_d = []
        for f in range(fold):
            cols = slice(f * HEAD_DIM, (f + 1) * HEAD_DIM)
            parts_q.append(q_ref[first : first + QROWS, cols])
            parts_d.append((go_ref[first : first + QROWS, cols].astype(F32) * factor).astype(BF16))
        query = jnp.concatenate(parts_q, axis=0)
        dout = jnp.concatenate(parts_d, axis=0)
        scores = lax.dot_general(k_all[:seen, :], query, BY_COLS, preferred_element_type=F32)
        dprobs = lax.dot_general(v_all[:seen, :], dout, BY_COLS, preferred_element_type=F32)
        return first, seen, query, dout, scores, dprobs

    def middle(first, seen, query, dout, scores, dprobs):
        tail = jnp.where(key <= row, scores[seen - QROWS :, :], -jnp.inf)
        scores = jnp.concatenate([scores[: seen - QROWS, :], tail], axis=0)
        peak = jnp.max(scores, axis=0, keepdims=True)
        expo = jnp.exp2((scores - peak) * (scale * math.log2(math.e)))
        probs = expo * (1.0 / jnp.sum(expo, axis=0, keepdims=True))
        probs_b = probs.astype(BF16)
        delta = jnp.sum(probs_b.astype(F32) * dprobs, axis=0, keepdims=True)
        dscores = (probs * (dprobs - delta)).astype(BF16)
        return first, seen, query, dout, probs_b, dscores

    def end(first, seen, query, dout, probs_b, dscores):
        grad_q = jnp.dot(k_turned[:, :seen], dscores, preferred_element_type=F32) * scale
        for f in range(fold):
            gq_ref[first : first + QROWS, f * HEAD_DIM : (f + 1) * HEAD_DIM] = (
                grad_q[:, f * QROWS : (f + 1) * QROWS].T.astype(BF16)
            )
        acc_k[:seen, :] += jnp.dot(dscores, query, preferred_element_type=F32)
        acc_v[:seen, :] += jnp.dot(probs_b, dout, preferred_element_type=F32)

    blocks = range(0, rows, QROWS)
    ready = begin(0)
    waiting = None
    for first in blocks:
        following = begin(first + QROWS) if first + QROWS < rows else None
        if waiting is not None:
            end(*waiting)
        waiting = middle(*ready)
        ready = following
    end(*waiting)

    sum_ref[:, :HEAD_DIM] = acc_k[:prompt_len, :] * scale
    sum_ref[:, HEAD_DIM:] = acc_v[:prompt_len, :]
    x = raw_ref[...]
    factor = lax.rsqrt(jnp.mean(x * x, axis=-1, keepdims=True) + EPS)
    normed = x * factor
    grad = acc_k[prompt_len:, :] * scale
    unturned = grad * cos_ref[...] - pltpu.roll(grad, HEAD_DIM // 2, 1) * sin_ref[...]
    inner = jnp.mean(unturned * normed, axis=-1, keepdims=True)
    g_ref[0, 0] = (factor * (unturned - normed * inner)).T.astype(BF16)
    g_ref[0, 1] = acc_v[prompt_len:, :].T.astype(BF16)


def attend(first, per, offset, chunk_heads, coef, ints, query, grad_output, prompt_both, own_both, raw, cosine, sine, before, after):
    rows, query_width = query.shape
    width = raw.shape[1]
    heads = width // HEAD_DIM
    fold = query_width // width
    parts = len(prompt_both)
    shard = prompt_both[0].shape[0]
    prompt_len = parts * shard
    total = prompt_len + rows
    here = lambda h: (0, first + h)
    there = lambda h: (0, heads + first + h)
    scalar = pl.BlockSpec(memory_space=pltpu.SMEM)
    table = pl.BlockSpec((rows, HEAD_DIM), lambda h: (0, 0))
    wide = pl.BlockSpec((rows, fold * HEAD_DIM), here)
    in_specs = [scalar, scalar, wide, wide]
    in_specs += [pl.BlockSpec((shard, HEAD_DIM), here)] * parts + [pl.BlockSpec((shard, HEAD_DIM), there)] * parts
    in_specs += [pl.BlockSpec((rows, HEAD_DIM), here), pl.BlockSpec((rows, HEAD_DIM), there)]
    in_specs += [pl.BlockSpec((rows, HEAD_DIM), here), table, table]
    operands = [coef, ints, query, grad_output, *prompt_both, *prompt_both, own_both, own_both, raw, cosine, sine]
    aliases = {}
    for i, value in enumerate(before):
        if value is not None:
            aliases[len(operands)] = i
            in_specs.append(pl.BlockSpec(memory_space=pl.ANY))
            operands.append(value)
    in_specs += [pl.BlockSpec(memory_space=pl.ANY)] * len(after)
    operands += after
    return pl.pallas_call(
        functools.partial(attend_kernel, parts, fold),
        grid=(per,),
        in_specs=in_specs,
        out_specs=[
            wide,
            pl.BlockSpec((prompt_len, 2 * HEAD_DIM), lambda h: (0, offset + h)),
            pl.BlockSpec((1, 2, HEAD_DIM, rows), lambda h: (h, 0, 0, 0)),
        ],
        out_shape=[
            jax.ShapeDtypeStruct((rows, query_width), BF16),
            jax.ShapeDtypeStruct((prompt_len, 2 * chunk_heads * HEAD_DIM), F32),
            jax.ShapeDtypeStruct((per, 2, HEAD_DIM, rows), BF16),
        ],
        scratch_shapes=[
            pltpu.VMEM((total, HEAD_DIM), BF16),
            pltpu.VMEM((total, HEAD_DIM), BF16),
            pltpu.VMEM((HEAD_DIM, total), BF16),
            pltpu.VMEM((total, HEAD_DIM), F32),
            pltpu.VMEM((total, HEAD_DIM), F32),
        ],
        input_output_aliases=aliases,
        compiler_params=pltpu.CompilerParams(vmem_limit_bytes=VMEM),
        cost_estimate=FREE,
        name="attend",
    )(*operands)


def everyone(value, names):
    return lax.all_to_all(value, names, split_axis=0, concat_axis=0, tiled=True)


def weight_kernel(parts, tokens_count, *refs):
    states = refs[:parts]
    grads = refs[parts : 2 * parts]
    tokens = refs[2 * parts : 2 * parts + tokens_count]
    out_ref, scale_ref, side_ref = refs[-3:]
    columns, rows = grads[0].shape
    total_rows = parts * states[0].shape[-2]

    @pl.when(pl.program_id(0) == 0)
    def _():
        highest = jnp.zeros((1, rows), F32)
        for d, grad in enumerate(grads):
            value = grad[...]
            side_ref[:, d * rows : (d + 1) * rows] = value
            highest = jnp.maximum(highest, jnp.max(jnp.abs(value), axis=0, keepdims=True).astype(F32))
        peak = jnp.max(highest, axis=1, keepdims=True)
        for token in tokens:
            highest = jnp.max(jnp.abs(token[...].astype(F32)), axis=0, keepdims=True)
            peak = jnp.maximum(peak, jnp.max(highest, axis=1, keepdims=True))
        reach = jnp.maximum(peak * (STATE_BOUND * total_rows), 1e-30)
        exponent = jnp.clip(jnp.ceil(jnp.log2(reach)), -90.0, 120.0)
        scale_ref[...] = jnp.broadcast_to(exponent, scale_ref.shape)

    exponent = scale_ref[:1, :1]
    response = jnp.concatenate([part[:rows, :] for part in states], axis=0)
    prompt = jnp.concatenate([part[rows:, :] for part in states], axis=0)
    token = jnp.concatenate([token[...] for token in tokens], axis=0)
    total = jnp.dot(side_ref[...], response, preferred_element_type=F32)
    total = total + lax.dot_general(token, prompt, BY_ROWS, preferred_element_type=F32)
    out_ref[:columns, :] = total * jnp.exp2(14.0 - exponent)
    out_ref[columns:, :] = jnp.broadcast_to(exponent, (MARK, out_ref.shape[1]))


def weight_shares(states, grads, tokens):
    parts = len(states)
    rows, depth = states[0][0].shape
    columns = grads[0].shape[0]
    step = 2 * HEAD_DIM
    return pl.pallas_call(
        functools.partial(weight_kernel, parts, len(tokens)),
        grid=(depth // step,),
        in_specs=[
            pl.BlockSpec((rows, step), lambda j: (0, j))
            if index is None
            else pl.BlockSpec((None, rows, step), lambda j, index=index: (index, 0, j))
            for _, index in states
        ]
        + [pl.BlockSpec(x.shape, lambda j: (0, 0)) for x in (*grads, *tokens)],
        out_specs=pl.BlockSpec((columns + MARK, step), lambda j: (0, j)),
        out_shape=jax.ShapeDtypeStruct((columns + MARK, depth), F32),
        scratch_shapes=[pltpu.VMEM((8, HEAD_DIM), F32), pltpu.VMEM((columns, parts * grads[0].shape[1]), BF16)],
        compiler_params=pltpu.CompilerParams(vmem_limit_bytes=VMEM),
        cost_estimate=FREE,
        name="weight_shares",
    )(*[array for array, _ in states], *grads, *tokens)


def rows_kernel(first, place_ref, sums_ref, raw_ref, cos_ref, sin_ref, *refs):
    out_ref = refs[-1]
    sub = sums_ref.shape[1]
    own = pl.ds(pl.multiple_of(place_ref[3] * sub, sub), sub)
    turn = pl.ds(pl.multiple_of(cos_ref.shape[0] - raw_ref.shape[0] + place_ref[3] * sub, sub), sub)
    cosine = cos_ref[turn, :]
    sine = sin_ref[turn, :]
    for head in range(out_ref.shape[1] // (2 * HEAD_DIM)):
        start = 2 * head * HEAD_DIM
        both = jnp.sum(sums_ref[:, :, start : start + 2 * HEAD_DIM], axis=0)
        grad = both[:, :HEAD_DIM]
        raw = raw_ref[own, (first + head) * HEAD_DIM : (first + head + 1) * HEAD_DIM]
        factor = lax.rsqrt(jnp.mean(raw * raw, axis=-1, keepdims=True) + EPS)
        normed = raw * factor
        unturned = grad * cosine - pltpu.roll(grad, HEAD_DIM // 2, 1) * sine
        inner = jnp.mean(unturned * normed, axis=-1, keepdims=True)
        out_ref[:, start : start + HEAD_DIM] = (factor * (unturned - normed * inner)).astype(BF16)
        out_ref[:, start + HEAD_DIM : start + 2 * HEAD_DIM] = both[:, HEAD_DIM:].astype(BF16)


def row_grads(first, place, sums, raw, cosine, sine, after):
    return pl.pallas_call(
        functools.partial(rows_kernel, first),
        in_specs=[pl.BlockSpec(memory_space=pltpu.SMEM)]
        + [pl.BlockSpec(memory_space=pltpu.VMEM)] * 4
        + [pl.BlockSpec(memory_space=pl.ANY)] * len(after),
        out_shape=jax.ShapeDtypeStruct(sums.shape[1:], BF16),
        compiler_params=pltpu.CompilerParams(vmem_limit_bytes=VMEM),
        cost_estimate=FREE,
        name="row_grads",
    )(place, sums, raw, cosine, sine, *after)


def advantage_of(rewards, group_ids):
    onehot = (group_ids[:, None] == jnp.arange(NADV, dtype=jnp.int32)[None, :]).astype(F32)
    sums = jnp.stack(
        [
            jnp.sum(onehot, axis=0),
            jnp.sum(onehot * rewards[:, None], axis=0),
            jnp.sum(onehot * (rewards * rewards)[:, None], axis=0),
        ]
    )
    names = ("chip", "core", "resp")
    peers = lax.axis_size(names)
    sums = jnp.sum(everyone(jnp.broadcast_to(sums[None], (peers,) + sums.shape), names), axis=0)
    members = jnp.maximum(sums[0], 1.0)
    mean = sums[1] / members
    spread = jnp.sqrt(jnp.maximum(sums[2] / members - mean * mean, 0.0))
    own_mean = jnp.sum(onehot * mean[None, :], axis=1)
    own_spread = jnp.sum(onehot * spread[None, :], axis=1)
    return (rewards - own_mean) / jnp.maximum(own_spread, 0.5)


def exponent_of(payload):
    return payload[-MARK : 1 - MARK].astype(F32)


def values_of(payload, exponent):
    return payload[:-MARK].astype(F32) * jnp.exp2(exponent)


def body(prompt_states, response_states, queries, grad_output, key_weight, value_weight, rewards, lengths, group_ids):
    depth, width = key_weight.shape
    shard = prompt_states.shape[1]
    rows = response_states.shape[2]
    n_grp = lax.axis_size("grp")
    n_chip = lax.axis_size("chip")
    n_core = lax.axis_size("core")
    n_resp = lax.axis_size("resp")
    n_prompt = n_chip * n_core
    grp = lax.axis_index("grp")
    chip = lax.axis_index("chip")
    core = lax.axis_index("core")
    resp = lax.axis_index("resp")
    prompt = chip * n_core + core
    prompt_len = shard * n_prompt
    block = depth // (n_prompt * n_resp * n_grp)
    sub = shard // n_resp
    states = response_states[0, 0]
    own_prompt = prompt_states[0]

    groups = [(e, c) for e in range(n_grp) for c in range(n_core)]
    counts = (n_grp, n_chip, n_core, n_resp, block)
    place = jnp.stack([grp, chip, core, resp]).astype(jnp.int32)
    beside, across_grp = select_columns(states, own_prompt, place, groups[1:], counts)
    chosen = across_grp
    beside = exchange(beside, [("core", 1)])
    across_grp = exchange(across_grp, [("grp", 1)])

    advantage = advantage_of(rewards[0], group_ids[0])
    length = lengths[0]
    coef = advantage / length.astype(F32)
    ints = jnp.stack([length[0], prompt.astype(jnp.int32)])

    line = jnp.arange(rows + shard, dtype=jnp.int32)
    cosine, sine = rotary_tables(jnp.where(line < rows, prompt_len + line, prompt * shard + line - rows))
    (prompt_raw, mine, own_raw, own_both), parts = project(
        own_prompt,
        states,
        key_weight,
        value_weight,
        cosine,
        sine,
        place,
        groups[:1],
        counts,
        chosen,
    )
    prompt_both = [mine]
    for d in range(1, n_prompt):
        prompt_both.append(exchange(mine, [("chip", d // n_core), ("core", d % n_core)]))

    def run(first, per, chunk_first, chunk_heads, grads, sums, after):
        grads, sums, own_g = attend(
            first, per, first - chunk_first, chunk_heads, coef, ints, queries[0, 0], grad_output[0, 0],
            prompt_both, own_both, own_raw, cosine, sine, [grads, sums], after,
        )
        return grads, sums, own_g.reshape(-1, rows)

    def across(own_g):
        return [exchange(own_g, [("grp", e)]) for e in range(1, n_grp)]

    def everywhere(own_g, hops):
        held = [own_g] + hops
        return [exchange(held[e], [("core", c)]) if c else held[e] for e, c in groups]

    def row_tokens(sums, chunk_first, after):
        sums = everyone(sums.reshape(n_prompt * n_resp, sub, -1), ("chip", "core", "resp"))
        own = row_grads(chunk_first, place, sums, prompt_raw, cosine, sine, after)
        return [exchange(own, [("grp", e), ("core", c)]) if e or c else own for e, c in groups]

    wide = n_resp * block

    def chip_terms(shares):
        return [shares[:, d * wide : (d + 1) * wide].astype(jnp.float16) for d in range(1, n_chip)]

    def resp_terms(kept, sent):
        exponents = [exponent_of(x) for x in [kept] + sent]
        top = functools.reduce(jnp.maximum, exponents) + math.ceil(math.log2(n_chip))
        total = values_of(kept, exponents[0] - top)
        for payload, exponent in zip(sent, exponents[1:]):
            total = total + values_of(payload, exponent - top)
        payload = jnp.concatenate([total, jnp.broadcast_to(top, (MARK, wide))], axis=0).astype(jnp.float16)
        half = lax.dynamic_slice_in_dim(total * jnp.exp2(top - 14.0), resp * block, block, 1)
        pieces = []
        for d in range(1, n_resp):
            part = lax.dynamic_slice_in_dim(payload, (resp ^ d) * block, block, 1)
            pieces.append(exchange(part, [("resp", d)]))
        return half, pieces

    def finish(half, pieces):
        for part in pieces:
            half = half + values_of(part, exponent_of(part) - 14.0)
        return half, exchange(half, [("grp", 1)])

    early, late = CALLS
    grads, sums_early, g_early = run(0, early, 0, early, None, None, [])
    hops_early = across(g_early)
    across_grp = tied(across_grp, g_early)
    grads, sums_late, g_late = run(early, late, early, late, grads, None, [beside, across_grp])
    parts = [(parts[0], None), (beside, None), (across_grp, 0), (exchange(across_grp, [("core", 1)]), 1)]
    hops_early = [tied(x, g_late) for x in hops_early]
    g_late = tied(g_late, *hops_early)
    sums_late = tied(sums_late, *hops_early)
    tokens_early = row_tokens(sums_early, 0, [g_late])
    g_late = tied(g_late, *[token for token, (e, c) in zip(tokens_early, groups) if e])
    hops_late = across(g_late)
    shares_early = weight_shares(parts, everywhere(g_early, hops_early), tokens_early)
    hops_late = [tied(x, shares_early) for x in hops_late]
    tokens_late = row_tokens(sums_late, early, [shares_early])
    shares_late = weight_shares(parts, everywhere(g_late, hops_late), tokens_late)
    sent_early = [exchange(x, [("chip", d)]) for d, x in enumerate(chip_terms(shares_early), 1)]
    payload_late = chip_terms(shares_late)
    sent_early = [lax.optimization_barrier((x, payload_late[0]))[0] for x in sent_early]
    sent_late = [exchange(x, [("chip", d)]) for d, x in enumerate(payload_late, 1)]
    half_early, pieces_early = resp_terms(shares_early[:, :wide], sent_early)
    done_early = finish(half_early, pieces_early)
    sent_late = [lax.optimization_barrier((x, done_early[0]))[0] for x in sent_late]
    half_late, pieces_late = resp_terms(shares_late[:, :wide], sent_late)
    finished = [done_early, finish(half_late, pieces_late)]

    mine = jnp.concatenate([pair[0] for pair in finished], axis=0)
    theirs = jnp.concatenate([pair[1] for pair in finished], axis=0)
    low = jnp.where(grp == 0, mine, theirs)
    high = jnp.where(grp == 0, theirs, mine)
    both = jnp.concatenate([low, high], axis=1).reshape(width // HEAD_DIM, 2, HEAD_DIM, n_grp * block)
    sides = [both[:, side].reshape(width, n_grp * block).T for side in range(2)]
    return (grads[None, None], sides[0], sides[1])


def solution(mesh):
    devices = mesh.devices
    n_grp, n_prompt, n_resp = devices.shape
    split = jax.sharding.Mesh(
        devices.reshape(n_grp, n_prompt // 2, 2, n_resp), ("grp", "chip", "core", "resp")
    )
    prompt = ("chip", "core")
    owner = ("chip", "core", "resp")
    placed = (
        P("grp", prompt, None),
        P("grp", owner, None, None),
        P("grp", owner, None, None),
        P("grp", owner, None, None),
        P(),
        P(),
        P("grp", owner),
        P("grp", owner),
        P("grp", owner),
    )
    return jax.shard_map(
        body,
        mesh=split,
        in_specs=placed,
        out_specs=(
            P("grp", owner, None, None),
            P(owner, None),
            P(owner, None),
        ),
        check_vma=False,
    )
```

```python
import functools
import math

import jax
import jax.numpy as jnp
from jax import lax
from jax.experimental import pallas as pl
from jax.experimental.pallas import tpu as pltpu
from jax.sharding import PartitionSpec as P

HEAD_DIM = 128
NADV = 8
THETA = 1000000.0
EPS = 1e-06
STATE_BOUND = 6.0
QROWS = 128
CALLS = (2, 2)
VMEM = 58 * 1024 * 1024
MARK = 16
PROJECT_BLOCK = 1024

BF16 = jnp.bfloat16
FREE = pl.CostEstimate(flops=1, bytes_accessed=1, transcendentals=0)
F32 = jnp.float32
BY_ROWS = (((0,), (0,)), ((), ()))
BY_COLS = (((1,), (1,)), ((), ()))


def exchange(value, steps):
    names = tuple(name for name, step in steps if step)
    sizes = [lax.axis_size(name) for name in names]
    mask = 0
    for (name, step), size in zip([s for s in steps if s[1]], sizes):
        mask = mask * size + step
    total = math.prod(sizes)
    return lax.ppermute(value, names, [(j, j ^ mask) for j in range(total)])


def rotary_tables(positions):
    lane = jnp.arange(HEAD_DIM, dtype=jnp.int32)
    half = HEAD_DIM // 2
    steps = (lane % half).astype(F32)
    freq = THETA ** (-2.0 * steps / HEAD_DIM)
    angle = positions.astype(F32)[:, None] * freq[None, :]
    sign = jnp.where(lane < half, -1.0, 1.0).astype(F32)
    return jnp.cos(angle), jnp.sin(angle) * sign[None, :]


def column_copies(groups, counts, place_ref, source_ref, rows, sub_ref, first, targets, sems):
    n_grp, n_chip, n_core, n_resp, block = counts
    sub = targets[0].shape[0] - rows
    own = pl.ds(pl.multiple_of(first + place_ref[3] * sub, sub), sub)
    copies = []
    for i, (e, c) in enumerate(groups):
        copies.append([])
        for d in range(n_chip):
            for r in range(n_resp):
                chip = place_ref[1] ^ d
                core = place_ref[2] ^ c
                index = ((chip * n_core + core) * n_resp + r) * n_grp + (place_ref[0] ^ e)
                source = pl.ds(pl.multiple_of(index * block, block), block)
                j = d * n_resp + r
                target = slice(j * block, (j + 1) * block)
                pairs = (
                    (source_ref.at[:rows, source], targets[i].at[:rows, target]),
                    (sub_ref.at[own, source], targets[i].at[rows:, target]),
                )
                for m, (src, dst) in enumerate(pairs):
                    copies[-1].append(pltpu.make_async_copy(src, dst, sems.at[i, j, m]))
                    copies[-1][-1].start()
    return copies


def select_kernel(groups, counts, place_ref, states_ref, prompt_ref, *refs):
    beside, across, held, sems, out_sems = refs
    outs = [beside, across.at[0], across.at[1]]
    targets = [held.at[i] for i in range(len(groups))]
    copies = column_copies(groups, counts, place_ref, states_ref, states_ref.shape[0], prompt_ref, 0, targets, sems)
    leaving = []
    for i, arriving in enumerate(copies):
        for copy in arriving:
            copy.wait()
        leaving.append(pltpu.make_async_copy(held.at[i], outs[i], out_sems.at[i]))
        leaving[-1].start()
    for copy in leaving:
        copy.wait()


def select_columns(states, prompt, place, groups, counts):
    n_grp, n_chip, n_core, n_resp, block = counts
    sub = prompt.shape[0] // n_resp
    rows = states.shape[0] + sub
    width = n_chip * n_resp * block
    if block % HEAD_DIM:
        own = lax.dynamic_slice_in_dim(prompt, place[3] * sub, sub, 0)
        split = jnp.concatenate([states, own]).reshape(rows, n_chip, n_core, n_resp, n_grp, block)
        out = []
        for e, c in groups:
            part = lax.dynamic_index_in_dim(split, place[0] ^ e, 4, keepdims=False)
            part = lax.dynamic_index_in_dim(part, place[2] ^ c, 2, keepdims=False)
            parts = [lax.dynamic_index_in_dim(part, place[1] ^ d, 1, keepdims=False) for d in range(n_chip)]
            out.append(jnp.stack(parts, axis=1).reshape(rows, width))
        return out if len(out) == 1 else (out[0], jnp.stack(out[1:]))
    return pl.pallas_call(
        functools.partial(select_kernel, groups, counts),
        in_specs=[pl.BlockSpec(memory_space=pltpu.SMEM)] + [pl.BlockSpec(memory_space=pl.ANY)] * 2,
        out_specs=[pl.BlockSpec(memory_space=pl.ANY)] * 2,
        out_shape=[
            jax.ShapeDtypeStruct((rows, width), states.dtype),
            jax.ShapeDtypeStruct((2, rows, width), states.dtype),
        ],
        scratch_shapes=[
            pltpu.VMEM((len(groups), rows, width), states.dtype),
            pltpu.SemaphoreType.DMA((len(groups), n_chip * n_resp, 2)),
            pltpu.SemaphoreType.DMA((len(groups),)),
        ],
        compiler_params=pltpu.CompilerParams(vmem_limit_bytes=VMEM),
        cost_estimate=FREE,
        name="select_columns",
    )(place, states, prompt)


def project_kernel(groups, counts, place_ref, p_hbm, r_hbm, wk_hbm, wv_hbm, cos_ref, sin_ref, after_ref, *refs):
    p_raw, p_both, r_raw, r_both = refs[:4]
    selected = refs[4:-7]
    x_ref, wk_ref, wv_ref, acc_k, acc_v, sems, out_sems = refs[-7:]
    depth, width = wk_ref.shape
    shard = p_raw.shape[0]
    rows = r_raw.shape[0]
    steps = depth // PROJECT_BLOCK
    copies = []
    for k in range(steps):
        part = slice(k * PROJECT_BLOCK, (k + 1) * PROJECT_BLOCK)
        pairs = (
            (wk_hbm.at[part, :], wk_ref.at[part, :]),
            (p_hbm.at[:, part], x_ref.at[rows:, part]),
            (r_hbm.at[:, part], x_ref.at[:rows, part]),
            (wv_hbm.at[part, :], wv_ref.at[part, :]),
        )
        copies.append([pltpu.make_async_copy(src, dst, sems.at[k, i]) for i, (src, dst) in enumerate(pairs)])
        for copy in copies[-1]:
            copy.start()
    leaving = []
    for k in range(steps):
        part = slice(k * PROJECT_BLOCK, (k + 1) * PROJECT_BLOCK)
        for copy in copies[k]:
            copy.wait()
        if k == steps - 1 and selected:
            leaving = column_copies(groups, counts, place_ref, x_ref, rows, x_ref, rows, selected, out_sems)
        for acc, w_ref in ((acc_k, wk_ref), (acc_v, wv_ref)):
            share = jnp.dot(x_ref[:, part], w_ref[part, :], preferred_element_type=F32)
            if k:
                acc[...] += share
            else:
                acc[...] = share
    for place, raw_ref, both_ref in (
        (slice(rows, rows + shard), p_raw, p_both),
        (slice(0, rows), r_raw, r_both),
    ):
        both_ref[:, width:] = acc_v[place, :].astype(BF16)
        raw_ref[...] = acc_k[place, :]
        cosine = cos_ref[place, :]
        sine = sin_ref[place, :]
        for head in range(width // HEAD_DIM):
            cols = slice(head * HEAD_DIM, (head + 1) * HEAD_DIM)
            x = acc_k[place, cols]
            factor = lax.rsqrt(jnp.mean(x * x, axis=-1, keepdims=True) + EPS)
            normed = x * factor
            turned = normed * cosine + pltpu.roll(normed, HEAD_DIM // 2, 1) * sine
            both_ref[:, cols] = turned.astype(BF16)
    for copy in sum(leaving, []):
        copy.wait()


def project(prompt, response, key_weight, value_weight, cosine, sine, place, groups, counts, after):
    depth, width = key_weight.shape
    shard, rows = prompt.shape[0], response.shape[0]
    n_grp, n_chip, n_core, n_resp, block = counts
    direct = block % HEAD_DIM == 0
    blocks = n_chip * n_resp
    part = jax.ShapeDtypeStruct((rows + shard // n_resp, blocks * block), BF16)
    any_spec = pl.BlockSpec(memory_space=pl.ANY)
    vmem = pl.BlockSpec(memory_space=pltpu.VMEM)
    out = pl.pallas_call(
        functools.partial(project_kernel, groups, counts),
        in_specs=[pl.BlockSpec(memory_space=pltpu.SMEM)] + [any_spec] * 4 + [vmem] * 2 + [any_spec],
        out_specs=[vmem] * 4 + ([any_spec] * len(groups) if direct else []),
        out_shape=[
            jax.ShapeDtypeStruct((count, scale * width), kind)
            for count in (shard, rows)
            for scale, kind in ((1, F32), (2, BF16))
        ]
        + ([part] * len(groups) if direct else []),
        scratch_shapes=[pltpu.VMEM((shard + rows, depth), BF16)]
        + [pltpu.VMEM((depth, width), BF16)] * 2
        + [pltpu.VMEM((shard + rows, width), F32)] * 2
        + [
            pltpu.SemaphoreType.DMA((depth // PROJECT_BLOCK, 4)),
            pltpu.SemaphoreType.DMA((len(groups), blocks, 2)),
        ],
        compiler_params=pltpu.CompilerParams(vmem_limit_bytes=VMEM),
        cost_estimate=FREE,
        name="project",
    )(place, prompt, response, key_weight, value_weight, cosine, sine, after)
    if direct:
        return out[:4], out[4:]
    return out, select_columns(response, prompt, place, groups, counts)


def tied(value, *others):
    return pl.pallas_call(
        lambda *refs: None,
        in_specs=[pl.BlockSpec(memory_space=pl.ANY)] * (1 + len(others)),
        out_specs=pl.BlockSpec(memory_space=pl.ANY),
        out_shape=jax.ShapeDtypeStruct(value.shape, value.dtype),
        input_output_aliases={0: 0},
        cost_estimate=FREE,
        name="tied",
    )(value, *others)


def attend_kernel(parts, fold, coef_ref, ints_ref, q_ref, go_ref, *refs):
    prompt_k = refs[:parts]
    prompt_v = refs[parts : 2 * parts]
    own_k, own_v, raw_ref, cos_ref, sin_ref = refs[2 * parts : 2 * parts + 5]
    gq_ref, sum_ref, g_ref, k_all, v_all, k_turned, acc_k, acc_v = refs[-8:]
    rows = q_ref.shape[0]
    shard = prompt_k[0].shape[0]
    prompt_len = parts * shard
    scale = HEAD_DIM ** (-0.5)
    length = ints_ref[0]
    coef = coef_ref[0]
    prompt = ints_ref[1]
    for d in range(parts):
        place = pl.ds(pl.multiple_of((prompt ^ d) * shard, shard), shard)
        k_all[place, :] = prompt_k[d][...]
        v_all[place, :] = prompt_v[d][...]
    k_all[prompt_len:, :] = own_k[...]
    v_all[prompt_len:, :] = own_v[...]
    k_turned[...] = k_all[...].T
    acc_k[...] = jnp.zeros_like(acc_k)
    acc_v[...] = jnp.zeros_like(acc_v)
    width = fold * QROWS
    key = lax.broadcasted_iota(jnp.int32, (QROWS, width), 0)
    row = lax.broadcasted_iota(jnp.int32, (QROWS, width), 1) % QROWS

    def begin(first):
        seen = prompt_len + first + QROWS
        position = first + lax.broadcasted_iota(jnp.int32, (QROWS, HEAD_DIM), 0)
        factor = jnp.where(position < length, coef, 0.0)
        parts_q = []
        parts_d = []
        for f in range(fold):
            cols = slice(f * HEAD_DIM, (f + 1) * HEAD_DIM)
            parts_q.append(q_ref[first : first + QROWS, cols])
            parts_d.append((go_ref[first : first + QROWS, cols].astype(F32) * factor).astype(BF16))
        query = jnp.concatenate(parts_q, axis=0)
        dout = jnp.concatenate(parts_d, axis=0)
        scores = lax.dot_general(k_all[:seen, :], query, BY_COLS, preferred_element_type=F32)
        dprobs = lax.dot_general(v_all[:seen, :], dout, BY_COLS, preferred_element_type=F32)
        return first, seen, query, dout, scores, dprobs

    def middle(first, seen, query, dout, scores, dprobs):
        tail = jnp.where(key <= row, scores[seen - QROWS :, :], -jnp.inf)
        scores = jnp.concatenate([scores[: seen - QROWS, :], tail], axis=0)
        peak = jnp.max(scores, axis=0, keepdims=True)
        expo = jnp.exp2((scores - peak) * (scale * math.log2(math.e)))
        probs = expo * (1.0 / jnp.sum(expo, axis=0, keepdims=True))
        probs_b = probs.astype(BF16)
        delta = jnp.sum(probs_b.astype(F32) * dprobs, axis=0, keepdims=True)
        dscores = (probs * (dprobs - delta)).astype(BF16)
        return first, seen, query, dout, probs_b, dscores

    def end(first, seen, query, dout, probs_b, dscores):
        grad_q = jnp.dot(k_turned[:, :seen], dscores, preferred_element_type=F32) * scale
        for f in range(fold):
            gq_ref[first : first + QROWS, f * HEAD_DIM : (f + 1) * HEAD_DIM] = (
                grad_q[:, f * QROWS : (f + 1) * QROWS].T.astype(BF16)
            )
        acc_k[:seen, :] += jnp.dot(dscores, query, preferred_element_type=F32)
        acc_v[:seen, :] += jnp.dot(probs_b, dout, preferred_element_type=F32)

    blocks = range(0, rows, QROWS)
    ready = begin(0)
    waiting = None
    for first in blocks:
        following = begin(first + QROWS) if first + QROWS < rows else None
        if waiting is not None:
            end(*waiting)
        waiting = middle(*ready)
        ready = following
    end(*waiting)

    sum_ref[:, :HEAD_DIM] = acc_k[:prompt_len, :] * scale
    sum_ref[:, HEAD_DIM:] = acc_v[:prompt_len, :]
    x = raw_ref[...]
    factor = lax.rsqrt(jnp.mean(x * x, axis=-1, keepdims=True) + EPS)
    normed = x * factor
    grad = acc_k[prompt_len:, :] * scale
    unturned = grad * cos_ref[...] - pltpu.roll(grad, HEAD_DIM // 2, 1) * sin_ref[...]
    inner = jnp.mean(unturned * normed, axis=-1, keepdims=True)
    g_ref[0, 0] = (factor * (unturned - normed * inner)).T.astype(BF16)
    g_ref[0, 1] = acc_v[prompt_len:, :].T.astype(BF16)


def attend(first, per, offset, chunk_heads, coef, ints, query, grad_output, prompt_both, own_both, raw, cosine, sine, before, after):
    rows, query_width = query.shape
    width = raw.shape[1]
    heads = width // HEAD_DIM
    fold = query_width // width
    parts = len(prompt_both)
    shard = prompt_both[0].shape[0]
    prompt_len = parts * shard
    total = prompt_len + rows
    here = lambda h: (0, first + h)
    there = lambda h: (0, heads + first + h)
    scalar = pl.BlockSpec(memory_space=pltpu.SMEM)
    table = pl.BlockSpec((rows, HEAD_DIM), lambda h: (0, 0))
    wide = pl.BlockSpec((rows, fold * HEAD_DIM), here)
    in_specs = [scalar, scalar, wide, wide]
    in_specs += [pl.BlockSpec((shard, HEAD_DIM), here)] * parts + [pl.BlockSpec((shard, HEAD_DIM), there)] * parts
    in_specs += [pl.BlockSpec((rows, HEAD_DIM), here), pl.BlockSpec((rows, HEAD_DIM), there)]
    in_specs += [pl.BlockSpec((rows, HEAD_DIM), here), table, table]
    operands = [coef, ints, query, grad_output, *prompt_both, *prompt_both, own_both, own_both, raw, cosine, sine]
    aliases = {}
    for i, value in enumerate(before):
        if value is not None:
            aliases[len(operands)] = i
            in_specs.append(pl.BlockSpec(memory_space=pl.ANY))
            operands.append(value)
    in_specs += [pl.BlockSpec(memory_space=pl.ANY)] * len(after)
    operands += after
    return pl.pallas_call(
        functools.partial(attend_kernel, parts, fold),
        grid=(per,),
        in_specs=in_specs,
        out_specs=[
            wide,
            pl.BlockSpec((prompt_len, 2 * HEAD_DIM), lambda h: (0, offset + h)),
            pl.BlockSpec((1, 2, HEAD_DIM, rows), lambda h: (h, 0, 0, 0)),
        ],
        out_shape=[
            jax.ShapeDtypeStruct((rows, query_width), BF16),
            jax.ShapeDtypeStruct((prompt_len, 2 * chunk_heads * HEAD_DIM), F32),
            jax.ShapeDtypeStruct((per, 2, HEAD_DIM, rows), BF16),
        ],
        scratch_shapes=[
            pltpu.VMEM((total, HEAD_DIM), BF16),
            pltpu.VMEM((total, HEAD_DIM), BF16),
            pltpu.VMEM((HEAD_DIM, total), BF16),
            pltpu.VMEM((total, HEAD_DIM), F32),
            pltpu.VMEM((total, HEAD_DIM), F32),
        ],
        input_output_aliases=aliases,
        compiler_params=pltpu.CompilerParams(vmem_limit_bytes=VMEM),
        cost_estimate=FREE,
        name="attend",
    )(*operands)


def everyone(value, names):
    return lax.all_to_all(value, names, split_axis=0, concat_axis=0, tiled=True)


def weight_kernel(parts, tokens_count, *refs):
    states = refs[:parts]
    grads = refs[parts : 2 * parts]
    tokens = refs[2 * parts : 2 * parts + tokens_count]
    out_ref, scale_ref, side_ref = refs[-3:]
    columns, rows = grads[0].shape
    total_rows = parts * states[0].shape[-2]

    @pl.when(pl.program_id(0) == 0)
    def _():
        highest = jnp.zeros((1, rows), F32)
        for d, grad in enumerate(grads):
            value = grad[...]
            side_ref[:, d * rows : (d + 1) * rows] = value
            highest = jnp.maximum(highest, jnp.max(jnp.abs(value), axis=0, keepdims=True).astype(F32))
        peak = jnp.max(highest, axis=1, keepdims=True)
        for token in tokens:
            highest = jnp.max(jnp.abs(token[...].astype(F32)), axis=0, keepdims=True)
            peak = jnp.maximum(peak, jnp.max(highest, axis=1, keepdims=True))
        reach = jnp.maximum(peak * (STATE_BOUND * total_rows), 1e-30)
        exponent = jnp.clip(jnp.ceil(jnp.log2(reach)), -90.0, 120.0)
        scale_ref[...] = jnp.broadcast_to(exponent, scale_ref.shape)

    exponent = scale_ref[:1, :1]
    response = jnp.concatenate([part[:rows, :] for part in states], axis=0)
    prompt = jnp.concatenate([part[rows:, :] for part in states], axis=0)
    token = jnp.concatenate([token[...] for token in tokens], axis=0)
    total = jnp.dot(side_ref[...], response, preferred_element_type=F32)
    total = total + lax.dot_general(token, prompt, BY_ROWS, preferred_element_type=F32)
    out_ref[:columns, :] = total * jnp.exp2(14.0 - exponent)
    out_ref[columns:, :] = jnp.broadcast_to(exponent, (MARK, out_ref.shape[1]))


def weight_shares(states, grads, tokens):
    parts = len(states)
    rows, depth = states[0][0].shape
    columns = grads[0].shape[0]
    step = 2 * HEAD_DIM
    return pl.pallas_call(
        functools.partial(weight_kernel, parts, len(tokens)),
        grid=(depth // step,),
        in_specs=[
            pl.BlockSpec((rows, step), lambda j: (0, j))
            if index is None
            else pl.BlockSpec((None, rows, step), lambda j, index=index: (index, 0, j))
            for _, index in states
        ]
        + [pl.BlockSpec(x.shape, lambda j: (0, 0)) for x in (*grads, *tokens)],
        out_specs=pl.BlockSpec((columns + MARK, step), lambda j: (0, j)),
        out_shape=jax.ShapeDtypeStruct((columns + MARK, depth), F32),
        scratch_shapes=[pltpu.VMEM((8, HEAD_DIM), F32), pltpu.VMEM((columns, parts * grads[0].shape[1]), BF16)],
        compiler_params=pltpu.CompilerParams(vmem_limit_bytes=VMEM),
        cost_estimate=FREE,
        name="weight_shares",
    )(*[array for array, _ in states], *grads, *tokens)


def rows_kernel(first, place_ref, sums_ref, raw_ref, cos_ref, sin_ref, *refs):
    out_ref = refs[-1]
    sub = sums_ref.shape[1]
    own = pl.ds(pl.multiple_of(place_ref[3] * sub, sub), sub)
    turn = pl.ds(pl.multiple_of(cos_ref.shape[0] - raw_ref.shape[0] + place_ref[3] * sub, sub), sub)
    cosine = cos_ref[turn, :]
    sine = sin_ref[turn, :]
    for head in range(out_ref.shape[1] // (2 * HEAD_DIM)):
        start = 2 * head * HEAD_DIM
        both = jnp.sum(sums_ref[:, :, start : start + 2 * HEAD_DIM], axis=0)
        grad = both[:, :HEAD_DIM]
        raw = raw_ref[own, (first + head) * HEAD_DIM : (first + head + 1) * HEAD_DIM]
        factor = lax.rsqrt(jnp.mean(raw * raw, axis=-1, keepdims=True) + EPS)
        normed = raw * factor
        unturned = grad * cosine - pltpu.roll(grad, HEAD_DIM // 2, 1) * sine
        inner = jnp.mean(unturned * normed, axis=-1, keepdims=True)
        out_ref[:, start : start + HEAD_DIM] = (factor * (unturned - normed * inner)).astype(BF16)
        out_ref[:, start + HEAD_DIM : start + 2 * HEAD_DIM] = both[:, HEAD_DIM:].astype(BF16)


def row_grads(first, place, sums, raw, cosine, sine, after):
    return pl.pallas_call(
        functools.partial(rows_kernel, first),
        in_specs=[pl.BlockSpec(memory_space=pltpu.SMEM)]
        + [pl.BlockSpec(memory_space=pltpu.VMEM)] * 4
        + [pl.BlockSpec(memory_space=pl.ANY)] * len(after),
        out_shape=jax.ShapeDtypeStruct(sums.shape[1:], BF16),
        compiler_params=pltpu.CompilerParams(vmem_limit_bytes=VMEM),
        cost_estimate=FREE,
        name="row_grads",
    )(place, sums, raw, cosine, sine, *after)


def advantage_of(rewards, group_ids):
    onehot = (group_ids[:, None] == jnp.arange(NADV, dtype=jnp.int32)[None, :]).astype(F32)
    sums = jnp.stack(
        [
            jnp.sum(onehot, axis=0),
            jnp.sum(onehot * rewards[:, None], axis=0),
            jnp.sum(onehot * (rewards * rewards)[:, None], axis=0),
        ]
    )
    names = ("chip", "core", "resp")
    peers = lax.axis_size(names)
    sums = jnp.sum(everyone(jnp.broadcast_to(sums[None], (peers,) + sums.shape), names), axis=0)
    members = jnp.maximum(sums[0], 1.0)
    mean = sums[1] / members
    spread = jnp.sqrt(jnp.maximum(sums[2] / members - mean * mean, 0.0))
    own_mean = jnp.sum(onehot * mean[None, :], axis=1)
    own_spread = jnp.sum(onehot * spread[None, :], axis=1)
    return (rewards - own_mean) / jnp.maximum(own_spread, 0.5)


def exponent_of(payload):
    return payload[-MARK : 1 - MARK].astype(F32)


def values_of(payload, exponent):
    return payload[:-MARK].astype(F32) * jnp.exp2(exponent)


def body(prompt_states, response_states, queries, grad_output, key_weight, value_weight, rewards, lengths, group_ids):
    depth, width = key_weight.shape
    shard = prompt_states.shape[1]
    rows = response_states.shape[2]
    n_grp = lax.axis_size("grp")
    n_chip = lax.axis_size("chip")
    n_core = lax.axis_size("core")
    n_resp = lax.axis_size("resp")
    n_prompt = n_chip * n_core
    grp = lax.axis_index("grp")
    chip = lax.axis_index("chip")
    core = lax.axis_index("core")
    resp = lax.axis_index("resp")
    prompt = chip * n_core + core
    prompt_len = shard * n_prompt
    block = depth // (n_prompt * n_resp * n_grp)
    sub = shard // n_resp
    states = response_states[0, 0]
    own_prompt = prompt_states[0]

    groups = [(e, c) for e in range(n_grp) for c in range(n_core)]
    counts = (n_grp, n_chip, n_core, n_resp, block)
    place = jnp.stack([grp, chip, core, resp]).astype(jnp.int32)
    beside, across_grp = select_columns(states, own_prompt, place, groups[1:], counts)
    chosen = across_grp
    beside = exchange(beside, [("core", 1)])
    across_grp = exchange(across_grp, [("grp", 1)])

    advantage = advantage_of(rewards[0], group_ids[0])
    length = lengths[0]
    coef = advantage / length.astype(F32)
    ints = jnp.stack([length[0], prompt.astype(jnp.int32)])

    line = jnp.arange(rows + shard, dtype=jnp.int32)
    cosine, sine = rotary_tables(jnp.where(line < rows, prompt_len + line, prompt * shard + line - rows))
    (prompt_raw, mine, own_raw, own_both), parts = project(
        own_prompt,
        states,
        key_weight,
        value_weight,
        cosine,
        sine,
        place,
        groups[:1],
        counts,
        chosen,
    )
    prompt_both = [mine]
    for d in range(1, n_prompt):
        prompt_both.append(exchange(mine, [("chip", d // n_core), ("core", d % n_core)]))

    def run(first, per, chunk_first, chunk_heads, grads, sums, after):
        grads, sums, own_g = attend(
            first, per, first - chunk_first, chunk_heads, coef, ints, queries[0, 0], grad_output[0, 0],
            prompt_both, own_both, own_raw, cosine, sine, [grads, sums], after,
        )
        return grads, sums, own_g.reshape(-1, rows)

    def across(own_g):
        return [exchange(own_g, [("grp", e)]) for e in range(1, n_grp)]

    def everywhere(own_g, hops):
        held = [own_g] + hops
        return [exchange(held[e], [("core", c)]) if c else held[e] for e, c in groups]

    def row_tokens(sums, chunk_first, after):
        sums = everyone(sums.reshape(n_prompt * n_resp, sub, -1), ("chip", "core", "resp"))
        own = row_grads(chunk_first, place, sums, prompt_raw, cosine, sine, after)
        return [exchange(own, [("grp", e), ("core", c)]) if e or c else own for e, c in groups]

    wide = n_resp * block

    def chip_terms(shares):
        return [exchange(shares[:, d * wide : (d + 1) * wide].astype(jnp.float16), [("chip", d)]) for d in range(1, n_chip)]

    def resp_terms(kept, sent):
        exponents = [exponent_of(x) for x in [kept] + sent]
        top = functools.reduce(jnp.maximum, exponents) + math.ceil(math.log2(n_chip))
        total = values_of(kept, exponents[0] - top)
        for payload, exponent in zip(sent, exponents[1:]):
            total = total + values_of(payload, exponent - top)
        payload = jnp.concatenate([total, jnp.broadcast_to(top, (MARK, wide))], axis=0).astype(jnp.float16)
        half = lax.dynamic_slice_in_dim(total * jnp.exp2(top - 14.0), resp * block, block, 1)
        pieces = []
        for d in range(1, n_resp):
            part = lax.dynamic_slice_in_dim(payload, (resp ^ d) * block, block, 1)
            pieces.append(exchange(part, [("resp", d)]))
        return half, pieces

    def finish(half, pieces):
        for part in pieces:
            half = half + values_of(part, exponent_of(part) - 14.0)
        return half, exchange(half, [("grp", 1)])

    early, late = CALLS
    grads, sums_early, g_early = run(0, early, 0, early, None, None, [])
    hops_early = across(g_early)
    across_grp = tied(across_grp, g_early)
    grads, sums_late, g_late = run(early, late, early, late, grads, None, [beside, across_grp])
    parts = [(parts[0], None), (beside, None), (across_grp, 0), (exchange(across_grp, [("core", 1)]), 1)]
    hops_early = [tied(x, g_late) for x in hops_early]
    g_late = tied(g_late, *hops_early)
    sums_late = tied(sums_late, *hops_early)
    tokens_early = row_tokens(sums_early, 0, [g_late])
    g_late = tied(g_late, *[token for token, (e, c) in zip(tokens_early, groups) if e])
    hops_late = across(g_late)
    shares_early = weight_shares(parts, everywhere(g_early, hops_early), tokens_early)
    hops_late = [tied(x, shares_early) for x in hops_late]
    tokens_late = row_tokens(sums_late, early, [shares_early])
    shares_late = weight_shares(parts, everywhere(g_late, hops_late), tokens_late)
    sent_early = chip_terms(shares_early)
    sent_late = chip_terms(shares_late)
    half_early, pieces_early = resp_terms(shares_early[:, :wide], sent_early)
    done_early = finish(half_early, pieces_early)
    sent_late = [lax.optimization_barrier((x, done_early[0]))[0] for x in sent_late]
    half_late, pieces_late = resp_terms(shares_late[:, :wide], sent_late)
    finished = [done_early, finish(half_late, pieces_late)]

    mine = jnp.concatenate([pair[0] for pair in finished], axis=0)
    theirs = jnp.concatenate([pair[1] for pair in finished], axis=0)
    low = jnp.where(grp == 0, mine, theirs)
    high = jnp.where(grp == 0, theirs, mine)
    both = jnp.concatenate([low, high], axis=1).reshape(width // HEAD_DIM, 2, HEAD_DIM, n_grp * block)
    sides = [both[:, side].reshape(width, n_grp * block).T for side in range(2)]
    return (grads[None, None], sides[0], sides[1])


def solution(mesh):
    devices = mesh.devices
    n_grp, n_prompt, n_resp = devices.shape
    split = jax.sharding.Mesh(
        devices.reshape(n_grp, n_prompt // 2, 2, n_resp), ("grp", "chip", "core", "resp")
    )
    prompt = ("chip", "core")
    owner = ("chip", "core", "resp")
    placed = (
        P("grp", prompt, None),
        P("grp", owner, None, None),
        P("grp", owner, None, None),
        P("grp", owner, None, None),
        P(),
        P(),
        P("grp", owner),
        P("grp", owner),
        P("grp", owner),
    )
    return jax.shard_map(
        body,
        mesh=split,
        in_specs=placed,
        out_specs=(
            P("grp", owner, None, None),
            P(owner, None),
            P(owner, None),
        ),
        check_vma=False,
    )
```
